32 devices in a mesh: dp: 8 (over y, x, core), tensor: 4 (over z).
Axes of the slice: x: 2, y: 2, z: 4, core: 2. Of those that a mesh axis runs over, the one named last changes fastest.
Arguments:
- tokens: bfloat16 [2, 8192, 1152], P(None, 'dp'), may hold values from -6 to 6
- conditioning: bfloat16 [2, 32, 1152], P(None, 'dp'), may hold values from -6 to 6
- lengths: int32 [2, 32], P(None, 'dp'), may hold values from 0 to 1024, as said below
- out_grad: bfloat16 [2, 8192, 1152], P(None, 'dp'), may hold values from -6 to 6
- ada_weight: bfloat16 [1152, 6912], P(None, 'tensor'), may hold values from -0.1875 to 0.1875
- ada_bias: float32 [6912], P('tensor'), may hold values from -1.75 to 1.75
- qkv_weight: bfloat16 [3, 1152, 1152], P(None, None, 'tensor'), may hold values from -0.1875 to 0.1875
- qv_bias: float32 [2, 1152], P(None, 'tensor'), may hold values from -1.75 to 1.75
- out_weight: bfloat16 [1152, 1152], P('tensor'), may hold values from -2 to 2
- out_bias: float32 [1152], replicated, may hold values from -1.75 to 1.75
- up_weight: bfloat16 [1152, 4608], P(None, 'tensor'), may hold values from -0.1875 to 0.1875
- up_bias: float32 [4608], P('tensor'), may hold values from -1.75 to 1.75
- down_weight: bfloat16 [4608, 1152], P('tensor'), may hold values from -0.09375 to 0.09375
- down_bias: float32 [1152], replicated, may hold values from -1.75 to 1.75
Outputs:
- layer_out: bfloat16 [2, 8192, 1152], P(None, ('dp', 'tensor'))
- tokens_grad: float32 [2, 8192, 1152], P(None, ('dp', 'tensor'))
- conditioning_grad: float32 [2, 32, 1152], P(None, 'dp')
- ada_weight_grad: float32 [1152, 6912], P(None, 'tensor')
- ada_bias_grad: float32 [6912], P('tensor')
- qkv_weight_grad: float32 [3, 1152, 1152], P(None, None, 'tensor')
- qv_bias_grad: float32 [2, 1152], P(None, 'tensor')
- out_weight_grad: float32 [1152, 1152], P('tensor')
- out_bias_grad: float32 [1152], replicated
- up_weight_grad: float32 [1152, 4608], P(None, 'tensor')
- up_bias_grad: float32 [4608], P('tensor')
- down_weight_grad: float32 [4608, 1152], P('tensor')
- down_bias_grad: float32 [1152], replicated
The draws below stay inside these ranges and needn't reach their ends.
Inputs may be any that keep to these rules, and one draw needn't show every extreme that they name: `lengths`: each pack's slots come in runs of 4: a run holds one latent of 1024 tokens followed by zeros, or 2 to 4 latents of 256 tokens followed by zeros. A pack's latents lie end to end from its first row; the rows after them are padding.
All inputs are finite; a program needn't handle non-finite values.
Results may differ from the reference program's by a relative error of at most 0.013.
The reference program's roundings to bfloat16 on the way count: a program that leaves them out, or rounds other values in their place, can miss the bound.
Values may be sent and summed in bfloat16 or wider, within the bound.
No kernel may reach another device: no remote copies, remote signals or barrier semaphores. Data moves between devices by JAX's collectives and lax.ppermute only.
A program may use at most 384 MiB of HBM per device.

```python
import jax
import jax.numpy as jnp
from jax import lax

D = 1152
HEADS = 16
HEAD_DIM = 72
FF = 4608
MB = 2
LONG = 1024
SHORT = 256
TOK_MB = 1024
SLOTS = 4
TOKENS_MB = 8192
IMAGES = 32
N_DP = 8


def draw_lengths(key, part):
    key = jax.random.fold_in(key, 11)
    pack_count = MB * (IMAGES // SLOTS)
    ratio = LONG // SHORT
    frame_count = SLOTS // ratio
    kinds = jax.random.randint(jax.random.fold_in(key, 1), (pack_count, frame_count), 0, 2)
    shorts = jax.random.randint(jax.random.fold_in(key, 2), (pack_count, frame_count), 2, ratio + 1)
    other = (MB - 1) * (IMAGES // SLOTS)
    kinds = kinds.at[0, 0].set(1)
    kinds = kinds.at[other, 0].set(0)
    shorts = shorts.at[other, 0].set(2)
    index = jnp.arange(ratio, dtype=jnp.int32)
    short_rows = jnp.where(index[None, None, :] < shorts[:, :, None], SHORT, 0)
    long_rows = jnp.where(index == 0, LONG, 0)[None, None, :]
    chosen = jnp.where(kinds[:, :, None] == 1, long_rows, short_rows)
    return chosen.reshape(MB, IMAGES).astype(jnp.int32)


def steps_of(key, extent, pieces, low, high):
    gain, own = 1.0, jax.random.fold_in(key, 6)
    for dim, blocks in pieces:
        heights = jnp.exp(jax.random.uniform(jax.random.fold_in(own, dim), (blocks,), jnp.float32, low / len(pieces), high / len(pieces)))
        gain = gain * jnp.repeat(heights, extent[dim] // blocks).reshape([-1 if axis == dim else 1 for axis in range(len(extent))])
    return gain


def gaussian(stream_key, dims, deviation, limit, shards=(), kind=jnp.bfloat16):
    drawn = jax.random.normal(stream_key, dims, jnp.float32) * deviation
    if len(shards) > 0:
        drawn = steps_of(stream_key, dims, shards, -0.22, 0.18) * drawn
    return jnp.clip(drawn, min=-limit, max=limit).astype(kind)


def setup_inputs(seed: int = 0) -> dict:
    splits = jax.random.split(jax.random.key(seed), 15)
    tokens = gaussian(splits[0], (MB, TOKENS_MB, D), 1.0, 6.0, ((1, 8),))
    conditioning = gaussian(splits[1], (MB, IMAGES, D), 1.0, 6.0, ((1, 8),))
    lengths = draw_lengths(jax.random.fold_in(splits[14], 71), 0)
    out_grad = gaussian(splits[3], (MB, TOKENS_MB, D), 1.0, 6.0, ((1, 8),))
    ada_weight = gaussian(splits[4], (D, 6 * D), D ** -0.5, 0.1875, ((1, 4),))
    ada_bias = gaussian(splits[5], (6 * D,), 0.3, 1.75, ((0, 4),), jnp.float32)
    qkv_weight = gaussian(splits[6], (3, D, D), D ** -0.5, 0.1875, ((2, 4),))
    qv_bias = gaussian(splits[7], (2, D), 0.3, 1.75, ((1, 4),), jnp.float32)
    out_weight = gaussian(splits[8], (D, D), (max(D // 128, 1)) ** -0.5, 2.0, ((0, 4),))
    out_bias = gaussian(splits[9], (D,), 0.3, 1.75, (), jnp.float32)
    up_weight = gaussian(splits[10], (D, FF), D ** -0.5, 0.1875, ((1, 4),))
    up_bias = gaussian(splits[11], (FF,), 0.3, 1.75, ((0, 4),), jnp.float32)
    down_weight = gaussian(splits[12], (FF, D), FF ** -0.5, 0.09375, ((0, 4),))
    down_bias = gaussian(splits[13], (D,), 0.3, 1.75, (), jnp.float32)
    return dict(tokens=tokens, conditioning=conditioning, lengths=lengths, out_grad=out_grad, ada_weight=ada_weight, ada_bias=ada_bias, qkv_weight=qkv_weight, qv_bias=qv_bias, out_weight=out_weight, out_bias=out_bias, up_weight=up_weight, up_bias=up_bias, down_weight=down_weight, down_bias=down_bias)


EPSILON = 1e-06
MASKED = -1e+30
HIGHEST = lax.Precision.HIGHEST

@jax.custom_vjp
def low(v):
    return lax.optimization_barrier(v.astype(jnp.bfloat16)).astype(jnp.float32)

@jax.custom_vjp
def low_back(v):
    return v

def low_keep(v):
    return (low(v), None)

def low_pass(kept, grad):
    return (grad,)

def back_keep(v):
    return (v, None)

def back_low(kept, grad):
    return (low(grad),)
low.defvjp(low_keep, low_pass)
low_back.defvjp(back_keep, back_low)

def segment_info(lengths_row, row_count):
    boundary = jnp.cumsum(lengths_row).astype(jnp.int32)
    position = jnp.arange(row_count, dtype=jnp.int32)
    segment = lax.optimization_barrier(jnp.sum((boundary[None, :] <= position[:, None]).astype(jnp.int32), axis=1)).astype(jnp.int32)
    slot_count = lengths_row.shape[0]
    onehot = (segment[:, None] == jnp.arange(slot_count, dtype=jnp.int32)[None, :]).astype(jnp.float32)
    validity = (segment < slot_count).astype(jnp.float32)
    return (segment, validity, onehot)

def normalize(values):
    centred = values - lax.optimization_barrier(jnp.mean(values, axis=-1, keepdims=True))
    inverse = lax.rsqrt(lax.optimization_barrier(jnp.mean(centred * centred, axis=-1, keepdims=True)) + EPSILON)
    return centred * inverse

def pack_forward(item, weights):
    tokens, condition, lengths_row = item
    ada_weight, ada_bias, qkv_weight, qv_bias, out_weight, out_bias, up_weight, up_bias, down_weight, down_bias = weights
    row_count = tokens.shape[0]
    segment, validity, onehot = segment_info(lengths_row, row_count)
    cond_act = low(jax.nn.silu(condition))
    modulation = low_back(jnp.dot(cond_act, ada_weight, precision=HIGHEST)) + ada_bias
    per_token = jnp.dot(onehot, modulation, precision=HIGHEST)
    shift_one, scale_one, gate_one, shift_two, scale_two, gate_two = jnp.split(per_token, 6, axis=1)
    hidden_one = low(normalize(tokens) * (1.0 + scale_one) + shift_one)
    query_rows = low(low_back(jnp.dot(hidden_one, qkv_weight[0], precision=HIGHEST)) + qv_bias[0])
    key_rows = low(low_back(jnp.dot(hidden_one, qkv_weight[1], precision=HIGHEST)))
    value_rows = low(low_back(jnp.dot(hidden_one, qkv_weight[2], precision=HIGHEST)) + qv_bias[1])
    head_shape = (row_count, HEADS, HEAD_DIM)
    raw_scores = low_back(jnp.einsum('qhd,khd->hqk', query_rows.reshape(head_shape), key_rows.reshape(head_shape), precision=HIGHEST))
    allowed = segment[:, None] == segment[None, :]
    scores = jnp.where(allowed[None], raw_scores * HEAD_DIM ** (-0.5), MASKED)
    row_max = lax.optimization_barrier(jnp.max(scores, axis=-1, keepdims=True))
    exponent = jnp.exp(scores - row_max)
    softmaxed = exponent / lax.optimization_barrier(jnp.sum(exponent, axis=-1, keepdims=True))
    attended = jnp.einsum('hqk,khd->qhd', low(softmaxed), value_rows.reshape(head_shape), precision=HIGHEST)
    attended = low(low_back(attended.reshape(row_count, HEADS * HEAD_DIM)))
    attn_out = low_back(jnp.dot(attended, out_weight, precision=HIGHEST)) + out_bias
    residual_mid = tokens + gate_one * attn_out
    hidden_two = low(normalize(residual_mid) * (1.0 + scale_two) + shift_two)
    pre_act = low_back(jnp.dot(hidden_two, up_weight, precision=HIGHEST)) + up_bias
    activated = low(jax.nn.gelu(pre_act, approximate=True))
    mlp_out = low_back(jnp.dot(activated, down_weight, precision=HIGHEST)) + down_bias
    return validity[:, None] * (residual_mid + gate_two * mlp_out)

def reference(tokens, conditioning, lengths, out_grad, ada_weight, ada_bias, qkv_weight, qv_bias, out_weight, out_bias, up_weight, up_bias, down_weight, down_bias):
    pack_count = MB * N_DP
    token_packs = tokens.astype(jnp.float32).reshape(pack_count, TOK_MB, D)
    cond_packs = conditioning.astype(jnp.float32).reshape(pack_count, SLOTS, D)
    length_packs = lengths.reshape(pack_count, SLOTS)
    grad_packs = out_grad.astype(jnp.float32).reshape(pack_count, TOK_MB, D)
    weights = tuple((weight.astype(jnp.float32) for weight in (ada_weight, ada_bias, qkv_weight, qv_bias, out_weight, out_bias, up_weight, up_bias, down_weight, down_bias)))

    def whole(token_arg, cond_arg, weight_arg):
        step_fn = jax.checkpoint(lambda item: pack_forward(item, weight_arg))
        return lax.map(step_fn, (token_arg, cond_arg, length_packs))
    result, pullback = jax.vjp(whole, token_packs, cond_packs, weights)
    token_grad, cond_grad, weight_grads = pullback(grad_packs)
    return (result.reshape(MB, TOKENS_MB, D).astype(jnp.bfloat16), token_grad.reshape(MB, TOKENS_MB, D), cond_grad.reshape(MB, IMAGES, D), weight_grads[0], weight_grads[1], weight_grads[2], weight_grads[3], weight_grads[4], weight_grads[5], weight_grads[6], weight_grads[7], weight_grads[8], weight_grads[9])
```

```python
import functools
import math

import jax
import jax.numpy as jnp
from jax import lax
from jax.experimental import pallas as pl
from jax.experimental.pallas import tpu as pltpu
from jax.sharding import PartitionSpec as P

HEAD_DIM = 72
EPSILON = 1e-06
LOG2E = math.log2(math.e)
GELU_C = 0.7978845608
GELU_A = 0.044715
VMEM = 56 * 1024 * 1024
BF = jnp.bfloat16
F32 = jnp.float32


def nn(a, b):
    return lax.dot_general(a, b, (((1,), (0,)), ((), ())), preferred_element_type=F32)


def nt(a, b):
    return lax.dot_general(a, b, (((1,), (1,)), ((), ())), preferred_element_type=F32)


def tn(a, b):
    return lax.dot_general(a, b, (((0,), (0,)), ((), ())), preferred_element_type=F32)


def params(semantics=None):
    return pltpu.CompilerParams(vmem_limit_bytes=VMEM)


def cost(flops, moved, exps=0):
    return pl.CostEstimate(flops=int(flops), bytes_accessed=int(moved), transcendentals=int(exps))


def normalize(values):
    centred = values - jnp.mean(values, axis=-1, keepdims=True)
    inverse = lax.rsqrt(jnp.mean(centred * centred, axis=-1, keepdims=True) + EPSILON)
    return centred * inverse, inverse


def norm_backward(grad, normed, inverse):
    return inverse * (
        grad
        - jnp.mean(grad, axis=-1, keepdims=True)
        - normed * jnp.mean(grad * normed, axis=-1, keepdims=True)
    )


def project_kernel(tok_ref, mod_ref, w_ref, bias_ref, hid_ref, q_ref, k_ref, v_ref):
    normed, _ = normalize(tok_ref[0].astype(F32))
    hidden = (normed * (1.0 + mod_ref[0, 1:2, :]) + mod_ref[0, 0:1, :]).astype(BF)
    hid_ref[0] = hidden
    heads = q_ref.shape[1]
    size = q_ref.shape[3]
    for which, out in enumerate((q_ref, k_ref, v_ref)):
        proj = nn(hidden, w_ref[which])
        if which == 0:
            proj = proj + bias_ref[0:1, :]
        if which == 2:
            proj = proj + bias_ref[1:2, :]
        proj = proj.astype(BF)
        for h in range(heads):
            out[0, h] = proj[:, h * size : (h + 1) * size]


def project(tokens, mod_blocks, qkv_weight, qv_bias, blocks):
    micro, rows, width = tokens.shape
    share = rows // blocks
    local = qkv_weight.shape[2]
    heads = local // HEAD_DIM
    head_shape = jax.ShapeDtypeStruct((micro, heads, rows, HEAD_DIM), BF)
    head_spec = pl.BlockSpec((1, heads, share, HEAD_DIM), lambda m, b: (m, 0, b, 0))
    return pl.pallas_call(
        project_kernel,
        grid=(micro, blocks),
        in_specs=[
            pl.BlockSpec((1, share, width), lambda m, b: (m, b, 0)),
            pl.BlockSpec((1, 6, width), lambda m, b: (m * blocks + b, 0, 0)),
            pl.BlockSpec(qkv_weight.shape, lambda m, b: (0, 0, 0)),
            pl.BlockSpec(qv_bias.shape, lambda m, b: (0, 0)),
        ],
        out_specs=[
            pl.BlockSpec((1, share, width), lambda m, b: (m, b, 0)),
            head_spec,
            head_spec,
            head_spec,
        ],
        out_shape=[jax.ShapeDtypeStruct(tokens.shape, BF), head_shape, head_shape, head_shape],
        compiler_params=params(),
        cost_estimate=cost(2 * micro * rows * width * 3 * local, 20e6),
        name="project",
    )(tokens, mod_blocks, qkv_weight, qv_bias)


def attend_kernel(info_ref, q_ref, k_ref, v_ref, att_ref, lse_ref):
    heads, share, size = q_ref.shape[1:]
    block = info_ref[0]
    whole = info_ref[1 + pl.program_id(0)]
    factor = size ** (-0.5) * LOG2E

    def run(span):
        for h in range(heads):
            keys = k_ref[0, h, span, :]
            values = v_ref[0, h, span, :]
            scores = nt(q_ref[0, h], keys) * factor
            top = jnp.max(scores, axis=-1, keepdims=True)
            weight = jnp.exp2(scores - top)
            total = jnp.sum(weight, axis=-1, keepdims=True)
            out = nn(weight.astype(BF), values) / total
            att_ref[0, :, h * size : (h + 1) * size] = out.astype(BF)
            lse = jnp.broadcast_to(top + jnp.log2(total), (share, 128))
            lse_ref[0, h : h + 1, :] = lse.T[0:1, :]

    @pl.when(whole == 1)
    def _():
        run(slice(None))

    @pl.when(whole == 0)
    def _():
        run(pl.ds(pl.multiple_of(block * share, share), share))


def attend(info, query, key, value, blocks):
    micro, heads, rows, size = query.shape
    share = rows // blocks
    full = pl.BlockSpec((1, heads, rows, size), lambda m, s: (m, 0, 0, 0))
    return pl.pallas_call(
        attend_kernel,
        grid_spec=pltpu.PrefetchScalarGridSpec(
            num_scalar_prefetch=1,
            grid=(micro,),
            in_specs=[
                pl.BlockSpec((1, heads, share, size), lambda m, s: (m, 0, s[0], 0)),
                full,
                full,
            ],
            out_specs=[
                pl.BlockSpec((1, share, heads * size), lambda m, s: (m, 0, 0)),
                pl.BlockSpec((1, heads, share), lambda m, s: (m, 0, 0)),
            ],
        ),
        out_shape=[
            jax.ShapeDtypeStruct((micro, share, heads * size), BF),
            jax.ShapeDtypeStruct((micro, heads, share), F32),
        ],
        compiler_params=params(),
        cost_estimate=cost(
            4 * micro * heads * share * rows * 256, 6e6, micro * heads * share * rows
        ),
        name="attend",
    )(info, query, key, value)


def middle_kernel(info_ref, a0, a1, a2, a3, w_ref, bias_ref, tok_ref, mod_ref, attn_ref, mid_ref, hid_ref):
    rank = info_ref[0]
    total = bias_ref[0:1, :]
    for shift, part in enumerate((a0, a1, a2, a3)):
        total = total + nn(part[0], w_ref[lax.rem(rank + 4 - shift, 4)])
    attn_ref[0] = total
    mid = tok_ref[0].astype(F32) + mod_ref[0, 2:3, :] * total
    mid_ref[0] = mid
    normed, _ = normalize(mid)
    hid_ref[0] = (normed * (1.0 + mod_ref[0, 4:5, :]) + mod_ref[0, 3:4, :]).astype(BF)


def middle(info, parts, out_full, out_bias, tokens, mod_blocks, blocks):
    micro, share, local = parts[0].shape
    width = tokens.shape[2]
    part = pl.BlockSpec((1, share, local), lambda m, s: (m, 0, 0))
    row = pl.BlockSpec((1, share, width), lambda m, s: (m, 0, 0))
    return pl.pallas_call(
        middle_kernel,
        grid_spec=pltpu.PrefetchScalarGridSpec(
            num_scalar_prefetch=1,
            grid=(micro,),
            in_specs=[part] * 4
            + [
                pl.BlockSpec(out_full.shape, lambda m, s: (0, 0, 0)),
                pl.BlockSpec((1, width), lambda m, s: (0, 0)),
                pl.BlockSpec((1, share, width), lambda m, s: (m, s[0], 0)),
                pl.BlockSpec((1, 6, width), lambda m, s: (m * blocks + s[0], 0, 0)),
            ],
            out_specs=[row, row, row],
        ),
        out_shape=[
            jax.ShapeDtypeStruct((micro, share, width), F32),
            jax.ShapeDtypeStruct((micro, share, width), F32),
            jax.ShapeDtypeStruct((micro, share, width), BF),
        ],
        compiler_params=params(),
        cost_estimate=cost(2 * micro * share * width * width, 12e6),
        name="middle",
    )(info, *parts, out_full, out_bias, tokens, mod_blocks)


def feed_kernel(first, shapes, *refs):
    n_up, n_down = shapes
    xo, xt, go, gt = refs[:4]
    up_parts = refs[4 : 4 + n_up]
    down_parts = refs[4 + n_up : 4 + n_up + n_down]
    at = 4 + n_up + n_down
    bias_ref = refs[at]
    at += 1
    if not first:
        mlp_in, gh_in = refs[at : at + 2]
        at += 2
    mlp_ref, gh_ref, wu_ref, wd_ref, bsum_ref = refs[at : at + 5]
    xs, gs, us, ds, acts, dps = refs[at + 5 :]
    half = xo.shape[0]
    units = us.shape[0]
    step = pl.program_id(0)
    chunk = 256

    @pl.when(step == 0)
    def _():
        xs[:half] = xo[...]
        xs[half:] = xt[...]
        gs[:half] = go[...]
        gs[half:] = gt[...]

    def fill(target, parts):
        start = 0
        for ref in parts:
            block = ref[...]
            block = block.reshape(-1, block.shape[-1])
            target[start : start + block.shape[0]] = block
            start += block.shape[0]

    fill(us, up_parts)
    fill(ds, down_parts)
    bias = bias_ref[0]

    def rows_step(i, sums):
        rows = pl.ds(pl.multiple_of(i * chunk, chunk), chunk)
        pre = nt(xs[rows, :], us[...]) + bias
        square = pre * pre
        tanh = jnp.tanh(GELU_C * pre * (1.0 + GELU_A * square))
        act = (0.5 * pre * (1.0 + tanh)).astype(BF)
        acts[rows, :] = act
        slope = 0.5 * (1.0 + tanh) + (0.5 * GELU_C) * pre * (1.0 - tanh * tanh) * (
            1.0 + 3.0 * GELU_A * square
        )
        dpre = nt(gs[rows, :], ds[...]) * slope
        low = dpre.astype(BF)
        dps[rows, :] = low
        mlp = nn(act, ds[...])
        gh = nn(low, us[...])
        old_mlp = mlp_ref[rows, :]
        old_gh = gh_ref[rows, :]
        mlp_ref[rows, :] = old_mlp + mlp
        gh_ref[rows, :] = old_gh + gh
        return sums + jnp.sum(dpre, axis=0, keepdims=True)

    @pl.when(step == 0)
    def _():
        if first:
            mlp_ref[...] = jnp.zeros_like(mlp_ref)
            gh_ref[...] = jnp.zeros_like(gh_ref)
        else:
            mlp_ref[...] = mlp_in[...]
            gh_ref[...] = gh_in[...]

    bsum_ref[0] = lax.fori_loop(0, 2 * half // chunk, rows_step, jnp.zeros((1, units), F32))
    for start in range(0, units, 256):
        stop = min(start + 256, units)
        wu_ref[0, start:stop] = tn(dps[:, start:stop], xs[...]).astype(BF)
        wd_ref[0, start:stop] = tn(acts[:, start:stop], gs[...]).astype(BF)


def feed(own_x, other_x, own_g, other_g, ups, downs, bias, carry):
    half, width = own_x.shape
    count, _, units = bias.shape
    first = carry is None
    rows = pl.BlockSpec((half, width), lambda k: (0, 0))
    acc = pl.BlockSpec((2 * half, width), lambda k: (0, 0))
    wspec = pl.BlockSpec((1, units, width), lambda k: (k, 0, 0))
    in_specs = [rows] * 4
    operands = [own_x, other_x, own_g, other_g]
    for array, block, index in ups + downs:
        in_specs.append(pl.BlockSpec(block, index))
        operands.append(array)
    in_specs.append(pl.BlockSpec((1, 1, units), lambda k: (k, 0, 0)))
    operands.append(bias)
    if not first:
        in_specs += [acc, acc]
        operands += list(carry)
    return pl.pallas_call(
        functools.partial(feed_kernel, first, (len(ups), len(downs))),
        grid=(count,),
        in_specs=in_specs,
        out_specs=[acc, acc, wspec, wspec, pl.BlockSpec((1, 1, units), lambda k: (k, 0, 0))],
        out_shape=[
            jax.ShapeDtypeStruct((2 * half, width), F32),
            jax.ShapeDtypeStruct((2 * half, width), F32),
            jax.ShapeDtypeStruct((count, units, width), BF),
            jax.ShapeDtypeStruct((count, units, width), BF),
            jax.ShapeDtypeStruct((count, 1, units), F32),
        ],
        scratch_shapes=[
            pltpu.VMEM((2 * half, width), BF),
            pltpu.VMEM((2 * half, width), BF),
            pltpu.VMEM((units, width), BF),
            pltpu.VMEM((units, width), BF),
            pltpu.VMEM((2 * half, units), BF),
            pltpu.VMEM((2 * half, units), BF),
        ],
        compiler_params=params(),
        cost_estimate=cost(
            12 * count * 2 * half * width * units, 20e6 + count * 6e6, count * 2 * half * units
        ),
        name="feed",
    )(*operands)


def between_kernel(
    info_ref, gho, ght, mlpo, mlpt, mid_ref, attn_ref, og_ref, mod_ref, dbias_ref, w_ref,
    a0, a1, a2, a3, layer_ref, gmid_ref, d0, d1, d2, d3, wout_ref, sums_ref,
):
    rank = info_ref[0]
    micro = pl.program_id(0)
    valid = info_ref[1 + micro].astype(F32)
    mod = mod_ref[0]
    mid = mid_ref[0]
    attn = attn_ref[0]
    normed, inverse = normalize(mid)
    mlp_out = mlpo[...] + mlpt[...] + dbias_ref[0:1, :]
    layer_ref[0] = (valid * (mid + mod[5:6, :] * mlp_out)).astype(BF)
    grad_y = og_ref[0].astype(F32) * valid
    grad_hidden = gho[...] + ght[...]
    grad_mid = grad_y + norm_backward(grad_hidden * (1.0 + mod[4:5, :]), normed, inverse)
    gmid_ref[0] = grad_mid
    grad_attn = grad_mid * mod[2:3, :]
    sums_ref[0, 0:1, :] = jnp.sum(grad_mid * attn, axis=0, keepdims=True)
    sums_ref[0, 1:2, :] = jnp.sum(grad_hidden, axis=0, keepdims=True)
    sums_ref[0, 2:3, :] = jnp.sum(grad_hidden * normed, axis=0, keepdims=True)
    sums_ref[0, 3:4, :] = jnp.sum(grad_y * mlp_out, axis=0, keepdims=True)
    sums_ref[0, 4:5, :] = jnp.sum(grad_attn, axis=0, keepdims=True)
    sums_ref[0, 5:6, :] = jnp.sum(grad_y * mod[5:6, :], axis=0, keepdims=True)
    low = grad_attn.astype(BF)
    for shift, (out, part) in enumerate(((d0, a0), (d1, a1), (d2, a2), (d3, a3))):
        out[0] = nt(low, w_ref[lax.rem(rank + 4 - shift, 4)]).astype(BF)
        update = tn(part[0], low)
        wout_ref[shift] = jnp.where(micro == 0, update, wout_ref[shift] + update)


def between(info, feed_own, feed_other, mid, attn, out_grad, mod_blocks, down_bias, out_full, parts, blocks):
    micro, share, width = mid.shape
    local = parts[0].shape[2]
    half = pl.BlockSpec((share, width), lambda m, s: (m, 0))
    row = pl.BlockSpec((1, share, width), lambda m, s: (m, 0, 0))
    part = pl.BlockSpec((1, share, local), lambda m, s: (m, 0, 0))
    mlp_own, gh_own = feed_own
    mlp_other, gh_other = feed_other
    dshape = jax.ShapeDtypeStruct((micro, share, local), BF)
    return pl.pallas_call(
        between_kernel,
        grid_spec=pltpu.PrefetchScalarGridSpec(
            num_scalar_prefetch=1,
            grid=(micro,),
            in_specs=[half] * 4
            + [
                row,
                row,
                pl.BlockSpec((1, share, width), lambda m, s: (m, s[0], 0)),
                pl.BlockSpec((1, 6, width), lambda m, s: (m * blocks + s[0], 0, 0)),
                pl.BlockSpec((1, width), lambda m, s: (0, 0)),
                pl.BlockSpec(out_full.shape, lambda m, s: (0, 0, 0)),
            ]
            + [part] * 4,
            out_specs=[row, row, part, part, part, part]
            + [
                pl.BlockSpec((blocks, local, width), lambda m, s: (0, 0, 0)),
                pl.BlockSpec((1, 8, width), lambda m, s: (m, 0, 0)),
            ],
        ),
        out_shape=[
            jax.ShapeDtypeStruct((micro, share, width), BF),
            jax.ShapeDtypeStruct((micro, share, width), F32),
            dshape,
            dshape,
            dshape,
            dshape,
            jax.ShapeDtypeStruct((blocks, local, width), F32),
            jax.ShapeDtypeStruct((micro, 8, width), F32),
        ],
        compiler_params=params(),
        cost_estimate=cost(4 * micro * share * width * width, 30e6),
        name="between",
    )(info, gh_own, gh_other, mlp_own, mlp_other, mid, attn, out_grad, mod_blocks, down_bias, out_full, *parts)


def attend_back_kernel(
    info_ref, q_ref, k_ref, v_ref, l0, l1, l2, l3, g0, g1, g2, g3, w_ref,
    dq_ref, dk_ref, dv_ref, part_ref, dos, dqs, dks, dvs,
):
    _, heads, rows, size = q_ref.shape
    share = g0.shape[1]
    rank = info_ref[0]
    whole = info_ref[1]
    scale = size ** (-0.5)
    factor = scale * LOG2E
    lses = (l0, l1, l2, l3)
    for shift, grad in enumerate((g0, g1, g2, g3)):
        for h in range(heads):
            dos[h, shift] = grad[0, :, h * size : (h + 1) * size]

    def block_of(shift):
        return pl.multiple_of(lax.rem(rank + shift, 4) * share, share)

    def tile(h, shift, keys, values, keys_t):
        query = q_ref[0, h, pl.ds(block_of(shift), share), :]
        grad = dos[h, shift]
        lse = lses[shift][0, pl.ds(h, 1), :]
        probs = jnp.exp2(nt(keys, query) * factor - lse)
        dprobs = nt(values, grad)
        inner = jnp.sum(probs * dprobs, axis=0, keepdims=True)
        dscores = (probs * (dprobs - inner) * scale).astype(BF)
        dqs[h, pl.ds(block_of(shift), share), :] = nn(keys_t, dscores).T.astype(BF)
        return nn(dscores, query), nn(probs.astype(BF), grad)

    @pl.when(whole == 1)
    def _():
        def head(h, carry):
            keys = k_ref[0, h]
            values = v_ref[0, h]
            keys_t = keys.astype(F32).T.astype(BF)
            dkey, dvalue = tile(h, 0, keys, values, keys_t)
            for shift in range(1, 4):
                more_key, more_value = tile(h, shift, keys, values, keys_t)
                dkey = dkey + more_key
                dvalue = dvalue + more_value
            dks[h] = dkey.astype(BF)
            dvs[h] = dvalue.astype(BF)
            return carry

        lax.fori_loop(0, heads, head, 0)

    @pl.when(whole == 0)
    def _():
        def head(h, carry):
            for shift in range(4):
                span = pl.ds(block_of(shift), share)
                keys = k_ref[0, h, span, :]
                values = v_ref[0, h, span, :]
                dkey, dvalue = tile(h, shift, keys, values, keys.astype(F32).T.astype(BF))
                dks[h, span, :] = dkey.astype(BF)
                dvs[h, span, :] = dvalue.astype(BF)
            return carry

        lax.fori_loop(0, heads, head, 0)

    for src, dst in ((dqs, dq_ref), (dks, dk_ref), (dvs, dv_ref)):
        for h in range(heads):
            dst[:, h * size : (h + 1) * size] = src[h]

    def out_rows(i, carry):
        span = pl.ds(pl.multiple_of(i * share, share), share)
        part_ref[span, :] = (
            nt(dq_ref[span, :], w_ref[0]) + nt(dk_ref[span, :], w_ref[1]) + nt(dv_ref[span, :], w_ref[2])
        ).astype(BF)
        return carry

    lax.fori_loop(0, rows // share, out_rows, 0)


def attend_back(micro, info, query, key, value, lses, grads, qkv_weight):
    _, heads, rows, size = query.shape
    share = rows // 4
    local = heads * size
    width = qkv_weight.shape[1]
    full = pl.BlockSpec((1, heads, rows, size), lambda i, s: (micro, 0, 0, 0))
    return pl.pallas_call(
        attend_back_kernel,
        grid_spec=pltpu.PrefetchScalarGridSpec(
            num_scalar_prefetch=1,
            grid=(1,),
            in_specs=[full] * 3
            + [pl.BlockSpec((1, heads, share), lambda i, s: (micro, 0, 0))] * 4
            + [pl.BlockSpec((1, share, local), lambda i, s: (micro, 0, 0))] * 4
            + [pl.BlockSpec(qkv_weight.shape, lambda i, s: (0, 0, 0))],
            out_specs=[pl.BlockSpec((rows, local), lambda i, s: (0, 0))] * 3
            + [pl.BlockSpec((rows, width), lambda i, s: (0, 0))],
            scratch_shapes=[
                pltpu.VMEM((heads, 4, share, size), BF),
                pltpu.VMEM((heads, rows, size), BF),
                pltpu.VMEM((heads, rows, size), BF),
                pltpu.VMEM((heads, rows, size), BF),
            ],
        ),
        out_shape=[jax.ShapeDtypeStruct((rows, local), BF)] * 3
        + [jax.ShapeDtypeStruct((rows, width), BF)],
        compiler_params=params(),
        cost_estimate=cost(10 * heads * rows * rows * 256, 12e6, heads * rows * rows),
        name="attend_back",
    )(info, query, key, value, *lses, *grads, qkv_weight)


def finish_kernel(info_ref, grad_ref, tok_ref, mod_ref, gmid_ref, out_ref, sums_ref):
    normed, inverse = normalize(tok_ref[0].astype(F32))
    grad = grad_ref[0].astype(F32)
    out_ref[0] = gmid_ref[0] + norm_backward(grad * (1.0 + mod_ref[0, 1:2, :]), normed, inverse)
    sums_ref[0, 0:1, :] = jnp.sum(grad, axis=0, keepdims=True)
    sums_ref[0, 1:2, :] = jnp.sum(grad * normed, axis=0, keepdims=True)


def finish(info, grad, tokens, mod_blocks, gmid, blocks):
    micro, share, width = gmid.shape
    row = pl.BlockSpec((1, share, width), lambda m, s: (m, 0, 0))
    return pl.pallas_call(
        finish_kernel,
        grid_spec=pltpu.PrefetchScalarGridSpec(
            num_scalar_prefetch=1,
            grid=(micro,),
            in_specs=[
                row,
                pl.BlockSpec((1, share, width), lambda m, s: (m, s[0], 0)),
                pl.BlockSpec((1, 6, width), lambda m, s: (m * blocks + s[0], 0, 0)),
                row,
            ],
            out_specs=[row, pl.BlockSpec((1, 2, width), lambda m, s: (m, 0, 0))],
        ),
        out_shape=[
            jax.ShapeDtypeStruct((micro, share, width), F32),
            jax.ShapeDtypeStruct((micro, 2, width), F32),
        ],
        compiler_params=params(),
        cost_estimate=cost(micro * share * width * 20, 8e6),
        name="finish",
    )(info, grad, tokens, mod_blocks, gmid)


def turn(array, shift):
    count = lax.axis_size("tensor")
    return lax.ppermute(array, "tensor", [(i, (i + shift) % count) for i in range(count)])


def flip(array, bit):
    return lax.ppermute(array, "dp", [(i, i ^ bit) for i in range(lax.axis_size("dp"))])


def by_rank(array, rank, axis):
    count = array.shape[axis]
    index = jnp.mod(rank - jnp.arange(count), count)
    return jnp.take(array, index, axis=axis)


def by_quarter(array, quarter, axis):
    index = jnp.bitwise_xor(jnp.arange(4), quarter)
    return jnp.take(array, index, axis=axis)


def add(a, b):
    return (a.astype(F32) + b.astype(F32)).astype(BF)


CORE, SIDE_X, SIDE_Y = 1, 2, 4


def local(
    tokens, conditioning, lengths, out_grad, ada_weight, ada_bias, qkv_weight, qv_bias,
    out_weight, out_bias, up_weight, up_bias, down_weight, down_bias,
):
    groups = lax.axis_size("tensor")
    dp = lax.axis_size("dp")
    rank = lax.axis_index("tensor")
    place = lax.axis_index("dp")
    core = jnp.bitwise_and(place, 1)
    quarter = jnp.bitwise_and(place >> 1, 3)
    micro, rows, width = tokens.shape
    share = rows // groups
    slots = lengths.shape[1]
    part = up_weight.shape[1]
    half = part // 2
    piece = half // 4
    columns = ada_weight.shape[1]

    up_half = lax.dynamic_slice_in_dim(up_weight, core * half, half, 1).T
    down_half = lax.dynamic_slice_in_dim(down_weight, core * half, half, 0)
    mine = jnp.concatenate(
        [
            lax.dynamic_slice_in_dim(up_half, quarter * piece, piece, 0),
            lax.dynamic_slice_in_dim(down_half, quarter * piece, piece, 0),
        ]
    )
    received = [turn(mine, k) for k in (1, 2, 3)]
    up0 = jnp.stack([r[:piece] for r in received])
    down0 = jnp.stack([r[piece:] for r in received])
    up_x = flip(up0, SIDE_X)
    down_y = flip(down0, SIDE_Y)
    up_y = flip(jnp.stack([up0, up_x]), SIDE_Y)
    down_x = flip(jnp.stack([down0, down_y]), SIDE_X)
    out_full = lax.all_gather(out_weight, "tensor", axis=0)

    cond_float = conditioning.astype(F32)
    cond_act = jax.nn.silu(cond_float).astype(BF).reshape(micro * slots, width)
    ada_part = jnp.dot(cond_act, ada_weight, preferred_element_type=F32) + ada_bias
    small = jnp.concatenate([ada_part, jnp.pad(up_bias, (0, columns - part))[None]])
    gathered = lax.all_gather(small, "tensor", axis=0)
    modulation = gathered[:, : micro * slots].transpose(1, 0, 2).reshape(micro, slots, 6 * width)
    boundary = jnp.cumsum(lengths, axis=1)
    starts = jnp.arange(groups, dtype=jnp.int32) * share
    segment = jnp.sum((boundary[:, None, :] <= starts[None, :, None]).astype(jnp.int32), axis=2)
    onehot = (segment[:, :, None] == jnp.arange(slots)[None, None, :]).astype(F32)
    mod_blocks = jnp.sum(onehot[:, :, :, None] * modulation[:, None], axis=2)
    mod_blocks = mod_blocks.reshape(micro * groups, 6, width)
    whole = (segment[:, groups - 1] == 0).astype(jnp.int32)
    valid = (segment < slots).astype(jnp.int32)
    own_valid = lax.dynamic_index_in_dim(valid, rank, 1, False)
    own_gate = lax.dynamic_index_in_dim(
        mod_blocks.reshape(micro, groups, 6, width), rank, 1, False
    )[:, 5:6]

    bias_all = by_rank(gathered[:, micro * slots, :part], rank, 0).reshape(groups, 2, half)
    bias_all = lax.dynamic_index_in_dim(bias_all, core, 1, False)
    bias_rel = by_quarter(bias_all.reshape(groups, 4, piece), quarter, 1).reshape(groups, half)
    bias_own = bias_all[0].reshape(1, 1, half)
    bias_far = bias_rel[1:].reshape(groups - 1, 1, half)

    hidden_one, query, key, value = project(tokens, mod_blocks, qkv_weight, qv_bias, groups)

    own_grad = lax.dynamic_slice_in_dim(out_grad, rank * share, share, 1).astype(F32)
    grad_mlp = own_grad * (own_valid.astype(F32)[:, None, None] * own_gate)
    own_g = grad_mlp.astype(BF).reshape(micro * share, width)
    other_g = flip(own_g, CORE)

    att = [None] * groups
    lse = [None] * groups
    parts = [None] * groups
    for shift in (1, 2, 3, 0):
        info = jnp.concatenate([jnp.mod(rank + shift, groups)[None], whole])
        att[shift], lse[shift] = attend(info, query, key, value, groups)
        parts[shift] = turn(att[shift], shift) if shift else att[shift]

    rank_info = rank[None]
    attn, mid, hidden_two = middle(
        rank_info, parts, out_full, out_bias[None], tokens, mod_blocks, groups
    )
    own_x = hidden_two.reshape(micro * share, width)
    other_x = flip(own_x, CORE)

    near = lambda k: (0, 0)
    far = lambda k: (k, 0, 0)
    pair = lambda k: (0, k, 0, 0)
    mlp, gh, wu0, wd0, bsum0 = feed(
        own_x, other_x, own_g, other_g,
        [(up_half, (half, width), near)],
        [(down_half, (half, width), near)],
        bias_own, None,
    )
    one = (1, piece, width)
    two = (2, 1, piece, width)
    mlp, gh, wu, wd, bsum = feed(
        own_x, other_x, own_g, other_g,
        [(up0, one, far), (up_x, one, far), (up_y, two, pair)],
        [
            (down0, one, far),
            (down_x, (1, 1, piece, width), lambda k: (0, k, 0, 0)),
            (down_y, one, far),
            (down_x, (1, 1, piece, width), lambda k: (1, k, 0, 0)),
        ],
        bias_far, (mlp, gh),
    )
    mine_rows = micro * share
    passed = flip(jnp.stack([mlp[mine_rows:], gh[mine_rows:]]), CORE)
    layer_out, grad_mid, d0, d1, d2, d3, out_wgrad, sums = between(
        jnp.concatenate([rank_info, own_valid]),
        (mlp[:mine_rows], gh[:mine_rows]),
        (passed[0], passed[1]),
        mid, attn, out_grad, mod_blocks, down_bias[None], out_full, parts, groups,
    )
    grads = [d0] + [turn(d, -k) for k, d in ((1, d1), (2, d2), (3, d3))]

    pieces = []
    shares = []
    for m in range(micro):
        info = jnp.stack([rank, whole[m]])
        dq, dk, dv, partial = attend_back(m, info, query, key, value, lse, grads, qkv_weight)
        pieces.append((dq, dk, dv))
        shares.append(lax.psum_scatter(partial, "tensor", scatter_dimension=0, tiled=True))
    tokens_grad, sums_one = finish(
        rank_info, jnp.stack(shares), tokens, mod_blocks, grad_mid, groups
    )

    wu = wu.reshape(groups - 1, 4, piece, width)
    wd = wd.reshape(groups - 1, 4, piece, width)
    wu0 = by_quarter(wu0.reshape(1, 4, piece, width), quarter, 1)
    wd0 = by_quarter(wd0.reshape(1, 4, piece, width), quarter, 1)
    wu = jnp.concatenate([wu0, wu])
    wd = jnp.concatenate([wd0, wd])
    wu = add(wu[:, :2], flip(wu[:, 2:], SIDE_Y))
    wd = wd.reshape(groups, 2, 2, piece, width)
    wd = add(wd[:, :, 0], flip(wd[:, :, 1], SIDE_X))
    wu = add(wu[:, 0], flip(wu[:, 1], SIDE_X))
    wd = add(wd[:, 0], flip(wd[:, 1], SIDE_Y))
    summed = jnp.stack([wu, wd], axis=1)
    arrived = [summed[0]] + [turn(summed[k], -k) for k in (1, 2, 3)]
    total = sum(a.astype(F32) for a in arrived).astype(BF)
    bit = 8
    while bit < dp:
        total = add(total, flip(total, bit))
        bit *= 2
    both = jnp.stack([total, flip(total, SIDE_X)], axis=1)
    both = jnp.concatenate([both, flip(both, SIDE_Y)], axis=1)
    both = by_quarter(both, quarter, 1).reshape(2, half, width)
    away = flip(both, CORE)
    low = jnp.where(core == 0, both, away)
    high = jnp.where(core == 0, away, both)
    both = jnp.concatenate([low, high], axis=1).astype(F32)
    up_weight_grad = both[0].T
    down_weight_grad = both[1]

    stacked = [jnp.stack([pieces[m][i] for m in range(micro)]) for i in range(3)]
    attn_grads = [
        jnp.einsum("mte,mtd->ed", s, hidden_one, preferred_element_type=F32).astype(BF)
        for s in stacked
    ]
    out_low = out_wgrad.astype(BF)
    out_mine = [out_low[0]] + [turn(out_low[k], -k) for k in (1, 2, 3)]
    attn_grads.append(sum(a.astype(F32) for a in out_mine).astype(BF))
    block = jnp.concatenate(attn_grads)
    size = block.shape[0] // 2
    for bit in (CORE, SIDE_X, SIDE_Y):
        side = (jnp.bitwise_and(place, bit) > 0).astype(jnp.int32)
        keep = lax.dynamic_slice_in_dim(block, side * size, size, 0)
        give = lax.dynamic_slice_in_dim(block, (1 - side) * size, size, 0)
        block = add(keep, flip(give, bit))
        size //= 2
    bit = 8
    while bit < dp:
        block = add(block, flip(block, bit))
        bit *= 2
    for bit in (SIDE_Y, SIDE_X, CORE):
        side = jnp.bitwise_and(place, bit) > 0
        other = flip(block, bit)
        block = jnp.concatenate(
            [jnp.where(side, other, block), jnp.where(side, block, other)]
        )
    block = block.astype(F32)
    local_width = qkv_weight.shape[2]
    qkv_weight_grad = block[: 3 * local_width].reshape(3, local_width, width).transpose(0, 2, 1)
    out_weight_grad = block[3 * local_width :]

    qv_sums = jnp.stack(
        [jnp.sum(stacked[0].astype(F32), axis=(0, 1)), jnp.sum(stacked[2].astype(F32), axis=(0, 1))]
    )
    bsum_rel = by_quarter(bsum.reshape(groups - 1, 4, piece), quarter, 1).reshape(groups - 1, half)
    up_sums = by_rank(jnp.concatenate([bsum0.reshape(1, half), bsum_rel]), rank, 0)
    early = jnp.concatenate([sums.reshape(-1), up_sums.reshape(-1)])
    late = jnp.concatenate([sums_one.reshape(-1), qv_sums.reshape(-1)])
    early = lax.all_gather(early, ("dp", "tensor"), axis=0).reshape(dp, groups, -1)
    late = lax.all_gather(late, ("dp", "tensor"), axis=0).reshape(dp, groups, -1)
    n_sums = micro * 8 * width
    rows_early = early[:, :, :n_sums].reshape(dp, groups, micro, 8, width)
    rows_late = late[:, :, : micro * 2 * width].reshape(dp, groups, micro, 2, width)
    out_bias_grad = jnp.sum(rows_early[:, :, :, 4], axis=(0, 1, 2))
    down_bias_grad = jnp.sum(rows_early[:, :, :, 5], axis=(0, 1, 2))
    up_all = early[:, :, n_sums:].reshape(dp // 2, 2, groups, groups, half)
    up_all = jnp.sum(lax.dynamic_index_in_dim(up_all, rank, 3, False), axis=(0, 2))
    up_bias_grad = up_all.reshape(part)
    qv_all = late[:, :, micro * 2 * width :].reshape(dp, groups, 2, local_width)
    qv_bias_grad = jnp.sum(lax.dynamic_index_in_dim(qv_all, rank, 1, False), axis=0)

    segments = lax.all_gather(segment, "dp", axis=0)
    pick = (segments[..., None] == jnp.arange(slots)).astype(F32)
    mod_rows = jnp.concatenate([rows_late, rows_early[:, :, :, :4]], axis=3)
    mod_rows = mod_rows.reshape(dp, groups, micro, 6 * width)
    own_columns = lax.dynamic_slice_in_dim(mod_rows, rank * columns, columns, 3)
    mod_grad = jnp.sum(
        pick.transpose(0, 2, 1, 3)[..., None] * own_columns[:, :, :, None], axis=1
    )
    ada_bias_grad = jnp.sum(mod_grad, axis=(0, 1, 2))
    mod_low = mod_grad.astype(BF).reshape(dp, micro * slots, columns)
    acts = lax.all_gather(cond_act, "dp", axis=0)
    ada_weight_grad = jnp.einsum("psd,pse->de", acts, mod_low, preferred_element_type=F32)
    own_mod = lax.dynamic_index_in_dim(mod_low, place, 0, False)
    cond_part = jnp.einsum("se,de->sd", own_mod, ada_weight, preferred_element_type=F32)
    cond_grad = (cond_part + turn(cond_part, 1) + turn(cond_part, 2) + turn(cond_part, 3)).reshape(
        micro, slots, width
    )
    sigmoid = jax.nn.sigmoid(cond_float)
    conditioning_grad = cond_grad * (sigmoid * (1.0 + cond_float * (1.0 - sigmoid)))

    return (
        layer_out,
        tokens_grad,
        conditioning_grad,
        ada_weight_grad,
        ada_bias_grad,
        qkv_weight_grad,
        qv_bias_grad,
        out_weight_grad,
        out_bias_grad,
        up_weight_grad,
        up_bias_grad,
        down_weight_grad,
        down_bias_grad,
    )


def solution(mesh):
    placed = (
        P(None, "dp", None),
        P(None, "dp", None),
        P(None, "dp"),
        P(None, "dp", None),
        P(None, "tensor"),
        P("tensor"),
        P(None, None, "tensor"),
        P(None, "tensor"),
        P("tensor", None),
        P(),
        P(None, "tensor"),
        P("tensor"),
        P("tensor", None),
        P(),
    )
    return jax.shard_map(
        local,
        mesh=mesh,
        in_specs=placed,
        out_specs=(
            P(None, ("dp", "tensor"), None),
            P(None, ("dp", "tensor"), None),
            P(None, "dp", None),
            P(None, "tensor"),
            P("tensor"),
            P(None, None, "tensor"),
            P(None, "tensor"),
            P("tensor", None),
            P(),
            P(None, "tensor"),
            P("tensor"),
            P("tensor", None),
            P(),
        ),
        check_vma=False,
    )
```

```python
import functools
import math

import jax
import jax.numpy as jnp
from jax import lax
from jax.experimental import pallas as pl
from jax.experimental.pallas import tpu as pltpu
from jax.sharding import Mesh
from jax.sharding import PartitionSpec as P

HEAD_DIM = 72
EPSILON = 1e-06
LOG2E = math.log2(math.e)
GELU_C = 0.7978845608
GELU_A = 0.044715
VMEM = 60 * 1024 * 1024
BF = jnp.bfloat16
F32 = jnp.float32


def nn(a, b):
    return lax.dot_general(a, b, (((1,), (0,)), ((), ())), preferred_element_type=F32)


def nt(a, b):
    return lax.dot_general(a, b, (((1,), (1,)), ((), ())), preferred_element_type=F32)


def tn(a, b):
    return lax.dot_general(a, b, (((0,), (0,)), ((), ())), preferred_element_type=F32)


def params():
    return pltpu.CompilerParams(vmem_limit_bytes=VMEM)


def cost(micros):
    return pl.CostEstimate(
        flops=int(micros * 1.15e9), bytes_accessed=int(micros * 1e5), transcendentals=0
    )


ANY = pl.BlockSpec(memory_space=pl.ANY)


def shape(dims, dtype):
    return pltpu.HBM(tuple(dims), dtype)


def skipping(kernel, start, count):
    def body(*refs):
        kernel(*refs[:start], *refs[start + count :])

    return body


def simple(kernel, outs, operands, scalars=None, after=(), scratch=(), name="glue", micros=3):
    count = len(after)
    n_scalar = 0 if scalars is None else 1
    n_in = len(operands)

    body = skipping(kernel, n_scalar + n_in, count)

    def whole(array):
        zeros = (0,) * len(array.shape)
        return pl.BlockSpec(array.shape, lambda *_: zeros)

    return pl.pallas_call(
        body,
        grid_spec=pltpu.PrefetchScalarGridSpec(
            num_scalar_prefetch=n_scalar,
            grid=(1,),
            in_specs=[whole(a) for a in operands] + [ANY] * count,
            out_specs=[whole(o) for o in outs],
            scratch_shapes=list(scratch),
        ),
        out_shape=list(outs),
        compiler_params=params(),
        cost_estimate=cost(micros),
        name=name,
    )(*([] if scalars is None else [scalars]), *operands, *after)


def normalize(values):
    centred = values - jnp.mean(values, axis=-1, keepdims=True)
    inverse = lax.rsqrt(jnp.mean(centred * centred, axis=-1, keepdims=True) + EPSILON)
    return centred * inverse, inverse


def norm_backward(grad, normed, inverse):
    return inverse * (
        grad
        - jnp.mean(grad, axis=-1, keepdims=True)
        - normed * jnp.mean(grad * normed, axis=-1, keepdims=True)
    )


def project_kernel(tok_ref, mod_ref, w_ref, bias_ref, hid_ref, q_ref, k_ref, v_ref):
    heads = q_ref.shape[1]
    size = q_ref.shape[3]
    share = tok_ref.shape[1] // mod_ref.shape[0]
    for i in range(mod_ref.shape[0]):
        rows = slice(i * share, (i + 1) * share)
        normed, _ = normalize(tok_ref[0, rows].astype(F32))
        hid_ref[0, rows] = (normed * (1.0 + mod_ref[i, 1:2, :]) + mod_ref[i, 0:1, :]).astype(BF)
    proj = (nt(hid_ref[0], w_ref[...]) + bias_ref[...]).astype(BF)
    for which, out in enumerate((q_ref, k_ref, v_ref)):
        for h in range(heads):
            at = (which * heads + h) * size
            out[0, h] = proj[:, at : at + size]


def project(tokens, mod_blocks, qkv_weight, qv_bias, blocks):
    micro, rows, width = tokens.shape
    share = rows // blocks
    local = qkv_weight.shape[1]
    heads = local // HEAD_DIM
    weight = qkv_weight.reshape(3 * local, width)
    bias = jnp.concatenate([qv_bias[0], jnp.zeros_like(qv_bias[0]), qv_bias[1]])[None]
    head_shape = shape((micro, heads, rows, HEAD_DIM), BF)
    head_spec = pl.BlockSpec((1, heads, 2 * share, HEAD_DIM), lambda m, b: (m, 0, b, 0))
    return pl.pallas_call(
        project_kernel,
        grid=(micro, blocks // 2),
        in_specs=[
            pl.BlockSpec((1, 2 * share, width), lambda m, b: (m, b, 0)),
            pl.BlockSpec((2, 6, width), lambda m, b: (m * (blocks // 2) + b, 0, 0)),
            pl.BlockSpec(weight.shape, lambda m, b: (0, 0)),
            pl.BlockSpec(bias.shape, lambda m, b: (0, 0)),
        ],
        out_specs=[
            pl.BlockSpec((1, 2 * share, width), lambda m, b: (m, b, 0)),
            head_spec,
            head_spec,
            head_spec,
        ],
        out_shape=[shape(tokens.shape, BF), head_shape, head_shape, head_shape],
        compiler_params=params(),
        cost_estimate=cost(0.01),
        name="project",
    )(tokens, mod_blocks, weight, bias)


def attend_kernel(info_ref, q_ref, k_ref, v_ref, a0, a1, a2, a3, lse_ref):
    _, heads, rows, size = q_ref.shape
    share = rows // 4
    rank = info_ref[0]
    whole = info_ref[1 + pl.program_id(0)]
    factor = size ** (-0.5) * LOG2E
    lane = lax.broadcasted_iota(jnp.int32, (share, 128), 1)

    def run(full):
        for shift, att_ref in enumerate((a0, a1, a2, a3)):
            block = pl.ds(pl.multiple_of(lax.rem(rank + shift, 4) * share, share), share)
            span = slice(None) if full else block
            logs = jnp.zeros((share, 128), F32)
            outs = []
            for h in range(heads):
                scores = nt(q_ref[0, h, block, :], k_ref[0, h, span, :])
                top = jnp.max(scores, axis=-1, keepdims=True)
                weight = jnp.exp2((scores - top) * factor)
                total = jnp.sum(weight, axis=-1, keepdims=True)
                out = nn(weight.astype(BF), v_ref[0, h, span, :])
                outs.append((out * (1.0 / total)).astype(BF))
                logs = jnp.where(lane == h, top * factor + jnp.log2(total), logs)
            att_ref[0] = pack_rows(jnp.concatenate(outs, axis=1))
            lse_ref[0, :, block] = logs.T[0:heads, :]

    @pl.when(whole == 1)
    def _():
        run(True)

    @pl.when(whole == 0)
    def _():
        run(False)


def attend(info, query, key, value, after=()):
    micro, heads, rows, size = query.shape
    share = rows // 4
    full = pl.BlockSpec((1, heads, rows, size), lambda m, s: (m, 0, 0, 0))
    packed = (share // 4, 4 * heads * size)
    part = pl.BlockSpec((1, *packed), lambda m, s: (m, 0, 0))
    return pl.pallas_call(
        skipping(attend_kernel, 4, len(after)),
        grid_spec=pltpu.PrefetchScalarGridSpec(
            num_scalar_prefetch=1,
            grid=(micro,),
            in_specs=[full] * 3 + [ANY] * len(after),
            out_specs=[part] * 4 + [pl.BlockSpec((1, heads, rows), lambda m, s: (m, 0, 0))],
        ),
        out_shape=[shape((micro, *packed), BF)] * 4 + [shape((micro, heads, rows), F32)],
        compiler_params=params(),
        cost_estimate=cost(0.01),
        name="attend",
    )(info, query, key, value, *after)


def middle_kernel(info_ref, a0, a1, a2, a3, w_ref, bias_ref, tok_ref, mod_ref, attn_ref, mid_ref, hid_ref):
    rank = info_ref[0]
    total = bias_ref[0:1, :]
    for shift, part in enumerate((a0, a1, a2, a3)):
        total = total + nn(unpack_rows(part[0]), w_ref[lax.rem(rank + 4 - shift, 4)])
    attn_ref[0] = total
    mid = tok_ref[0].astype(F32) + mod_ref[0, 2:3, :] * total
    mid_ref[0] = mid
    normed, _ = normalize(mid)
    hid_ref[0] = (normed * (1.0 + mod_ref[0, 4:5, :]) + mod_ref[0, 3:4, :]).astype(BF)


def middle(info, parts, out_full, out_bias, tokens, mod_blocks, blocks, after=()):
    micro = parts[0].shape[0]
    share, width = tokens.shape[1] // blocks, tokens.shape[2]
    part = pl.BlockSpec((1, *parts[0].shape[1:]), lambda m, s: (m, 0, 0))
    row = pl.BlockSpec((1, share, width), lambda m, s: (m, 0, 0))
    return pl.pallas_call(
        skipping(middle_kernel, 9, len(after)),
        grid_spec=pltpu.PrefetchScalarGridSpec(
            num_scalar_prefetch=1,
            grid=(micro,),
            in_specs=[part] * 4
            + [
                pl.BlockSpec(out_full.shape, lambda m, s: (0, 0, 0)),
                pl.BlockSpec((1, width), lambda m, s: (0, 0)),
                pl.BlockSpec((1, share, width), lambda m, s: (m, s[0], 0)),
                pl.BlockSpec((1, 6, width), lambda m, s: (m * blocks + s[0], 0, 0)),
            ]
            + [ANY] * len(after),
            out_specs=[row, row, row],
        ),
        out_shape=[
            shape((micro, share, width), F32),
            shape((micro, share, width), F32),
            shape((micro, share, width), BF),
        ],
        compiler_params=params(),
        cost_estimate=cost(8),
        name="middle",
    )(info, *parts, out_full, out_bias, tokens, mod_blocks, *after)


def feed_kernel(first, kinds, *refs):
    xo, xt, go, gt = refs[:4]
    at = 4
    weights = []
    for kind in kinds:
        weights.append(refs[at : at + kind])
        at += kind
    bias_ref = refs[at]
    at += 1
    if not first:
        carry = refs[at : at + 4]
        at += 4
    mo, mt, ho, ht, wuk, wus, wdk, wds, bsum_ref = refs[at : at + 9]
    xs, gs, us, ds, acts, dps, wtmp = refs[at + 9 :]
    half = xo.shape[0]
    units = us.shape[0]
    piece = units // 4
    step = pl.program_id(0)
    chunk = 512

    @pl.when(step == 0)
    def _():
        xs[:half] = xo[...]
        xs[half:] = xt[...]
        gs[:half] = go[...]
        gs[half:] = gt[...]
        if first:
            for ref in (mo, mt, ho, ht):
                ref[...] = jnp.zeros_like(ref)
        else:
            for ref, old in zip((mo, mt, ho, ht), carry):
                ref[...] = old[...]

    index = 0
    for parts in weights:
        blocks = [parts]
        if len(parts[0].shape) == 3:
            blocks = [[ref.at[i] for ref in parts] for i in range(parts[0].shape[0])]
        for block in blocks:

            @pl.when(step == index)
            def _(block=block):
                if len(block) == 2:
                    us[...] = block[0][...]
                    ds[...] = block[1][...]
                    return
                for j, ref in enumerate(block):
                    us[j * piece : (j + 1) * piece] = ref[:piece]
                    ds[j * piece : (j + 1) * piece] = ref[piece:]

            index += 1

    bias = bias_ref[0]

    def rows_step(base, mlp_ref, gh_ref):
        def run(i, sums):
            rows = pl.ds(pl.multiple_of(base + i * chunk, chunk), chunk)
            out = pl.ds(pl.multiple_of(i * chunk, chunk), chunk)
            pre = nt(xs[rows, :], us[...]) + bias
            square = pre * pre
            tanh = jnp.tanh(GELU_C * pre * (1.0 + GELU_A * square))
            act = (0.5 * pre * (1.0 + tanh)).astype(BF)
            acts[rows, :] = act
            slope = 0.5 * (1.0 + tanh) + (0.5 * GELU_C) * pre * (1.0 - tanh * tanh) * (
                1.0 + 3.0 * GELU_A * square
            )
            dpre = nt(gs[rows, :], ds[...]) * slope
            low = dpre.astype(BF)
            dps[rows, :] = low
            mlp_ref[out, :] = mlp_ref[out, :] + nn(act, ds[...])
            gh_ref[out, :] = gh_ref[out, :] + nn(low, us[...])
            return sums + jnp.sum(dpre, axis=0, keepdims=True)

        return run

    sums = jnp.zeros((1, units), F32)
    sums = lax.fori_loop(0, half // chunk, rows_step(0, mo, ho), sums)
    sums = lax.fori_loop(0, half // chunk, rows_step(half, mt, ht), sums)
    bsum_ref[0] = sums
    for lhs, rhs, order in ((dps, xs, ((wuk, 0), (wuk, 1), (wus, 0), (wus, 1))),
                            (acts, gs, ((wdk, 0), (wds, 0), (wdk, 1), (wds, 1)))):
        for start in range(0, units, 256):
            stop = min(start + 256, units)
            wtmp[start:stop] = tn(lhs[:, start:stop], rhs[...]).astype(BF)
        for j, (ref, place) in enumerate(order):
            ref[0, place] = wtmp[j * piece : (j + 1) * piece]


def feed(own_x, other_x, own_g, other_g, weights, bias, carry):
    half, width = own_x.shape
    count, _, units = bias.shape
    piece = units // 4
    first = carry is None

    def whole(array):
        zeros = (0,) * len(array.shape)
        return pl.BlockSpec(array.shape, lambda k: zeros)

    operands = [own_x, other_x, own_g, other_g]
    for parts in weights:
        operands += list(parts)
    in_specs = [whole(a) for a in operands]
    in_specs.append(pl.BlockSpec((1, 1, units), lambda k: (k, 0, 0)))
    operands.append(bias)
    acc = pl.BlockSpec((half, width), lambda k: (0, 0))
    if not first:
        in_specs += [acc] * 4
        operands += list(carry)
    wspec = pl.BlockSpec((1, 2, piece, width), lambda k: (k, 0, 0, 0))
    return pl.pallas_call(
        functools.partial(feed_kernel, first, tuple(len(p) for p in weights)),
        grid=(count,),
        in_specs=in_specs,
        out_specs=[acc] * 4 + [wspec] * 4 + [pl.BlockSpec((1, 1, units), lambda k: (k, 0, 0))],
        out_shape=[shape((half, width), F32)] * 4
        + [shape((count, 2, piece, width), BF)] * 4
        + [shape((count, 1, units), F32)],
        scratch_shapes=[
            pltpu.VMEM((2 * half, width), BF),
            pltpu.VMEM((2 * half, width), BF),
            pltpu.VMEM((units, width), BF),
            pltpu.VMEM((units, width), BF),
            pltpu.VMEM((2 * half, units), BF),
            pltpu.VMEM((2 * half, units), BF),
            pltpu.VMEM((units, width), BF),
        ],
        compiler_params=params(),
        cost_estimate=cost(34),
        name="feed",
    )(*operands)


def between_kernel(
    info_ref, gho, ght, mlpo, mlpt, mid_ref, attn_ref, og_ref, mod_ref, dbias_ref, w_ref,
    a0, a1, a2, a3, layer_ref, gmid_ref, d0, d1, d2, d3, wkeep, wsend, sums_ref, wout_ref,
):
    rank = info_ref[0]
    micro = pl.program_id(0)
    valid = info_ref[1 + micro].astype(F32)
    mod = mod_ref[0]
    mid = mid_ref[0]
    attn = attn_ref[0]
    normed, inverse = normalize(mid)
    mlp_out = mlpo[...] + mlpt[...] + dbias_ref[0:1, :]
    layer_ref[0] = (valid * (mid + mod[5:6, :] * mlp_out)).astype(BF)
    grad_y = og_ref[0].astype(F32) * valid
    grad_hidden = gho[...] + ght[...]
    grad_mid = grad_y + norm_backward(grad_hidden * (1.0 + mod[4:5, :]), normed, inverse)
    gmid_ref[0] = grad_mid
    grad_attn = grad_mid * mod[2:3, :]
    sums_ref[0, 0:1, :] = jnp.sum(grad_mid * attn, axis=0, keepdims=True)
    sums_ref[0, 1:2, :] = jnp.sum(grad_hidden, axis=0, keepdims=True)
    sums_ref[0, 2:3, :] = jnp.sum(grad_hidden * normed, axis=0, keepdims=True)
    sums_ref[0, 3:4, :] = jnp.sum(grad_y * mlp_out, axis=0, keepdims=True)
    sums_ref[0, 4:5, :] = jnp.sum(grad_attn, axis=0, keepdims=True)
    sums_ref[0, 5:6, :] = jnp.sum(grad_y * mod[5:6, :], axis=0, keepdims=True)
    low = grad_attn.astype(BF)
    for shift, (out, part) in enumerate(((d0, a0), (d1, a1), (d2, a2), (d3, a3))):
        out[0] = pack_rows(nt(low, w_ref[lax.rem(rank + 4 - shift, 4)]).astype(BF))
        update = tn(unpack_rows(part[0]), low)
        half = update.shape[0] // 2

        @pl.when(micro == 0)
        def _(shift=shift, update=update):
            wout_ref[shift] = update

        @pl.when(micro > 0)
        def _(shift=shift, update=update):
            wout_ref[shift] = wout_ref[shift] + update

    @pl.when(micro == pl.num_programs(0) - 1)
    def _():
        core = info_ref[3]
        for shift in range(4):
            here = pl.ds(pl.multiple_of(core * half, half), half)
            there = pl.ds(pl.multiple_of((1 - core) * half, half), half)
            wkeep[shift] = wout_ref[shift, here, :].astype(BF)
            wsend[shift] = wout_ref[shift, there, :].astype(BF)


def between(info, feed_own, feed_other, mid, attn, out_grad, mod_blocks, down_bias, out_full, parts, blocks, after=()):
    micro, share, width = mid.shape
    local = parts[0].shape[2] // 4
    half = pl.BlockSpec((share, width), lambda m, s: (m, 0))
    row = pl.BlockSpec((1, share, width), lambda m, s: (m, 0, 0))
    part = pl.BlockSpec((1, *parts[0].shape[1:]), lambda m, s: (m, 0, 0))
    mlp_own, gh_own = feed_own
    mlp_other, gh_other = feed_other
    dshape = shape(parts[0].shape, BF)
    return pl.pallas_call(
        skipping(between_kernel, 15, len(after)),
        grid_spec=pltpu.PrefetchScalarGridSpec(
            num_scalar_prefetch=1,
            grid=(micro,),
            in_specs=[half] * 4
            + [
                row,
                row,
                pl.BlockSpec((1, share, width), lambda m, s: (m, s[0], 0)),
                pl.BlockSpec((1, 6, width), lambda m, s: (m * blocks + s[0], 0, 0)),
                pl.BlockSpec((1, width), lambda m, s: (0, 0)),
                pl.BlockSpec(out_full.shape, lambda m, s: (0, 0, 0)),
            ]
            + [part] * 4
            + [ANY] * len(after),
            out_specs=[row, row, part, part, part, part]
            + [
                pl.BlockSpec((blocks, local // 2, width), lambda m, s: (0, 0, 0)),
                pl.BlockSpec((blocks, local // 2, width), lambda m, s: (0, 0, 0)),
                pl.BlockSpec((1, 8, width), lambda m, s: (m, 0, 0)),
            ],
            scratch_shapes=[pltpu.VMEM((blocks, local, width), F32)],
        ),
        out_shape=[
            shape((micro, share, width), BF),
            shape((micro, share, width), F32),
            dshape,
            dshape,
            dshape,
            dshape,
            shape((blocks, local // 2, width), BF),
            shape((blocks, local // 2, width), BF),
            shape((micro, 8, width), F32),
        ],
        compiler_params=params(),
        cost_estimate=cost(18),
        name="between",
    )(info, gh_own, gh_other, mlp_own, mlp_other, mid, attn, out_grad, mod_blocks, down_bias, out_full, *parts, *after)


def attend_back_kernel(
    last, count, info_ref, q_ref, k_ref, v_ref, lse_ref, g0, g1, g2, g3, w_ref, hid_ref, tok_ref, *refs
):
    if last:
        old_ref, refs = refs[0], refs[1:]
    refs = refs[count:]
    part_ref, refs = refs[0], refs[1:]
    if last:
        sums_ref, bias_ref, wkeep, wsend = refs[:4]
        refs = refs[4:]
    else:
        sums_ref, bias_ref, wout = refs[:3]
        refs = refs[3:]
    dos, dqs, dks, dvs, dq_ref, dk_ref, dv_ref, wtmp = refs
    _, heads, rows, size = q_ref.shape
    share = rows // 4
    local = heads * size
    rank = info_ref[0]
    whole = info_ref[1]
    scale = size ** (-0.5)
    factor = scale * LOG2E
    for shift, grad in enumerate((g0, g1, g2, g3)):
        grad = unpack_rows(grad[0])
        for h in range(heads):
            dos[h, shift] = grad[:, h * size : (h + 1) * size]

    def block_of(shift):
        return pl.multiple_of(lax.rem(rank + shift, 4) * share, share)

    def tile(h, shift, keys, values, keys_t):
        query = q_ref[0, h, pl.ds(block_of(shift), share), :]
        grad = dos[h, shift]
        lse = lse_ref[0, pl.ds(h, 1), pl.ds(block_of(shift), share)]
        probs = jnp.exp2(nt(keys, query) * factor - lse)
        dprobs = nt(values, grad)
        inner = jnp.sum(probs * dprobs, axis=0, keepdims=True)
        dscores = (probs * (dprobs - inner) * scale).astype(BF)
        dqs[h, pl.ds(block_of(shift), share), :] = nn(keys_t, dscores).T.astype(BF)
        return nn(dscores, query), nn(probs.astype(BF), grad)

    @pl.when(whole == 1)
    def _():
        def head(h, carry):
            keys = k_ref[0, h]
            values = v_ref[0, h]
            keys_t = keys.astype(F32).T.astype(BF)
            dkey, dvalue = tile(h, 0, keys, values, keys_t)
            for shift in range(1, 4):
                more_key, more_value = tile(h, shift, keys, values, keys_t)
                dkey = dkey + more_key
                dvalue = dvalue + more_value
            dks[h] = dkey.astype(BF)
            dvs[h] = dvalue.astype(BF)
            return carry

        lax.fori_loop(0, heads, head, 0)

    @pl.when(whole == 0)
    def _():
        def head(h, carry):
            for shift in range(4):
                span = pl.ds(block_of(shift), share)
                keys = k_ref[0, h, span, :]
                values = v_ref[0, h, span, :]
                dkey, dvalue = tile(h, shift, keys, values, keys.astype(F32).T.astype(BF))
                dks[h, span, :] = dkey.astype(BF)
                dvs[h, span, :] = dvalue.astype(BF)
            return carry

        lax.fori_loop(0, heads, head, 0)

    for src, dst in ((dqs, dq_ref), (dks, dk_ref), (dvs, dv_ref)):
        for h in range(heads):
            dst[:, h * size : (h + 1) * size] = src[h]

    def out_rows(i, carry):
        span = pl.ds(pl.multiple_of(i * share, share), share)
        grad = nn(dq_ref[span, :], w_ref[0]) + nn(dk_ref[span, :], w_ref[1]) + nn(dv_ref[span, :], w_ref[2])
        part_ref[span, :] = grad.astype(BF)
        normed, _ = normalize(tok_ref[0, span, :].astype(F32))
        sums_ref[pl.ds(2 * i, 1), :] = jnp.sum(grad, axis=0, keepdims=True)
        sums_ref[pl.ds(2 * i + 1, 1), :] = jnp.sum(grad * normed, axis=0, keepdims=True)
        return carry

    lax.fori_loop(0, rows // share, out_rows, 0)
    bias_ref[...] = jnp.zeros_like(bias_ref)
    bias_ref[0:1, :] = jnp.sum(dq_ref[...].astype(F32), axis=0, keepdims=True)
    bias_ref[1:2, :] = jnp.sum(dv_ref[...].astype(F32), axis=0, keepdims=True)
    for which, ref in enumerate((dq_ref, dk_ref, dv_ref)):
        span = slice(which * local, (which + 1) * local)
        update = tn(ref[...], hid_ref[0])
        if last:
            wtmp[span] = (old_ref[span] + update).astype(BF)
        else:
            wout[span] = update
    if last:
        core = info_ref[2]
        half = 3 * local // 2
        for ref, place in ((wkeep, core), (wsend, 1 - core)):
            ref[:half] = wtmp[pl.ds(pl.multiple_of(place * half, half), half), :]
            ref[half:] = jnp.zeros((ref.shape[0] - half, ref.shape[1]), BF)


def attend_back(micro, info, query, key, value, lse, grads, qkv_weight, hidden, tokens, old=None, after=()):
    _, heads, rows, size = query.shape
    share = rows // 4
    local = heads * size
    width = qkv_weight.shape[2]
    last = old is not None
    full = pl.BlockSpec((1, heads, rows, size), lambda i, s: (micro, 0, 0, 0))
    row = pl.BlockSpec((1, rows, width), lambda i, s: (micro, 0, 0))

    def flat(*dims):
        return pl.BlockSpec(dims, lambda i, s: (0,) * len(dims))

    outs = [((rows, width), BF), ((8, width), F32), ((8, local), F32)]
    if last:
        outs += [((-(-3 * local // 128) * 64, width), BF)] * 2
    else:
        outs += [((3 * local, width), F32)]
    return pl.pallas_call(
        functools.partial(attend_back_kernel, last, len(after)),
        grid_spec=pltpu.PrefetchScalarGridSpec(
            num_scalar_prefetch=1,
            grid=(1,),
            in_specs=[full] * 3
            + [pl.BlockSpec((1, heads, rows), lambda i, s: (micro, 0, 0))]
            + [pl.BlockSpec((1, *grads[0].shape[1:]), lambda i, s: (micro, 0, 0))] * 4
            + [flat(*qkv_weight.shape), row, row]
            + ([flat(3 * local, width)] if last else [])
            + [ANY] * len(after),
            out_specs=[flat(*dims) for dims, _ in outs],
            scratch_shapes=[
                pltpu.VMEM((heads, 4, share, size), BF),
                pltpu.VMEM((heads, rows, size), BF),
                pltpu.VMEM((heads, rows, size), BF),
                pltpu.VMEM((heads, rows, size), BF),
                pltpu.VMEM((rows, local), BF),
                pltpu.VMEM((rows, local), BF),
                pltpu.VMEM((rows, local), BF),
                pltpu.VMEM((3 * local, width), BF),
            ],
        ),
        out_shape=[shape(dims, dtype) for dims, dtype in outs],
        compiler_params=params(),
        cost_estimate=cost(30),
        name="attend_back",
    )(info, query, key, value, lse, *grads, qkv_weight, hidden, tokens, *([old] if last else []), *after)


def finish_kernel(info_ref, grad_ref, tok_ref, mod_ref, gmid_ref, out_ref):
    normed, inverse = normalize(tok_ref[0].astype(F32))
    grad = grad_ref[...].astype(F32)
    out_ref[0] = gmid_ref[0] + norm_backward(grad * (1.0 + mod_ref[0, 1:2, :]), normed, inverse)


def finish(info, micro, grad, tokens, mod_blocks, gmid, blocks, old=None, after=()):
    _, share, width = gmid.shape
    more = ([] if old is None else [old]) + list(after)
    return pl.pallas_call(
        skipping(finish_kernel, 5, len(more)),
        grid_spec=pltpu.PrefetchScalarGridSpec(
            num_scalar_prefetch=1,
            grid=(1,),
            in_specs=[
                pl.BlockSpec((share, width), lambda i, s: (0, 0)),
                pl.BlockSpec((1, share, width), lambda i, s: (micro, s[0], 0)),
                pl.BlockSpec((1, 6, width), lambda i, s: (micro * blocks + s[0], 0, 0)),
                pl.BlockSpec((1, share, width), lambda i, s: (micro, 0, 0)),
            ]
            + [ANY] * len(more),
            out_specs=[pl.BlockSpec((1, share, width), lambda i, s: (micro, 0, 0))],
        ),
        out_shape=[shape(gmid.shape, F32)],
        input_output_aliases={} if old is None else {5: 0},
        compiler_params=params(),
        cost_estimate=cost(3),
        name="finish",
    )(info, grad, tokens, mod_blocks, gmid, *more)[0]


def in_order(row, quarter, piece):
    parts = [row[:, i * piece : (i + 1) * piece] for i in range(4)]
    out = []
    for j in range(4):
        source = jnp.bitwise_xor(quarter, j)
        value = parts[3]
        for i in range(3):
            value = jnp.where(source == i, parts[i], value)
        out.append(value)
    return jnp.concatenate(out, axis=1)


def ada_kernel(info, cond_ref, w_ref, bias_ref, units_ref, small_ref, act_ref):
    value = cond_ref[...].astype(F32)
    act = (value / (1.0 + jnp.exp(-value))).astype(BF)
    act_ref[...] = act
    count = act.shape[0]
    small_ref[...] = jnp.zeros_like(small_ref)
    small_ref[:count] = nt(act, w_ref[...]) + bias_ref[...]
    half = units_ref.shape[1] // 2
    mine = jnp.where(info[1] == 0, units_ref[:, :half], units_ref[:, half:])
    small_ref[count : count + 1, :half] = in_order(mine, info[2], half // 4)


def modulate_kernel(info, s0, s1, s2, s3, mod_ref, far_ref, near_ref, lanes, full):
    rank = info[0]
    for shift, ref in enumerate((s0, s1, s2, s3)):
        lanes[lax.rem(rank + 4 - shift, 4)] = ref[...]
    full[...] = jnp.concatenate([lanes[i] for i in range(4)], axis=1)
    width = mod_ref.shape[2]
    for i in range(mod_ref.shape[0]):
        segment = info[3 + i]
        slot = (i // 4) * 4 + jnp.minimum(segment, 3)
        row = full[pl.ds(slot, 1), :] * (segment < 4).astype(F32)
        for j in range(6):
            mod_ref[i, j : j + 1, :] = row[:, j * width : (j + 1) * width]
    half = far_ref.shape[2]
    for ref, order in ((far_ref, (s2, s1)), (near_ref, (s3, s0))):
        for i, source in enumerate(order):
            ref[i] = source[8:9, :half]


def pile_kernel(info, l0, l1, sums, far, near, out):
    rank = info[0]
    out[...] = jnp.zeros_like(out)
    for m, late in enumerate((l0, l1)):
        for slot in range(4):
            row = 6 * (4 * m + slot)
            for i in range(2):
                total = jnp.zeros((1, out.shape[1]), F32)
                for block in range(4):
                    inside = (info[3 + m * 4 + block] == slot).astype(F32)
                    total = total + inside * late[2 * block + i : 2 * block + i + 1, :]
                out[row + i : row + i + 1, :] = total
            inside = (info[3 + m * 4 + rank] == slot).astype(F32)
            out[row + 2 : row + 6, :] = inside * sums[m, 0:4, :]
    out[48:50, :] = sums[0, 4:6, :] + sums[1, 4:6, :]
    half = far.shape[2]
    for k, (ref, i) in enumerate(((near, 1), (far, 1), (far, 0), (near, 0))):
        out[pl.ds(50 + lax.rem(rank + 4 - k, 4), 1), :half] = ref[i]


def sum_kernel(a, b, out):
    out[...] = a[...] + b[...]


def slots_kernel(info, mine, got, b0, b1, act_ref, pay_ref, low_ref, full):
    rank = info[0]
    width = mine.shape[1]
    total = mine[...] + got[...]
    for row in range(8):
        for i in range(6):
            full[row : row + 1, i * width : (i + 1) * width] = total[6 * row + i : 6 * row + i + 1, :]
    columns = pay_ref.shape[1]
    half = columns - width
    pay_ref[...] = jnp.zeros_like(pay_ref)
    for i in range(4):

        @pl.when(rank == i)
        def _(i=i):
            own = full[:, i * columns : (i + 1) * columns]
            pay_ref[0:8, :] = own
            low_ref[...] = own.astype(BF)
            pay_ref[8:9, width:] = in_order(total[50 + i : 51 + i, :half], info[2], half // 4)

    pay_ref[8:9, :width] = total[48:49]
    pay_ref[9:10, :width] = total[49:50]
    both = b0[0:2, :] + b1[0:2, :]
    pay_ref[9:10, width:] = jnp.concatenate([both[0:1], both[1:2]], axis=1)
    pay_ref[10:18, :width] = act_ref[...].astype(F32)


def tail_kernel(info, pay_ref, ada_ref, ada_b, out_b, down_b, up_b, qv_b):
    width = out_b.shape[1]
    columns = pay_ref.shape[2]
    half = columns - width
    count = pay_ref.shape[0]
    mods = jnp.concatenate([pay_ref[i, 0:8, :] for i in range(count)], axis=0)
    acts = jnp.concatenate([pay_ref[i, 10:18, :width] for i in range(count)], axis=0)
    ada_ref[...] = tn(mods.astype(BF), acts.astype(BF))
    ada_b[...] = jnp.sum(mods, axis=0, keepdims=True)
    sums = [pay_ref[0, 8:10, :], pay_ref[1, 8:10, :]]
    for i in range(2, count):
        sums[i % 2] = sums[i % 2] + pay_ref[i, 8:10, :]
    total = sums[0] + sums[1]
    out_b[...] = total[0:1, :width]
    down_b[...] = total[1:2, :width]
    low = jnp.where(info[1] == 0, sums[0][0:1, width:], sums[1][0:1, width:])
    high = jnp.where(info[1] == 0, sums[1][0:1, width:], sums[0][0:1, width:])
    up_b[...] = jnp.concatenate([low, high], axis=1)
    qv_b[0:1, :] = total[1:2, width : width + half // 2]
    qv_b[1:2, :] = total[1:2, width + half // 2 :]


def pack_kernel(info, up_ref, down_ref, up_out, down_out, mine_ref, turned):
    turned[...] = up_ref[...].T
    half = up_out.shape[0]
    piece = half // 4
    for j in range(4):
        at = info[1] * half + jnp.bitwise_xor(info[2], j) * piece
        rows = pl.ds(pl.multiple_of(at, piece), piece)
        up = turned[rows, :]
        down = down_ref[rows, :]
        up_out[j * piece : (j + 1) * piece] = up
        down_out[j * piece : (j + 1) * piece] = down
        if j == 0:
            mine_ref[:piece] = up
            mine_ref[piece:] = down


def tick_kernel(out):
    out[...] = jnp.zeros_like(out)


def copy_kernel(*refs):
    count = len(refs) // 2
    for source, out in zip(refs[:count], refs[count:]):
        out[...] = source[...]


def stack_kernel(first, second, out):
    out[0] = first[...]
    out[1] = second[...]


def pack_rows(array):
    rows = array.shape[0] // 4
    return jnp.concatenate([array[i * rows : (i + 1) * rows] for i in range(4)], axis=1)


def unpack_rows(array):
    columns = array.shape[1] // 4
    return jnp.concatenate([array[:, i * columns : (i + 1) * columns] for i in range(4)], axis=0)


def plus(a, b):
    return a.astype(F32) + b.astype(F32)


def halve_kernel(uk, ur, dk, dr, u_keep, u_send, d_keep, d_send):
    for keep, got, mine, give in ((uk, ur, u_keep, u_send), (dk, dr, d_keep, d_send)):
        for i in range(keep.shape[0]):
            mine[i] = plus(keep[i, 0], got[i, 0]).astype(BF)
            give[i] = plus(keep[i, 1], got[i, 1]).astype(BF)


def quarter_kernel(uk, ur, dk, dr, first, second):
    piece = uk.shape[1]
    for i, out in enumerate((first, second)):
        out[:piece] = plus(uk[i], ur[i]).astype(BF)
        out[piece:] = plus(dk[i], dr[i]).astype(BF)


def mix_kernel(o_rows, info, uk, us, dk, ds, ok, og, u_keep, u_send, d_keep, d_send, room, sums):
    room[...] = jnp.zeros_like(room)
    for k in range(4):
        sums[...] = plus(ok[k], og[k])
        for i in range(4):
            room[k, jnp.bitwise_xor(info[2], i), :o_rows] = sums[i * o_rows : (i + 1) * o_rows].astype(BF)
    piece = uk.shape[2]
    wide = room.shape[2]
    for keep, send, mine, give, planes, near, far in (
        (uk, us, u_keep, u_send, (0, 1), (0, 1), (2, 3)),
        (dk, ds, d_keep, d_send, (2, 3), (0, 2), (1, 3)),
    ):
        for source, out, order in ((keep, mine, near), (send, give, far)):
            at = 0
            for place in range(2):
                for i in range(2):
                    out[at : at + piece] = source[i, place]
                    at += piece
                for k in planes:
                    out[at : at + wide] = room[k, order[place]]
                    at += wide


def halve_flat_kernel(uk, ur, dk, dr, u_keep, u_send, d_keep, d_send):
    for keep, got, mine, give in ((uk, ur, u_keep, u_send), (dk, dr, d_keep, d_send)):
        half = mine.shape[0]
        mine[...] = plus(keep[:half], got[:half]).astype(BF)
        give[...] = plus(keep[half:], got[half:]).astype(BF)


def last_kernel(uk, ur, dk, dr, third, o1, o2, own):
    wide = o1.shape[0]
    piece = (uk.shape[0] - 2 * wide) // 2
    up = plus(uk[...], ur[...]).astype(BF)
    down = plus(dk[...], dr[...]).astype(BF)
    for out, i in ((third, 0), (own, 1)):
        out[:piece] = up[i * piece : (i + 1) * piece]
        out[piece : 2 * piece] = down[i * piece : (i + 1) * piece]
    own[2 * piece :] = up[2 * piece : 2 * piece + wide]
    o1[...] = up[2 * piece + wide :]
    o2[...] = down[2 * piece : 2 * piece + wide]
    third[2 * piece :] = down[2 * piece + wide :]


def split_rows(total, bit, keep, send):
    half = total.shape[0] // 2
    keep[...] = total[pl.ds(pl.multiple_of(bit * half, half), half), :]
    send[...] = total[pl.ds(pl.multiple_of((1 - bit) * half, half), half), :]


def first_kernel(info, mine, got, keep, send, total):
    total[...] = plus(mine[...], got[...]).astype(BF)
    split_rows(total, jnp.bitwise_and(info[2], 1), keep, send)


def second_kernel(info, mine, got, keep, send, total):
    total[...] = plus(mine[...], got[...]).astype(BF)
    split_rows(total, info[2] >> 1, keep, send)


def merge_kernel(keep, got, own, first, second, third, o1, o2, out):
    at = keep.shape[0]
    out[:at] = plus(keep[...], got[...]).astype(BF)
    rows = first.shape[0]
    out[at : at + rows] = (plus(own[:rows], first[...]) + plus(second[...], third[:rows])).astype(BF)
    out[at + rows :] = (plus(own[rows:], o1[...]) + plus(o2[...], third[rows:])).astype(BF)


def order_kernel(o_rows, w_rows, info, b0, b1, b2, b3, halves, others, room):
    piece = halves.shape[1] // 4
    wide = room.shape[1]
    for j, ref in enumerate((b0, b1, b2, b3)):
        quarter = jnp.bitwise_xor(info[2], j)
        place = 2 * jnp.bitwise_and(quarter, 1) + (quarter >> 1)
        others[pl.ds(pl.multiple_of(place * w_rows, w_rows), w_rows), :] = ref[:w_rows]
        rows = pl.ds(pl.multiple_of(quarter * piece, piece), piece)
        halves[0, rows, :] = ref[w_rows : w_rows + piece]
        halves[1, rows, :] = ref[w_rows + piece : w_rows + 2 * piece]
        room[quarter] = ref[w_rows + 2 * piece :]
    outs = jnp.concatenate([room[i, :o_rows] for i in range(4)], axis=0)
    others[4 * w_rows :] = outs


def spread_kernel(info, own, other, own_o, other_o, up_out, down_out, qkv_out, out_out, turned, total):
    half = own.shape[1]
    here = pl.ds(pl.multiple_of(info[1] * half, half), half)
    there = pl.ds(pl.multiple_of((1 - info[1]) * half, half), half)
    turned[here, :] = own[0]
    turned[there, :] = other[0]
    down_out[here, :] = own[1].astype(F32)
    down_out[there, :] = other[1].astype(F32)
    rows = out_out.shape[0] // 2
    count = total.shape[0] // 2
    for ref, core in ((own_o, info[1]), (other_o, 1 - info[1])):
        out_out[pl.ds(pl.multiple_of(core * rows, rows), rows), :] = ref[ref.shape[0] - rows :].astype(F32)
        total[pl.ds(pl.multiple_of(core * count, count), count), :] = ref[:count]
    local = qkv_out.shape[1]
    for i in range(3):
        qkv_out[i] = total[i * local : (i + 1) * local].astype(F32)
    up_out[...] = turned[...].astype(F32).T


def turn(array, shift):
    count = lax.axis_size("tensor")
    return lax.ppermute(array, "tensor", [(i, (i + shift) % count) for i in range(count)])


def flip(array, axis):
    return lax.ppermute(array, axis, [(0, 1), (1, 0)])


def diagonal(array):
    return lax.ppermute(array, ("y", "x"), [(0, 3), (1, 2), (2, 1), (3, 0)])


def over_rest(array):
    count = lax.axis_size("rest")
    bit = 1
    while bit < count:
        other = lax.ppermute(array, "rest", [(i, i ^ bit) for i in range(count)])
        array = plus(array, other).astype(BF)
        bit *= 2
    return array


DP = ("rest", "y", "x", "core")


def local(
    tokens, conditioning, lengths, out_grad, ada_weight, ada_bias, qkv_weight, qv_bias,
    out_weight, out_bias, up_weight, up_bias, down_weight, down_bias,
):
    groups = lax.axis_size("tensor")
    rank = lax.axis_index("tensor")
    core = lax.axis_index("core")
    quarter = 2 * lax.axis_index("y") + lax.axis_index("x")
    micro, rows, width = tokens.shape
    share = rows // groups
    slots = lengths.shape[1]
    part = up_weight.shape[1]
    half = part // 2
    piece = half // 4
    columns = ada_weight.shape[1]
    local_width = qkv_weight.shape[2]
    ada_turned = ada_weight.T
    qkv_turned = qkv_weight.transpose(0, 2, 1)
    here = jnp.stack([rank, core, quarter]).astype(jnp.int32)

    boundary = jnp.cumsum(lengths, axis=1)
    starts = jnp.arange(groups, dtype=jnp.int32) * share
    segment = jnp.sum((boundary[:, None, :] <= starts[None, :, None]).astype(jnp.int32), axis=2)
    whole = (segment[:, groups - 1] == 0).astype(jnp.int32)
    own_valid = (lax.dynamic_index_in_dim(segment, rank, 1, False) < slots).astype(jnp.int32)
    info = jnp.concatenate([here, segment.reshape(-1)])

    small, cond_act = simple(
        ada_kernel,
        [shape((16, columns), F32), shape((micro * slots, width), BF)],
        [conditioning.reshape(micro * slots, width), ada_turned, ada_bias[None], up_bias[None]],
        info,
        name="ada", micros=0.01,
    )
    smalls = [small] + [turn(small, k) for k in (1, 2, 3)]

    up_near, down_near, mine = simple(
        pack_kernel,
        [shape((half, width), BF), shape((half, width), BF), shape((2 * piece, width), BF)],
        [up_weight, down_weight],
        info,
        after=(cond_act,),
        scratch=[pltpu.VMEM((part, width), BF)],
        name="pack", micros=0.01,
    )
    got = {k: turn(mine, k) for k in (2, 1, 3)}
    out_rows = lax.dynamic_slice_in_dim(out_weight, quarter * (local_width // 4), local_width // 4, 0)
    out_full = lax.all_gather(out_rows, ("tensor", "y", "x"), axis=0, tiled=True)
    out_full = out_full.reshape(groups, local_width, width)

    mod_blocks, bias_a, bias_b = simple(
        modulate_kernel,
        [
            shape((micro * groups, 6, width), F32),
            shape((2, 1, half), F32),
            shape((2, 1, half), F32),
        ],
        smalls,
        info,
        after=(mine,),
        scratch=[pltpu.VMEM((4, 16, columns), F32), pltpu.VMEM((16, 6 * width), F32)],
        name="modulate", micros=0.01,
    )
    hidden_one, query, key, value = project(tokens, mod_blocks, qkv_turned, qv_bias, groups)

    own_gate = lax.dynamic_index_in_dim(
        mod_blocks.reshape(micro, groups, 6, width), rank, 1, False
    )[:, 5:6]
    own_grad = lax.dynamic_slice_in_dim(out_grad, rank * share, share, 1).astype(F32)
    grad_mlp = own_grad * (own_valid.astype(F32)[:, None, None] * own_gate)
    own_g = grad_mlp.astype(BF).reshape(micro * share, width)
    other_g = flip(own_g, "core")

    *att, lse = attend(jnp.concatenate([rank[None], whole]), query, key, value, after=(other_g,))
    parts = [att[0], turn(att[1], 1), turn(att[2], 2), turn(att[3], 3)]

    (two,) = simple(
        stack_kernel, [shape((2, 2 * piece, width), BF)], [got[2], got[1]], after=(lse,), name="two", micros=0.01
    )
    two_parts = (two, flip(two, "x"), flip(two, "y"), diagonal(two))

    def release(arrays, after):
        return simple(
            copy_kernel, [shape(a.shape, a.dtype) for a in arrays], arrays, after=after, name="release"
        )

    attn, mid, hidden_two = middle(
        here, parts, out_full, out_bias[None], tokens, mod_blocks, groups,
    )
    own_x = hidden_two.reshape(micro * share, width)
    other_x = flip(own_x, "core")
    (third,) = release([got[3]], (mid,) + two_parts[1:])
    third_parts = (third, flip(third, "x"), flip(third, "y"), diagonal(third))
    *carry, uk_a, us_a, dk_a, ds_a, bsum_a = feed(
        own_x, other_x, own_g, other_g, [two_parts], bias_a, None
    )
    ur_a = flip(us_a, "y")
    dr_a = flip(ds_a, "x")
    mlp_own, mlp_send, gh_own, gh_send, uk_b, us_b, dk_b, ds_b, bsum_b = feed(
        own_x, other_x, own_g, other_g, [third_parts, (up_near, down_near)], bias_b, carry
    )
    gh_got = flip(gh_send, "core")
    mlp_got = flip(mlp_send, "core")
    piece_shapes = [shape((2, piece, width), BF)] * 4
    uk_a, us_a, dk_a, ds_a = simple(
        halve_kernel, piece_shapes, [uk_a, ur_a, dk_a, dr_a], after=(gh_own,), name="halve", micros=100
    )
    ur_a = flip(us_a, "x")
    dr_a = flip(ds_a, "y")
    layer_out, grad_mid, d0, d1, d2, d3, o_keep, o_send, sums = between(
        jnp.concatenate([here[:1], own_valid, here[1:2]]),
        (mlp_own, gh_own),
        (mlp_got, gh_got),
        mid, attn, out_grad, mod_blocks, down_bias[None], out_full, parts, groups,
        after=(uk_a,),
    )
    grads = [d0] + [turn(d, -k) for k, d in ((1, d1), (2, d2), (3, d3))]
    o_got = flip(o_send, "core")
    o_rows = o_keep.shape[1] // 4
    o_room = -(-o_rows // 16) * 16

    (tick,) = simple(tick_kernel, [shape((8, 128), F32)], [], after=(d0, ur_a, dr_a), name="tick", micros=100)

    side = 4 * piece + 4 * o_room
    u_keep, u_send, d_keep, d_send = simple(
        functools.partial(mix_kernel, o_rows),
        [shape((side, width), BF)] * 4,
        [uk_b, us_b, dk_b, ds_b, o_keep, o_got],
        info,
        after=(tick,),
        scratch=[pltpu.VMEM((4, 4, o_room, width), BF), pltpu.VMEM((4 * o_rows, width), F32)],
        name="mix",
    )
    u_got = flip(u_send, "y")
    d_got = flip(d_send, "x")
    block_shape = shape((2 * piece, width), BF)
    t2, t1 = simple(
        quarter_kernel,
        [block_shape] * 2,
        [uk_a, ur_a, dk_a, dr_a],
        after=(u_send, *grads[1:]),
        name="quarter",
    )
    token = (t1,)
    t2 = turn(t2, -2)
    t1 = turn(t1, -1)

    back_info = [jnp.stack([rank, whole[m], core]) for m in range(micro)]
    part_0, lsum_0, bias_0, old = attend_back(
        0, back_info[0], query, key, value, lse, grads, qkv_turned, hidden_one, tokens, after=token
    )
    share_0 = lax.psum_scatter(part_0, "tensor", scatter_dimension=0, tiled=True)
    half_shape = shape((side // 2, width), BF)
    u_keep, u_send, d_keep, d_send = simple(
        halve_flat_kernel,
        [half_shape] * 4,
        [u_keep, u_got, d_keep, d_got],
        after=(lsum_0, t1, t2),
        name="halve",
    )
    token = (u_keep,)
    u_got = flip(u_send, "x")
    d_got = flip(d_send, "y")
    part_1, lsum_1, bias_1, w_keep, w_send = attend_back(
        1, back_info[1], query, key, value, lse, grads, qkv_turned, hidden_one, tokens, old, after=token
    )
    w_got = flip(w_send, "core")
    def short(kernel, outs, operands, name, after=(), scratch=(), micros=3):
        return simple(
            kernel, outs, operands, info, after=after, scratch=scratch, name=name, micros=micros
        )

    def plain(kernel, outs, operands, name, after=(), micros=3):
        return simple(kernel, outs, operands, after=after, name=name, micros=micros)

    def rows_shape(count):
        return shape((count, width), BF)

    rows_all = w_keep.shape[0]
    keep, send = short(
        first_kernel,
        [rows_shape(rows_all // 2)] * 2,
        [w_keep, w_got],
        "first",
        scratch=[pltpu.VMEM((rows_all, width), BF)],
    )
    (pile,) = short(
        pile_kernel, [shape((56, width), F32)], [lsum_0, lsum_1, sums, bsum_a, bsum_b], "pile", (keep,)
    )
    pile_got = turn(pile, 2)
    o_shape = rows_shape(o_room)
    block_shape = rows_shape(2 * piece + o_room)
    t3, o1, o2, t0 = plain(
        last_kernel,
        [block_shape, o_shape, o_shape, block_shape],
        [u_keep, u_got, d_keep, d_got],
        "last",
        (pile, t1, t2),
    )
    token = (t3,)
    t3 = turn(t3, -3)
    o1 = turn(o1, -1)
    o2 = turn(o2, -2)
    tokens_grad = finish(here, 0, share_0, tokens, mod_blocks, grad_mid, groups, after=token)
    keep, send = short(
        second_kernel,
        [rows_shape(rows_all // 4)] * 2,
        [keep, flip(send, "x")],
        "second",
        (tokens_grad,),
        [pltpu.VMEM((rows_all // 2, width), BF)],
    )
    send_got = flip(send, "y")
    (pile,) = plain(
        sum_kernel, [shape(pile.shape, F32)], [pile, pile_got], "sum", (keep,), micros=40
    )
    pile_far = turn(pile, 1)
    (merged,) = plain(
        merge_kernel,
        [rows_shape(rows_all // 4 + 2 * piece + o_room)],
        [keep, send_got, t0, t1, t2, t3, o1, o2],
        "merge",
        (pile,),
        micros=0.1,
    )
    (part_1,) = release([part_1], (merged,))
    share_1 = lax.psum_scatter(part_1, "tensor", scatter_dimension=0, tiled=True)
    merged = over_rest(merged)
    all_four = [merged, flip(merged, "x"), flip(merged, "y"), diagonal(merged)]
    pay, mod_low = short(
        slots_kernel,
        [shape((24, columns), F32), shape((micro * slots, columns), BF)],
        [pile, pile_far, bias_0, bias_1, cond_act],
        "slots",
        (merged,),
        [pltpu.VMEM((micro * slots, 6 * width), F32)],
        micros=40,
    )
    pay_got = flip(pay, "core")
    cond_part = jnp.dot(mod_low, ada_turned, preferred_element_type=F32)

    cond_grad = cond_part + turn(cond_part, 2)
    cond_grad = cond_grad + turn(cond_grad, 1)

    def pair_kernel(mine, got, out):
        count = mine.shape[0]
        out[:count] = mine[...]
        out[count:] = got[...]

    def pair(mine, got, after=()):
        outs = [shape((2 * mine.shape[0], *mine.shape[1:]), F32)]
        return plain(pair_kernel, outs, [mine, got], "pair", after, micros=20)[0]

    pays = pair(pay[None], pay_got[None])
    pays = pair(pays, flip(pays, "x"))
    pays_got = flip(pays, "y")
    halves, others = short(
        functools.partial(order_kernel, o_rows, rows_all // 4),
        [shape((2, half, width), BF), rows_shape(rows_all + 4 * o_rows)],
        all_four,
        "order",
        (pays, cond_grad),
        [pltpu.VMEM((4, o_room, width), BF)],
        micros=0.1,
    )
    halves_got = flip(halves, "core")
    others_got = flip(others, "core")
    pays = pair(pays, pays_got, (halves,))
    if lax.axis_size("rest") > 1:
        pays = lax.all_gather(pays, "rest", axis=0, tiled=True)
    ada_weight_grad, ada_b, out_b, down_b, up_b, qv_bias_grad = short(
        tail_kernel,
        [
            shape(ada_turned.shape, F32),
            shape((1, columns), F32),
            shape((1, width), F32),
            shape((1, width), F32),
            shape((1, part), F32),
            shape(qv_bias.shape, F32),
        ],
        [pays],
        "tail",
    )
    up_weight_grad, down_weight_grad, qkv_weight_grad, out_weight_grad = short(
        spread_kernel,
        [
            shape(up_weight.shape, F32),
            shape(down_weight.shape, F32),
            shape(qkv_turned.shape, F32),
            shape(out_weight.shape, F32),
        ],
        [halves, halves_got, others, others_got],
        "spread",
        (ada_weight_grad,),
        [pltpu.VMEM((part, width), BF), pltpu.VMEM((3 * local_width, width), BF)],
    )
    cond_float = conditioning.astype(F32)
    sigmoid = jax.nn.sigmoid(cond_float)
    conditioning_grad = cond_grad.reshape(micro, slots, width) * (
        sigmoid * (1.0 + cond_float * (1.0 - sigmoid))
    )
    tokens_grad = finish(
        here, 1, share_1, tokens, mod_blocks, grad_mid, groups, tokens_grad, after=(up_weight_grad,)
    )

    return (
        layer_out,
        tokens_grad,
        conditioning_grad,
        ada_weight_grad.T,
        ada_b[0],
        qkv_weight_grad.transpose(0, 2, 1),
        qv_bias_grad,
        out_weight_grad,
        out_b[0],
        up_weight_grad,
        up_b[0],
        down_weight_grad,
        down_b[0],
    )


def solution(mesh):
    count, groups = mesh.devices.shape
    devices = mesh.devices.reshape(count // 8, 2, 2, 2, groups)
    fine = Mesh(devices, DP + ("tensor",))
    placed = (
        P(None, DP, None),
        P(None, DP, None),
        P(None, DP),
        P(None, DP, None),
        P(None, "tensor"),
        P("tensor"),
        P(None, None, "tensor"),
        P(None, "tensor"),
        P("tensor", None),
        P(),
        P(None, "tensor"),
        P("tensor"),
        P("tensor", None),
        P(),
    )
    return jax.shard_map(
        local,
        mesh=fine,
        in_specs=placed,
        out_specs=(
            P(None, DP + ("tensor",), None),
            P(None, DP + ("tensor",), None),
            P(None, DP, None),
            P(None, "tensor"),
            P("tensor"),
            P(None, None, "tensor"),
            P(None, "tensor"),
            P("tensor", None),
            P(),
            P(None, "tensor"),
            P("tensor"),
            P("tensor", None),
            P(),
        ),
        check_vma=False,
    )
```

```python
import functools
import math

import jax
import jax.numpy as jnp
from jax import lax
from jax.experimental import pallas as pl
from jax.experimental.pallas import tpu as pltpu
from jax.sharding import Mesh
from jax.sharding import PartitionSpec as P

HEAD_DIM = 72
EPSILON = 1e-06
LOG2E = math.log2(math.e)
GELU_C = 0.7978845608
GELU_A = 0.044715
VMEM = 60 * 1024 * 1024
BF = jnp.bfloat16
F32 = jnp.float32


def nn(a, b):
    return lax.dot_general(a, b, (((1,), (0,)), ((), ())), preferred_element_type=F32)


def nt(a, b):
    return lax.dot_general(a, b, (((1,), (1,)), ((), ())), preferred_element_type=F32)


def tn(a, b):
    return lax.dot_general(a, b, (((0,), (0,)), ((), ())), preferred_element_type=F32)


def params():
    return pltpu.CompilerParams(vmem_limit_bytes=VMEM)


def cost(micros):
    return pl.CostEstimate(
        flops=int(micros * 1.15e9), bytes_accessed=int(micros * 1e5), transcendentals=0
    )


ANY = pl.BlockSpec(memory_space=pl.ANY)


def shape(dims, dtype):
    return pltpu.HBM(tuple(dims), dtype)


def skipping(kernel, start, count):
    def body(*refs):
        kernel(*refs[:start], *refs[start + count :])

    return body


def simple(kernel, outs, operands, scalars=None, after=(), scratch=(), name="glue", micros=3):
    count = len(after)
    n_scalar = 0 if scalars is None else 1
    n_in = len(operands)

    body = skipping(kernel, n_scalar + n_in, count)

    def whole(array):
        zeros = (0,) * len(array.shape)
        return pl.BlockSpec(array.shape, lambda *_: zeros)

    return pl.pallas_call(
        body,
        grid_spec=pltpu.PrefetchScalarGridSpec(
            num_scalar_prefetch=n_scalar,
            grid=(1,),
            in_specs=[whole(a) for a in operands] + [ANY] * count,
            out_specs=[whole(o) for o in outs],
            scratch_shapes=list(scratch),
        ),
        out_shape=list(outs),
        compiler_params=params(),
        cost_estimate=cost(micros),
        name=name,
    )(*([] if scalars is None else [scalars]), *operands, *after)


def normalize(values):
    centred = values - jnp.mean(values, axis=-1, keepdims=True)
    inverse = lax.rsqrt(jnp.mean(centred * centred, axis=-1, keepdims=True) + EPSILON)
    return centred * inverse, inverse


def norm_backward(grad, normed, inverse):
    return inverse * (
        grad
        - jnp.mean(grad, axis=-1, keepdims=True)
        - normed * jnp.mean(grad * normed, axis=-1, keepdims=True)
    )


def project_kernel(tok_ref, mod_ref, w_ref, bias_ref, hid_ref, q_ref, k_ref, v_ref):
    heads = q_ref.shape[1]
    size = q_ref.shape[3]
    share = tok_ref.shape[1] // mod_ref.shape[0]
    for i in range(mod_ref.shape[0]):
        rows = slice(i * share, (i + 1) * share)
        normed, _ = normalize(tok_ref[0, rows].astype(F32))
        hid_ref[0, rows] = (normed * (1.0 + mod_ref[i, 1:2, :]) + mod_ref[i, 0:1, :]).astype(BF)
    proj = (nt(hid_ref[0], w_ref[...]) + bias_ref[...]).astype(BF)
    for which, out in enumerate((q_ref, k_ref, v_ref)):
        for h in range(heads):
            at = (which * heads + h) * size
            out[0, h] = proj[:, at : at + size]


def project(tokens, mod_blocks, qkv_weight, qv_bias, blocks):
    micro, rows, width = tokens.shape
    share = rows // blocks
    local = qkv_weight.shape[1]
    heads = local // HEAD_DIM
    weight = qkv_weight.reshape(3 * local, width)
    bias = jnp.concatenate([qv_bias[0], jnp.zeros_like(qv_bias[0]), qv_bias[1]])[None]
    head_shape = shape((micro, heads, rows, HEAD_DIM), BF)
    head_spec = pl.BlockSpec((1, heads, 2 * share, HEAD_DIM), lambda m, b: (m, 0, b, 0))
    return pl.pallas_call(
        project_kernel,
        grid=(micro, blocks // 2),
        in_specs=[
            pl.BlockSpec((1, 2 * share, width), lambda m, b: (m, b, 0)),
            pl.BlockSpec((2, 6, width), lambda m, b: (m * (blocks // 2) + b, 0, 0)),
            pl.BlockSpec(weight.shape, lambda m, b: (0, 0)),
            pl.BlockSpec(bias.shape, lambda m, b: (0, 0)),
        ],
        out_specs=[
            pl.BlockSpec((1, 2 * share, width), lambda m, b: (m, b, 0)),
            head_spec,
            head_spec,
            head_spec,
        ],
        out_shape=[shape(tokens.shape, BF), head_shape, head_shape, head_shape],
        compiler_params=params(),
        cost_estimate=cost(0.01),
        name="project",
    )(tokens, mod_blocks, weight, bias)


def attend_kernel(info_ref, q_ref, k_ref, v_ref, a0, a1, a2, a3, lse_ref):
    _, heads, rows, size = q_ref.shape
    share = rows // 4
    rank = info_ref[0]
    whole = info_ref[1 + pl.program_id(0)]
    factor = size ** (-0.5) * LOG2E
    lane = lax.broadcasted_iota(jnp.int32, (share, 128), 1)

    def run(full):
        for shift, att_ref in enumerate((a0, a1, a2, a3)):
            block = pl.ds(pl.multiple_of(lax.rem(rank + shift, 4) * share, share), share)
            span = slice(None) if full else block
            logs = jnp.zeros((share, 128), F32)
            outs = []
            for h in range(heads):
                scores = nt(q_ref[0, h, block, :], k_ref[0, h, span, :])
                top = jnp.max(scores, axis=-1, keepdims=True)
                weight = jnp.exp2((scores - top) * factor)
                total = jnp.sum(weight, axis=-1, keepdims=True)
                out = nn(weight.astype(BF), v_ref[0, h, span, :])
                outs.append((out * (1.0 / total)).astype(BF))
                logs = jnp.where(lane == h, top * factor + jnp.log2(total), logs)
            att_ref[0] = pack_rows(jnp.concatenate(outs, axis=1))
            lse_ref[0, :, block] = logs.T[0:heads, :]

    @pl.when(whole == 1)
    def _():
        run(True)

    @pl.when(whole == 0)
    def _():
        run(False)


def attend(info, query, key, value, after=()):
    micro, heads, rows, size = query.shape
    share = rows // 4
    full = pl.BlockSpec((1, heads, rows, size), lambda m, s: (m, 0, 0, 0))
    packed = (share // 4, 4 * heads * size)
    part = pl.BlockSpec((1, *packed), lambda m, s: (m, 0, 0))
    return pl.pallas_call(
        skipping(attend_kernel, 4, len(after)),
        grid_spec=pltpu.PrefetchScalarGridSpec(
            num_scalar_prefetch=1,
            grid=(micro,),
            in_specs=[full] * 3 + [ANY] * len(after),
            out_specs=[part] * 4 + [pl.BlockSpec((1, heads, rows), lambda m, s: (m, 0, 0))],
        ),
        out_shape=[shape((micro, *packed), BF)] * 4 + [shape((micro, heads, rows), F32)],
        compiler_params=params(),
        cost_estimate=cost(0.01),
        name="attend",
    )(info, query, key, value, *after)


def middle_kernel(info_ref, a0, a1, a2, a3, w_ref, bias_ref, tok_ref, mod_ref, attn_ref, mid_ref, hid_ref):
    rank = info_ref[0]
    total = bias_ref[0:1, :]
    for shift, part in enumerate((a0, a1, a2, a3)):
        total = total + nn(unpack_rows(part[0]), w_ref[lax.rem(rank + 4 - shift, 4)])
    attn_ref[0] = total
    mid = tok_ref[0].astype(F32) + mod_ref[0, 2:3, :] * total
    mid_ref[0] = mid
    normed, _ = normalize(mid)
    hid_ref[0] = (normed * (1.0 + mod_ref[0, 4:5, :]) + mod_ref[0, 3:4, :]).astype(BF)


def middle(info, parts, out_full, out_bias, tokens, mod_blocks, blocks, after=()):
    micro = parts[0].shape[0]
    share, width = tokens.shape[1] // blocks, tokens.shape[2]
    part = pl.BlockSpec((1, *parts[0].shape[1:]), lambda m, s: (m, 0, 0))
    row = pl.BlockSpec((1, share, width), lambda m, s: (m, 0, 0))
    return pl.pallas_call(
        skipping(middle_kernel, 9, len(after)),
        grid_spec=pltpu.PrefetchScalarGridSpec(
            num_scalar_prefetch=1,
            grid=(micro,),
            in_specs=[part] * 4
            + [
                pl.BlockSpec(out_full.shape, lambda m, s: (0, 0, 0)),
                pl.BlockSpec((1, width), lambda m, s: (0, 0)),
                pl.BlockSpec((1, share, width), lambda m, s: (m, s[0], 0)),
                pl.BlockSpec((1, 6, width), lambda m, s: (m * blocks + s[0], 0, 0)),
            ]
            + [ANY] * len(after),
            out_specs=[row, row, row],
        ),
        out_shape=[
            shape((micro, share, width), F32),
            shape((micro, share, width), F32),
            shape((micro, share, width), BF),
        ],
        compiler_params=params(),
        cost_estimate=cost(8),
        name="middle",
    )(info, *parts, out_full, out_bias, tokens, mod_blocks, *after)


def feed_kernel(first, kinds, *refs):
    xo, xt, go, gt = refs[:4]
    at = 4
    weights = []
    for kind in kinds:
        weights.append(refs[at : at + kind])
        at += kind
    bias_ref = refs[at]
    at += 1
    if not first:
        carry = refs[at : at + 4]
        at += 4
    mo, mt, ho, ht, wuk, wus, wdk, wds, bsum_ref = refs[at : at + 9]
    xs, gs, us, ds, acts, dps, wtmp = refs[at + 9 :]
    half = xo.shape[0]
    units = us.shape[0]
    piece = units // 4
    step = pl.program_id(0)
    chunk = 512

    @pl.when(step == 0)
    def _():
        xs[:half] = xo[...]
        xs[half:] = xt[...]
        gs[:half] = go[...]
        gs[half:] = gt[...]
        if first:
            for ref in (mo, mt, ho, ht):
                ref[...] = jnp.zeros_like(ref)
        else:
            for ref, old in zip((mo, mt, ho, ht), carry):
                ref[...] = old[...]

    index = 0
    for parts in weights:
        blocks = [parts]
        if len(parts[0].shape) == 3:
            blocks = [[ref.at[i] for ref in parts] for i in range(parts[0].shape[0])]
        for block in blocks:

            @pl.when(step == index)
            def _(block=block):
                if len(block) == 2:
                    us[...] = block[0][...]
                    ds[...] = block[1][...]
                    return
                for j in range(4):
                    up = block[j]
                    down = block[-1] if j == 3 else block[j]
                    us[j * piece : (j + 1) * piece] = up[:piece]
                    ds[j * piece : (j + 1) * piece] = down[down.shape[0] - piece :]

            index += 1

    bias = bias_ref[0]

    def rows_step(base, mlp_ref, gh_ref):
        def run(i, sums):
            rows = pl.ds(pl.multiple_of(base + i * chunk, chunk), chunk)
            out = pl.ds(pl.multiple_of(i * chunk, chunk), chunk)
            pre = nt(xs[rows, :], us[...]) + bias
            square = pre * pre
            tanh = jnp.tanh(GELU_C * pre * (1.0 + GELU_A * square))
            act = (0.5 * pre * (1.0 + tanh)).astype(BF)
            acts[rows, :] = act
            slope = 0.5 * (1.0 + tanh) + (0.5 * GELU_C) * pre * (1.0 - tanh * tanh) * (
                1.0 + 3.0 * GELU_A * square
            )
            dpre = nt(gs[rows, :], ds[...]) * slope
            low = dpre.astype(BF)
            dps[rows, :] = low
            mlp_ref[out, :] = mlp_ref[out, :] + nn(act, ds[...])
            gh_ref[out, :] = gh_ref[out, :] + nn(low, us[...])
            return sums + jnp.sum(dpre, axis=0, keepdims=True)

        return run

    sums = jnp.zeros((1, units), F32)
    sums = lax.fori_loop(0, half // chunk, rows_step(0, mo, ho), sums)
    sums = lax.fori_loop(0, half // chunk, rows_step(half, mt, ht), sums)
    bsum_ref[0] = sums
    for lhs, rhs, order in ((dps, xs, ((wuk, 0), (wuk, 1), (wus, 0), (wus, 1))),
                            (acts, gs, ((wdk, 0), (wds, 0), (wdk, 1), (wds, 1)))):
        for start in range(0, units, 256):
            stop = min(start + 256, units)
            wtmp[start:stop] = tn(lhs[:, start:stop], rhs[...]).astype(BF)
        for j, (ref, place) in enumerate(order):
            ref[0, place] = wtmp[j * piece : (j + 1) * piece]


def feed(own_x, other_x, own_g, other_g, weights, bias, carry):
    half, width = own_x.shape
    count, _, units = bias.shape
    piece = units // 4
    first = carry is None

    def whole(array):
        zeros = (0,) * len(array.shape)
        return pl.BlockSpec(array.shape, lambda k: zeros)

    operands = [own_x, other_x, own_g, other_g]
    for parts in weights:
        operands += list(parts)
    in_specs = [whole(a) for a in operands]
    in_specs.append(pl.BlockSpec((1, 1, units), lambda k: (k, 0, 0)))
    operands.append(bias)
    acc = pl.BlockSpec((half, width), lambda k: (0, 0))
    if not first:
        in_specs += [acc] * 4
        operands += list(carry)
    wspec = pl.BlockSpec((1, 2, piece, width), lambda k: (k, 0, 0, 0))
    return pl.pallas_call(
        functools.partial(feed_kernel, first, tuple(len(p) for p in weights)),
        grid=(count,),
        in_specs=in_specs,
        out_specs=[acc] * 4 + [wspec] * 4 + [pl.BlockSpec((1, 1, units), lambda k: (k, 0, 0))],
        out_shape=[shape((half, width), F32)] * 4
        + [shape((count, 2, piece, width), BF)] * 4
        + [shape((count, 1, units), F32)],
        scratch_shapes=[
            pltpu.VMEM((2 * half, width), BF),
            pltpu.VMEM((2 * half, width), BF),
            pltpu.VMEM((units, width), BF),
            pltpu.VMEM((units, width), BF),
            pltpu.VMEM((2 * half, units), BF),
            pltpu.VMEM((2 * half, units), BF),
            pltpu.VMEM((units, width), BF),
        ],
        compiler_params=params(),
        cost_estimate=cost(34),
        name="feed",
    )(*operands)


def between_kernel(
    info_ref, gho, ght, mlpo, mlpt, mid_ref, attn_ref, og_ref, mod_ref, dbias_ref, w_ref,
    a0, a1, a2, a3, layer_ref, gmid_ref, d0, d1, d2, d3, wkeep, wsend, sums_ref, wout_ref,
):
    rank = info_ref[0]
    micro = pl.program_id(0)
    valid = info_ref[1 + micro].astype(F32)
    mod = mod_ref[0]
    mid = mid_ref[0]
    attn = attn_ref[0]
    normed, inverse = normalize(mid)
    mlp_out = mlpo[...] + mlpt[...] + dbias_ref[0:1, :]
    layer_ref[0] = (valid * (mid + mod[5:6, :] * mlp_out)).astype(BF)
    grad_y = og_ref[0].astype(F32) * valid
    grad_hidden = gho[...] + ght[...]
    grad_mid = grad_y + norm_backward(grad_hidden * (1.0 + mod[4:5, :]), normed, inverse)
    gmid_ref[0] = grad_mid
    grad_attn = grad_mid * mod[2:3, :]
    sums_ref[0, 0:1, :] = jnp.sum(grad_mid * attn, axis=0, keepdims=True)
    sums_ref[0, 1:2, :] = jnp.sum(grad_hidden, axis=0, keepdims=True)
    sums_ref[0, 2:3, :] = jnp.sum(grad_hidden * normed, axis=0, keepdims=True)
    sums_ref[0, 3:4, :] = jnp.sum(grad_y * mlp_out, axis=0, keepdims=True)
    sums_ref[0, 4:5, :] = jnp.sum(grad_attn, axis=0, keepdims=True)
    sums_ref[0, 5:6, :] = jnp.sum(grad_y * mod[5:6, :], axis=0, keepdims=True)
    low = grad_attn.astype(BF)
    for shift, (out, part) in enumerate(((d0, a0), (d1, a1), (d2, a2), (d3, a3))):
        out[0] = pack_rows(nt(low, w_ref[lax.rem(rank + 4 - shift, 4)]).astype(BF))
        update = tn(unpack_rows(part[0]), low)
        half = update.shape[0] // 2

        @pl.when(micro == 0)
        def _(shift=shift, update=update):
            wout_ref[shift] = update

        @pl.when(micro > 0)
        def _(shift=shift, update=update):
            wout_ref[shift] = wout_ref[shift] + update

    @pl.when(micro == pl.num_programs(0) - 1)
    def _():
        core = info_ref[3]
        for shift in range(4):
            here = pl.ds(pl.multiple_of(core * half, half), half)
            there = pl.ds(pl.multiple_of((1 - core) * half, half), half)
            wkeep[shift] = wout_ref[shift, here, :].astype(BF)
            wsend[shift] = wout_ref[shift, there, :].astype(BF)


def between(info, feed_own, feed_other, mid, attn, out_grad, mod_blocks, down_bias, out_full, parts, blocks, after=()):
    micro, share, width = mid.shape
    local = parts[0].shape[2] // 4
    half = pl.BlockSpec((share, width), lambda m, s: (m, 0))
    row = pl.BlockSpec((1, share, width), lambda m, s: (m, 0, 0))
    part = pl.BlockSpec((1, *parts[0].shape[1:]), lambda m, s: (m, 0, 0))
    mlp_own, gh_own = feed_own
    mlp_other, gh_other = feed_other
    dshape = shape(parts[0].shape, BF)
    return pl.pallas_call(
        skipping(between_kernel, 15, len(after)),
        grid_spec=pltpu.PrefetchScalarGridSpec(
            num_scalar_prefetch=1,
            grid=(micro,),
            in_specs=[half] * 4
            + [
                row,
                row,
                pl.BlockSpec((1, share, width), lambda m, s: (m, s[0], 0)),
                pl.BlockSpec((1, 6, width), lambda m, s: (m * blocks + s[0], 0, 0)),
                pl.BlockSpec((1, width), lambda m, s: (0, 0)),
                pl.BlockSpec(out_full.shape, lambda m, s: (0, 0, 0)),
            ]
            + [part] * 4
            + [ANY] * len(after),
            out_specs=[row, row, part, part, part, part]
            + [
                pl.BlockSpec((blocks, local // 2, width), lambda m, s: (0, 0, 0)),
                pl.BlockSpec((blocks, local // 2, width), lambda m, s: (0, 0, 0)),
                pl.BlockSpec((1, 8, width), lambda m, s: (m, 0, 0)),
            ],
            scratch_shapes=[pltpu.VMEM((blocks, local, width), F32)],
        ),
        out_shape=[
            shape((micro, share, width), BF),
            shape((micro, share, width), F32),
            dshape,
            dshape,
            dshape,
            dshape,
            shape((blocks, local // 2, width), BF),
            shape((blocks, local // 2, width), BF),
            shape((micro, 8, width), F32),
        ],
        compiler_params=params(),
        cost_estimate=cost(18),
        name="between",
    )(info, gh_own, gh_other, mlp_own, mlp_other, mid, attn, out_grad, mod_blocks, down_bias, out_full, *parts, *after)


def attend_back_kernel(
    micro, last, count, info_ref, q_ref, k_ref, v_ref, lse_ref, g0, g1, g2, g3, w_ref, hid_ref, tok_ref, *refs
):
    if last:
        old_ref, refs = refs[0], refs[1:]
    refs = refs[count:]
    part_ref, refs = refs[0], refs[1:]
    if last:
        sums_ref, bias_ref, wkeep, wsend = refs[:4]
        refs = refs[4:]
    else:
        sums_ref, bias_ref, wout = refs[:3]
        refs = refs[3:]
    dos, dqs, dks, dvs, dq_ref, dk_ref, dv_ref, wtmp, w_here, hid_here, tok_here, sems, *old_here = refs
    copies = [
        pltpu.make_async_copy(source, here, sems.at[i])
        for i, (source, here) in enumerate(
            [(w_ref, w_here), (tok_ref.at[micro], tok_here), (hid_ref.at[micro], hid_here)]
            + ([(old_ref, old_here[0])] if last else [])
        )
    ]
    for copy in copies:
        copy.start()
    _, heads, rows, size = q_ref.shape
    share = rows // 4
    local = heads * size
    rank = info_ref[0]
    whole = info_ref[1]
    scale = size ** (-0.5)
    factor = scale * LOG2E
    for shift, grad in enumerate((g0, g1, g2, g3)):
        grad = unpack_rows(grad[0])
        for h in range(heads):
            dos[h, shift] = grad[:, h * size : (h + 1) * size]

    def block_of(shift):
        return pl.multiple_of(lax.rem(rank + shift, 4) * share, share)

    def tile(h, shift, keys, values, keys_t):
        query = q_ref[0, h, pl.ds(block_of(shift), share), :]
        grad = dos[h, shift]
        lse = lse_ref[0, pl.ds(h, 1), pl.ds(block_of(shift), share)]
        probs = jnp.exp2(nt(keys, query) * factor - lse)
        dprobs = nt(values, grad)
        inner = jnp.sum(probs * dprobs, axis=0, keepdims=True)
        dscores = (probs * (dprobs - inner)).astype(BF)
        dqs[h, pl.ds(block_of(shift), share), :] = (nn(keys_t, dscores) * scale).T.astype(BF)
        return nn(dscores, query), nn(probs.astype(BF), grad)

    @pl.when(whole == 1)
    def _():
        def head(h, carry):
            keys = k_ref[0, h]
            values = v_ref[0, h]
            keys_t = keys.astype(F32).T.astype(BF)
            dkey, dvalue = tile(h, 0, keys, values, keys_t)
            for shift in range(1, 4):
                more_key, more_value = tile(h, shift, keys, values, keys_t)
                dkey = dkey + more_key
                dvalue = dvalue + more_value
            dks[h] = (dkey * scale).astype(BF)
            dvs[h] = dvalue.astype(BF)
            return carry

        lax.fori_loop(0, heads, head, 0)

    @pl.when(whole == 0)
    def _():
        def head(h, carry):
            for shift in range(4):
                span = pl.ds(block_of(shift), share)
                keys = k_ref[0, h, span, :]
                values = v_ref[0, h, span, :]
                dkey, dvalue = tile(h, shift, keys, values, keys.astype(F32).T.astype(BF))
                dks[h, span, :] = (dkey * scale).astype(BF)
                dvs[h, span, :] = dvalue.astype(BF)
            return carry

        lax.fori_loop(0, heads, head, 0)

    for src, dst in ((dqs, dq_ref), (dks, dk_ref), (dvs, dv_ref)):
        for h in range(heads):
            dst[:, h * size : (h + 1) * size] = src[h]

    copies[0].wait()
    copies[1].wait()

    def out_rows(i, carry):
        span = pl.ds(pl.multiple_of(i * share, share), share)
        grad = nn(dq_ref[span, :], w_here[0]) + nn(dk_ref[span, :], w_here[1]) + nn(dv_ref[span, :], w_here[2])
        part_ref[span, :] = grad.astype(BF)
        normed, _ = normalize(tok_here[span, :].astype(F32))
        sums_ref[pl.ds(2 * i, 1), :] = jnp.sum(grad, axis=0, keepdims=True)
        sums_ref[pl.ds(2 * i + 1, 1), :] = jnp.sum(grad * normed, axis=0, keepdims=True)
        return carry

    lax.fori_loop(0, rows // share, out_rows, 0)
    bias_ref[...] = jnp.zeros_like(bias_ref)
    bias_ref[0:1, :] = jnp.sum(dq_ref[...].astype(F32), axis=0, keepdims=True)
    bias_ref[1:2, :] = jnp.sum(dv_ref[...].astype(F32), axis=0, keepdims=True)
    for copy in copies[2:]:
        copy.wait()
    for which, ref in enumerate((dq_ref, dk_ref, dv_ref)):
        span = slice(which * local, (which + 1) * local)
        update = tn(ref[...], hid_here[...])
        if last:
            wtmp[span] = (old_here[0][span] + update).astype(BF)
        else:
            wout[span] = update
    if last:
        core = info_ref[2]
        half = 3 * local // 2
        for ref, place in ((wkeep, core), (wsend, 1 - core)):
            ref[:half] = wtmp[pl.ds(pl.multiple_of(place * half, half), half), :]
            ref[half:] = jnp.zeros((ref.shape[0] - half, ref.shape[1]), BF)


def attend_back(micro, info, query, key, value, lse, grads, qkv_weight, hidden, tokens, old=None, after=()):
    _, heads, rows, size = query.shape
    share = rows // 4
    local = heads * size
    width = qkv_weight.shape[2]
    last = old is not None
    full = pl.BlockSpec((1, heads, rows, size), lambda i, s: (micro, 0, 0, 0))
    def flat(*dims):
        return pl.BlockSpec(dims, lambda i, s: (0,) * len(dims))

    outs = [((rows, width), BF), ((8, width), F32), ((8, local), F32)]
    if last:
        outs += [((-(-3 * local // 128) * 64, width), BF)] * 2
    else:
        outs += [((3 * local, width), F32)]
    return pl.pallas_call(
        functools.partial(attend_back_kernel, micro, last, len(after)),
        grid_spec=pltpu.PrefetchScalarGridSpec(
            num_scalar_prefetch=1,
            grid=(1,),
            in_specs=[full] * 3
            + [pl.BlockSpec((1, heads, rows), lambda i, s: (micro, 0, 0))]
            + [pl.BlockSpec((1, *grads[0].shape[1:]), lambda i, s: (micro, 0, 0))] * 4
            + [ANY] * (3 + int(last) + len(after)),
            out_specs=[flat(*dims) for dims, _ in outs],
            scratch_shapes=[
                pltpu.VMEM((heads, 4, share, size), BF),
                pltpu.VMEM((heads, rows, size), BF),
                pltpu.VMEM((heads, rows, size), BF),
                pltpu.VMEM((heads, rows, size), BF),
                pltpu.VMEM((rows, local), BF),
                pltpu.VMEM((rows, local), BF),
                pltpu.VMEM((rows, local), BF),
                pltpu.VMEM((3 * local, width), BF),
                pltpu.VMEM(qkv_weight.shape, BF),
                pltpu.VMEM((rows, width), BF),
                pltpu.VMEM((rows, width), BF),
                pltpu.SemaphoreType.DMA((4,)),
            ]
            + ([pltpu.VMEM((3 * local, width), F32)] if last else []),
        ),
        out_shape=[shape(dims, dtype) for dims, dtype in outs],
        compiler_params=params(),
        cost_estimate=cost(30),
        name="attend_back",
    )(info, query, key, value, lse, *grads, qkv_weight, hidden, tokens, *([old] if last else []), *after)


def finish_kernel(info_ref, grad_ref, tok_ref, mod_ref, gmid_ref, out_ref):
    normed, inverse = normalize(tok_ref[0].astype(F32))
    grad = grad_ref[...].astype(F32)
    out_ref[0] = gmid_ref[0] + norm_backward(grad * (1.0 + mod_ref[0, 1:2, :]), normed, inverse)


def finish(info, micro, grad, tokens, mod_blocks, gmid, blocks, old=None, after=()):
    _, share, width = gmid.shape
    more = ([] if old is None else [old]) + list(after)
    return pl.pallas_call(
        skipping(finish_kernel, 5, len(more)),
        grid_spec=pltpu.PrefetchScalarGridSpec(
            num_scalar_prefetch=1,
            grid=(1,),
            in_specs=[
                pl.BlockSpec((share, width), lambda i, s: (0, 0)),
                pl.BlockSpec((1, share, width), lambda i, s: (micro, s[0], 0)),
                pl.BlockSpec((1, 6, width), lambda i, s: (micro * blocks + s[0], 0, 0)),
                pl.BlockSpec((1, share, width), lambda i, s: (micro, 0, 0)),
            ]
            + [ANY] * len(more),
            out_specs=[pl.BlockSpec((1, share, width), lambda i, s: (micro, 0, 0))],
        ),
        out_shape=[shape(gmid.shape, F32)],
        input_output_aliases={} if old is None else {5: 0},
        compiler_params=params(),
        cost_estimate=cost(3),
        name="finish",
    )(info, grad, tokens, mod_blocks, gmid, *more)[0]


def in_order(row, quarter, piece):
    parts = [row[:, i * piece : (i + 1) * piece] for i in range(4)]
    out = []
    for j in range(4):
        source = jnp.bitwise_xor(quarter, j)
        value = parts[3]
        for i in range(3):
            value = jnp.where(source == i, parts[i], value)
        out.append(value)
    return jnp.concatenate(out, axis=1)


def ada_kernel(info, cond_ref, w_ref, bias_ref, units_ref, small_ref, act_ref):
    value = cond_ref[...].astype(F32)
    act = (value / (1.0 + jnp.exp(-value))).astype(BF)
    act_ref[...] = act
    count = act.shape[0]
    small_ref[...] = jnp.zeros_like(small_ref)
    small_ref[:count] = nt(act, w_ref[...]) + bias_ref[...]
    half = units_ref.shape[1] // 2
    mine = jnp.where(info[1] == 0, units_ref[:, :half], units_ref[:, half:])
    small_ref[count : count + 1, :half] = in_order(mine, info[2], half // 4)


def modulate_kernel(info, s0, s1, s2, s3, mod_ref, far_ref, near_ref, lanes, full):
    rank = info[0]
    for shift, ref in enumerate((s0, s1, s2, s3)):
        lanes[lax.rem(rank + 4 - shift, 4)] = ref[...]
    full[...] = jnp.concatenate([lanes[i] for i in range(4)], axis=1)
    width = mod_ref.shape[2]
    for i in range(mod_ref.shape[0]):
        segment = info[3 + i]
        slot = (i // 4) * 4 + jnp.minimum(segment, 3)
        row = full[pl.ds(slot, 1), :] * (segment < 4).astype(F32)
        for j in range(6):
            mod_ref[i, j : j + 1, :] = row[:, j * width : (j + 1) * width]
    half = far_ref.shape[2]
    for ref, order in ((far_ref, (s2, s1)), (near_ref, (s3, s0))):
        for i, source in enumerate(order):
            ref[i] = source[8:9, :half]


def pile_kernel(info, l0, l1, sums, far, near, out):
    rank = info[0]
    out[...] = jnp.zeros_like(out)
    for m, late in enumerate((l0, l1)):
        for slot in range(4):
            row = 6 * (4 * m + slot)
            for i in range(2):
                total = jnp.zeros((1, out.shape[1]), F32)
                for block in range(4):
                    inside = (info[3 + m * 4 + block] == slot).astype(F32)
                    total = total + inside * late[2 * block + i : 2 * block + i + 1, :]
                out[row + i : row + i + 1, :] = total
            inside = (info[3 + m * 4 + rank] == slot).astype(F32)
            out[row + 2 : row + 6, :] = inside * sums[m, 0:4, :]
    out[48:50, :] = sums[0, 4:6, :] + sums[1, 4:6, :]
    half = far.shape[2]
    for k, (ref, i) in enumerate(((near, 1), (far, 1), (far, 0), (near, 0))):
        out[pl.ds(50 + lax.rem(rank + 4 - k, 4), 1), :half] = ref[i]


def sum_kernel(a, b, out):
    out[...] = a[...] + b[...]


def slots_kernel(info, mine, got, b0, b1, act_ref, pay_ref, low_ref, full):
    rank = info[0]
    width = mine.shape[1]
    total = mine[...] + got[...]
    for row in range(8):
        for i in range(6):
            full[row : row + 1, i * width : (i + 1) * width] = total[6 * row + i : 6 * row + i + 1, :]
    columns = pay_ref.shape[1]
    half = columns - width
    pay_ref[...] = jnp.zeros_like(pay_ref)
    for i in range(4):

        @pl.when(rank == i)
        def _(i=i):
            own = full[:, i * columns : (i + 1) * columns]
            pay_ref[0:8, :] = own
            low_ref[...] = own.astype(BF)
            pay_ref[8:9, width:] = in_order(total[50 + i : 51 + i, :half], info[2], half // 4)

    pay_ref[8:9, :width] = total[48:49]
    pay_ref[9:10, :width] = total[49:50]
    both = b0[0:2, :] + b1[0:2, :]
    pay_ref[9:10, width:] = jnp.concatenate([both[0:1], both[1:2]], axis=1)
    pay_ref[10:18, :width] = act_ref[...].astype(F32)


def tail_kernel(info, pay_ref, ada_ref, ada_b, out_b, down_b, up_b, qv_b):
    width = out_b.shape[0]
    columns = pay_ref.shape[2]
    half = columns - width
    count = pay_ref.shape[0]
    mods = jnp.concatenate([pay_ref[i, 0:8, :] for i in range(count)], axis=0)
    acts = jnp.concatenate([pay_ref[i, 10:18, :width] for i in range(count)], axis=0)
    ada_ref[...] = tn(mods.astype(BF), acts.astype(BF))
    ada_b[...] = jnp.sum(mods, axis=0)
    sums = [pay_ref[0, 8:10, :], pay_ref[1, 8:10, :]]
    for i in range(2, count):
        sums[i % 2] = sums[i % 2] + pay_ref[i, 8:10, :]
    total = sums[0] + sums[1]
    out_b[...] = total[0, :width]
    down_b[...] = total[1, :width]
    low = jnp.where(info[1] == 0, sums[0][0:1, width:], sums[1][0:1, width:])
    high = jnp.where(info[1] == 0, sums[1][0:1, width:], sums[0][0:1, width:])
    up_b[...] = jnp.concatenate([low, high], axis=1)[0]
    qv_b[0:1, :] = total[1:2, width : width + half // 2]
    qv_b[1:2, :] = total[1:2, width + half // 2 :]


def pack_kernel(info, up_ref, down_ref, up_out, down_out, mine_ref, turned):
    turned[...] = up_ref[...].T
    half = up_out.shape[0]
    piece = half // 4
    for j in range(4):
        at = info[1] * half + jnp.bitwise_xor(info[2], j) * piece
        rows = pl.ds(pl.multiple_of(at, piece), piece)
        up = turned[rows, :]
        down = down_ref[rows, :]
        up_out[j * piece : (j + 1) * piece] = up
        down_out[j * piece : (j + 1) * piece] = down
        if j == 0:
            mine_ref[:piece] = up
            mine_ref[piece:] = down


def tick_kernel(out):
    out[...] = jnp.zeros_like(out)


def copy_kernel(*refs):
    count = len(refs) // 2
    for source, out in zip(refs[:count], refs[count:]):
        out[...] = source[...]


def stack_kernel(first, second, out):
    out[0] = first[...]
    out[1] = second[...]


def pack_rows(array):
    rows = array.shape[0] // 4
    return jnp.concatenate([array[i * rows : (i + 1) * rows] for i in range(4)], axis=1)


def unpack_rows(array):
    columns = array.shape[1] // 4
    return jnp.concatenate([array[:, i * columns : (i + 1) * columns] for i in range(4)], axis=0)


def corner_kernel(x_ref, y_ref, up_out, down_out):
    piece = up_out.shape[1]
    up_out[...] = x_ref[:, :piece]
    down_out[...] = y_ref[:, piece:]


def plus(a, b):
    return a.astype(F32) + b.astype(F32)


def halve_kernel(uk, ur, dk, dr, u_keep, u_send, d_keep, d_send):
    for keep, got, mine, give in ((uk, ur, u_keep, u_send), (dk, dr, d_keep, d_send)):
        for i in range(keep.shape[0]):
            mine[i] = plus(keep[i, 0], got[i, 0]).astype(BF)
            give[i] = plus(keep[i, 1], got[i, 1]).astype(BF)


def quarter_kernel(uk, ur, dk, dr, first, second):
    piece = uk.shape[1]
    for i, out in enumerate((first, second)):
        out[:piece] = plus(uk[i], ur[i]).astype(BF)
        out[piece:] = plus(dk[i], dr[i]).astype(BF)


def mix_kernel(o_rows, info, uk, us, dk, ds, ok, og, u_keep, u_send, d_keep, d_send, room, sums):
    room[...] = jnp.zeros_like(room)
    for k in range(4):
        sums[...] = plus(ok[k], og[k])
        for i in range(4):
            room[k, jnp.bitwise_xor(info[2], i), :o_rows] = sums[i * o_rows : (i + 1) * o_rows].astype(BF)
    piece = uk.shape[2]
    wide = room.shape[2]
    for keep, send, mine, give, planes, near, far in (
        (uk, us, u_keep, u_send, (0, 1), (0, 1), (2, 3)),
        (dk, ds, d_keep, d_send, (2, 3), (0, 2), (1, 3)),
    ):
        for source, out, order in ((keep, mine, near), (send, give, far)):
            at = 0
            for place in range(2):
                for i in range(2):
                    out[at : at + piece] = source[i, place]
                    at += piece
                for k in planes:
                    out[at : at + wide] = room[k, order[place]]
                    at += wide


def halve_flat_kernel(uk, ur, dk, dr, u_keep, u_send, d_keep, d_send):
    for keep, got, mine, give in ((uk, ur, u_keep, u_send), (dk, dr, d_keep, d_send)):
        half = mine.shape[0]
        mine[...] = plus(keep[:half], got[:half]).astype(BF)
        give[...] = plus(keep[half:], got[half:]).astype(BF)


def last_kernel(uk, ur, dk, dr, third, o1, o2, own):
    wide = o1.shape[0]
    piece = (uk.shape[0] - 2 * wide) // 2
    up = plus(uk[...], ur[...]).astype(BF)
    down = plus(dk[...], dr[...]).astype(BF)
    for out, i in ((third, 0), (own, 1)):
        out[:piece] = up[i * piece : (i + 1) * piece]
        out[piece : 2 * piece] = down[i * piece : (i + 1) * piece]
    own[2 * piece :] = up[2 * piece : 2 * piece + wide]
    o1[...] = up[2 * piece + wide :]
    o2[...] = down[2 * piece : 2 * piece + wide]
    third[2 * piece :] = down[2 * piece + wide :]


def split_rows(total, bit, keep, send):
    half = total.shape[0] // 2
    keep[...] = total[pl.ds(pl.multiple_of(bit * half, half), half), :]
    send[...] = total[pl.ds(pl.multiple_of((1 - bit) * half, half), half), :]


def first_kernel(info, mine, got, keep, send, total):
    total[...] = plus(mine[...], got[...]).astype(BF)
    split_rows(total, jnp.bitwise_and(info[2], 1), keep, send)


def second_kernel(info, mine, got, keep, send, total):
    total[...] = plus(mine[...], got[...]).astype(BF)
    split_rows(total, info[2] >> 1, keep, send)


def merge_kernel(keep, got, own, first, second, third, o1, o2, out):
    at = keep.shape[0]
    out[:at] = plus(keep[...], got[...]).astype(BF)
    rows = first.shape[0]
    out[at : at + rows] = (plus(own[:rows], first[...]) + plus(second[...], third[:rows])).astype(BF)
    out[at + rows :] = (plus(own[rows:], o1[...]) + plus(o2[...], third[rows:])).astype(BF)


def order_kernel(o_rows, w_rows, info, b0, b1, b2, b3, halves, others, room):
    piece = halves.shape[1] // 4
    wide = room.shape[1]
    for j, ref in enumerate((b0, b1, b2, b3)):
        quarter = jnp.bitwise_xor(info[2], j)
        place = 2 * jnp.bitwise_and(quarter, 1) + (quarter >> 1)
        others[pl.ds(pl.multiple_of(place * w_rows, w_rows), w_rows), :] = ref[:w_rows]
        rows = pl.ds(pl.multiple_of(quarter * piece, piece), piece)
        halves[0, rows, :] = ref[w_rows : w_rows + piece]
        halves[1, rows, :] = ref[w_rows + piece : w_rows + 2 * piece]
        room[quarter] = ref[w_rows + 2 * piece :]
    outs = jnp.concatenate([room[i, :o_rows] for i in range(4)], axis=0)
    others[4 * w_rows :] = outs


def spread_kernel(info, own, other, own_o, other_o, up_out, down_out, qkv_out, out_out, turned, total):
    half = own.shape[1]
    here = pl.ds(pl.multiple_of(info[1] * half, half), half)
    there = pl.ds(pl.multiple_of((1 - info[1]) * half, half), half)
    turned[here, :] = own[0]
    turned[there, :] = other[0]
    down_out[here, :] = own[1].astype(F32)
    down_out[there, :] = other[1].astype(F32)
    rows = out_out.shape[0] // 2
    count = total.shape[0] // 2
    for ref, core in ((own_o, info[1]), (other_o, 1 - info[1])):
        out_out[pl.ds(pl.multiple_of(core * rows, rows), rows), :] = ref[ref.shape[0] - rows :].astype(F32)
        total[pl.ds(pl.multiple_of(core * count, count), count), :] = ref[:count]
    local = qkv_out.shape[1]
    for i in range(3):
        qkv_out[i] = total[i * local : (i + 1) * local].astype(F32)
    up_out[...] = turned[...].astype(F32).T


def spread(info, operands, outs, after):
    up, down, qkv, out = outs
    width = up[0]
    tile = 384 if width % 384 == 0 else width
    return pl.pallas_call(
        skipping(spread_kernel, 5, len(after)),
        grid_spec=pltpu.PrefetchScalarGridSpec(
            num_scalar_prefetch=1,
            grid=(width // tile,),
            in_specs=[pl.BlockSpec((*a.shape[:2], tile), lambda i, s: (0, 0, i)) for a in operands[:2]]
            + [pl.BlockSpec((a.shape[0], tile), lambda i, s: (0, i)) for a in operands[2:]]
            + [ANY] * len(after),
            out_specs=[
                pl.BlockSpec((tile, up[1]), lambda i, s: (i, 0)),
                pl.BlockSpec((down[0], tile), lambda i, s: (0, i)),
                pl.BlockSpec((*qkv[:2], tile), lambda i, s: (0, 0, i)),
                pl.BlockSpec((out[0], tile), lambda i, s: (0, i)),
            ],
            scratch_shapes=[pltpu.VMEM((up[1], tile), BF), pltpu.VMEM((3 * qkv[1], tile), BF)],
        ),
        out_shape=[shape(dims, F32) for dims in outs],
        compiler_params=params(),
        cost_estimate=cost(6),
        name="spread",
    )(info, *operands, *after)


def turn(array, shift):
    count = lax.axis_size("tensor")
    return lax.ppermute(array, "tensor", [(i, (i + shift) % count) for i in range(count)])


def flip(array, axis):
    return lax.ppermute(array, axis, [(0, 1), (1, 0)])


def diagonal(array):
    return lax.ppermute(array, ("y", "x"), [(0, 3), (1, 2), (2, 1), (3, 0)])


def over_rest(array):
    count = lax.axis_size("rest")
    bit = 1
    while bit < count:
        other = lax.ppermute(array, "rest", [(i, i ^ bit) for i in range(count)])
        array = plus(array, other).astype(BF)
        bit *= 2
    return array


DP = ("rest", "y", "x", "core")


def local(
    tokens, conditioning, lengths, out_grad, ada_weight, ada_bias, qkv_weight, qv_bias,
    out_weight, out_bias, up_weight, up_bias, down_weight, down_bias,
):
    groups = lax.axis_size("tensor")
    rank = lax.axis_index("tensor")
    core = lax.axis_index("core")
    quarter = 2 * lax.axis_index("y") + lax.axis_index("x")
    micro, rows, width = tokens.shape
    share = rows // groups
    slots = lengths.shape[1]
    part = up_weight.shape[1]
    half = part // 2
    piece = half // 4
    columns = ada_weight.shape[1]
    local_width = qkv_weight.shape[2]
    ada_turned = ada_weight.T
    qkv_turned = qkv_weight.transpose(0, 2, 1)
    here = jnp.stack([rank, core, quarter]).astype(jnp.int32)

    boundary = jnp.cumsum(lengths, axis=1)
    starts = jnp.arange(groups, dtype=jnp.int32) * share
    segment = jnp.sum((boundary[:, None, :] <= starts[None, :, None]).astype(jnp.int32), axis=2)
    whole = (segment[:, groups - 1] == 0).astype(jnp.int32)
    own_valid = (lax.dynamic_index_in_dim(segment, rank, 1, False) < slots).astype(jnp.int32)
    info = jnp.concatenate([here, segment.reshape(-1)])

    small, cond_act = simple(
        ada_kernel,
        [shape((16, columns), F32), shape((micro * slots, width), BF)],
        [conditioning.reshape(micro * slots, width), ada_turned, ada_bias[None], up_bias[None]],
        info,
        name="ada", micros=0.01,
    )
    smalls = [small] + [turn(small, k) for k in (1, 2, 3)]

    up_near, down_near, mine = simple(
        pack_kernel,
        [shape((half, width), BF), shape((half, width), BF), shape((2 * piece, width), BF)],
        [up_weight, down_weight],
        info,
        after=(cond_act,),
        scratch=[pltpu.VMEM((part, width), BF)],
        name="pack", micros=0.01,
    )
    got = {k: turn(mine, k) for k in (2, 1, 3)}
    out_rows = lax.dynamic_slice_in_dim(out_weight, quarter * (local_width // 4), local_width // 4, 0)
    out_full = lax.all_gather(out_rows, ("tensor", "y", "x"), axis=0, tiled=True)
    out_full = out_full.reshape(groups, local_width, width)

    mod_blocks, bias_a, bias_b = simple(
        modulate_kernel,
        [
            shape((micro * groups, 6, width), F32),
            shape((2, 1, half), F32),
            shape((2, 1, half), F32),
        ],
        smalls,
        info,
        after=(mine,),
        scratch=[pltpu.VMEM((4, 16, columns), F32), pltpu.VMEM((16, 6 * width), F32)],
        name="modulate", micros=0.01,
    )
    hidden_one, query, key, value = project(tokens, mod_blocks, qkv_turned, qv_bias, groups)

    own_gate = lax.dynamic_index_in_dim(
        mod_blocks.reshape(micro, groups, 6, width), rank, 1, False
    )[:, 5:6]
    own_grad = lax.dynamic_slice_in_dim(out_grad, rank * share, share, 1).astype(F32)
    grad_mlp = own_grad * (own_valid.astype(F32)[:, None, None] * own_gate)
    own_g = grad_mlp.astype(BF).reshape(micro * share, width)
    other_g = flip(own_g, "core")

    (two,) = simple(
        stack_kernel,
        [shape((2, 2 * piece, width), BF)],
        [got[2], got[1]],
        after=(query,),
        name="two",
        micros=0.01,
    )
    *att, lse = attend(
        jnp.concatenate([rank[None], whole]), query, key, value, after=(two, other_g)
    )
    parts = [att[0], turn(att[1], 1), turn(att[2], 2), turn(att[3], 3)]
    two_parts = (two, flip(two, "x"), flip(two, "y"))

    def release(arrays, after, micros=3):
        return simple(
            copy_kernel, [shape(a.shape, a.dtype) for a in arrays], arrays, after=after, name="release", micros=micros
        )

    corner = simple(
        corner_kernel,
        [shape((2, piece, width), BF)] * 2,
        two_parts[1:],
        after=(lse,),
        name="corner",
    )
    two_parts = (*two_parts, flip(corner[0], "y"), flip(corner[1], "x"))
    attn, mid, hidden_two = middle(
        here, parts, out_full, out_bias[None], tokens, mod_blocks, groups, after=(corner[0],)
    )
    own_x = hidden_two.reshape(micro * share, width)
    other_x = flip(own_x, "core")
    (third,) = release([got[3]], (mid,) + two_parts[3:], 100)
    third_parts = (third, flip(third, "x"), flip(third, "y"), diagonal(third))
    *carry, uk_a, us_a, dk_a, ds_a, bsum_a = feed(
        own_x, other_x, own_g, other_g, [two_parts], bias_a, None
    )
    ur_a = flip(us_a, "y")
    dr_a = flip(ds_a, "x")
    mlp_own, mlp_send, gh_own, gh_send, uk_b, us_b, dk_b, ds_b, bsum_b = feed(
        own_x, other_x, own_g, other_g, [third_parts, (up_near, down_near)], bias_b, carry
    )
    gh_got = flip(gh_send, "core")
    mlp_got = flip(mlp_send, "core")
    piece_shapes = [shape((2, piece, width), BF)] * 4
    uk_a, us_a, dk_a, ds_a = simple(
        halve_kernel, piece_shapes, [uk_a, ur_a, dk_a, dr_a], after=(gh_own,), name="halve", micros=100
    )
    ur_a = flip(us_a, "x")
    dr_a = flip(ds_a, "y")
    layer_out, grad_mid, d0, d1, d2, d3, o_keep, o_send, sums = between(
        jnp.concatenate([here[:1], own_valid, here[1:2]]),
        (mlp_own, gh_own),
        (mlp_got, gh_got),
        mid, attn, out_grad, mod_blocks, down_bias[None], out_full, parts, groups,
        after=(uk_a,),
    )
    grads = [d0] + [turn(d, -k) for k, d in ((1, d1), (2, d2), (3, d3))]
    o_got = flip(o_send, "core")
    o_rows = o_keep.shape[1] // 4
    o_room = -(-o_rows // 16) * 16

    (tick,) = simple(tick_kernel, [shape((8, 128), F32)], [], after=(d0, ur_a, dr_a), name="tick", micros=100)

    side = 4 * piece + 4 * o_room
    u_keep, u_send, d_keep, d_send = simple(
        functools.partial(mix_kernel, o_rows),
        [shape((side, width), BF)] * 4,
        [uk_b, us_b, dk_b, ds_b, o_keep, o_got],
        info,
        after=(tick,),
        scratch=[pltpu.VMEM((4, 4, o_room, width), BF), pltpu.VMEM((4 * o_rows, width), F32)],
        name="mix",
    )
    u_got = flip(u_send, "y")
    d_got = flip(d_send, "x")
    block_shape = shape((2 * piece, width), BF)
    t2, t1 = simple(
        quarter_kernel,
        [block_shape] * 2,
        [uk_a, ur_a, dk_a, dr_a],
        after=(u_send, *grads[1:]),
        name="quarter",
    )
    token = (t1,)
    t2 = turn(t2, -2)
    t1 = turn(t1, -1)

    back_info = [jnp.stack([rank, whole[m], core]) for m in range(micro)]
    part_0, lsum_0, bias_0, old = attend_back(
        0, back_info[0], query, key, value, lse, grads, qkv_turned, hidden_one, tokens, after=token
    )
    share_0 = lax.psum_scatter(part_0, "tensor", scatter_dimension=0, tiled=True)
    half_shape = shape((side // 2, width), BF)
    u_keep, u_send, d_keep, d_send = simple(
        halve_flat_kernel,
        [half_shape] * 4,
        [u_keep, u_got, d_keep, d_got],
        after=(lsum_0,),
        name="halve",
    )
    token = (u_keep,)
    u_got = flip(u_send, "x")
    d_got = flip(d_send, "y")
    part_1, lsum_1, bias_1, w_keep, w_send = attend_back(
        1, back_info[1], query, key, value, lse, grads, qkv_turned, hidden_one, tokens, old, after=token
    )
    w_got = flip(w_send, "core")
    def short(kernel, outs, operands, name, after=(), scratch=(), micros=3):
        return simple(
            kernel, outs, operands, info, after=after, scratch=scratch, name=name, micros=micros
        )

    def plain(kernel, outs, operands, name, after=(), micros=3):
        return simple(kernel, outs, operands, after=after, name=name, micros=micros)

    def rows_shape(count):
        return shape((count, width), BF)

    (tick,) = simple(
        tick_kernel, [shape((8, 128), F32)], [], after=(lsum_1, t1, t2), name="tick", micros=100
    )

    o_shape = rows_shape(o_room)
    block_shape = rows_shape(2 * piece + o_room)
    t3, o1, o2, t0 = plain(
        last_kernel,
        [block_shape, o_shape, o_shape, block_shape],
        [u_keep, u_got, d_keep, d_got],
        "last",
        (tick,),
        micros=60,
    )
    token = (t3,)
    t3 = turn(t3, -3)
    o1 = turn(o1, -1)
    o2 = turn(o2, -2)
    rows_all = w_keep.shape[0]
    keep, send = short(
        first_kernel,
        [rows_shape(rows_all // 2)] * 2,
        [w_keep, w_got],
        "first",
        token,
        [pltpu.VMEM((rows_all, width), BF)],
    )
    (pile,) = short(
        pile_kernel, [shape((56, width), F32)], [lsum_0, lsum_1, sums, bsum_a, bsum_b], "pile", (keep,)
    )
    pile_got = turn(pile, 2)
    tokens_grad = finish(here, 0, share_0, tokens, mod_blocks, grad_mid, groups, after=(*token, pile))
    keep, send = short(
        second_kernel,
        [rows_shape(rows_all // 4)] * 2,
        [keep, flip(send, "x")],
        "second",
        (tokens_grad,),
        [pltpu.VMEM((rows_all // 2, width), BF)],
    )
    send_got = flip(send, "y")
    (tick,) = plain(tick_kernel, [shape((8, 128), F32)], [], "tick", (keep, o1, o2), micros=60)
    (merged,) = plain(
        merge_kernel,
        [rows_shape(rows_all // 4 + 2 * piece + o_room)],
        [keep, send_got, t0, t1, t2, t3, o1, o2],
        "merge",
        (tick,),
        micros=0.1,
    )
    (pile,) = plain(
        sum_kernel, [shape(pile.shape, F32)], [pile, pile_got], "sum", (merged,), micros=30
    )
    pile_far = turn(pile, 1)
    (part_1,) = release([part_1], (merged,))
    share_1 = lax.psum_scatter(part_1, "tensor", scatter_dimension=0, tiled=True)
    merged = over_rest(merged)
    all_four = [merged, flip(merged, "x"), flip(merged, "y"), diagonal(merged)]
    pay, mod_low = short(
        slots_kernel,
        [shape((24, columns), F32), shape((micro * slots, columns), BF)],
        [pile, pile_far, bias_0, bias_1, cond_act],
        "slots",
        (merged,),
        [pltpu.VMEM((micro * slots, 6 * width), F32)],
        micros=0.1,
    )
    pay_got = flip(pay, "core")
    cond_part = jnp.dot(mod_low, ada_turned, preferred_element_type=F32)

    cond_grad = cond_part + turn(cond_part, 2)
    cond_grad = cond_grad + turn(cond_grad, 1)

    def pair_kernel(mine, got, out):
        count = mine.shape[0]
        out[:count] = mine[...]
        out[count:] = got[...]

    def pair(mine, got, after=()):
        outs = [shape((2 * mine.shape[0], *mine.shape[1:]), F32)]
        return plain(pair_kernel, outs, [mine, got], "pair", after, micros=0.1)[0]

    pays = pair(pay[None], pay_got[None])
    pays = pair(pays, flip(pays, "x"))
    pays_got = flip(pays, "y")
    halves, others = short(
        functools.partial(order_kernel, o_rows, rows_all // 4),
        [shape((2, half, width), BF), rows_shape(rows_all + 4 * o_rows)],
        all_four,
        "order",
        (pays, cond_grad),
        [pltpu.VMEM((4, o_room, width), BF)],
        micros=0.1,
    )
    halves_got = flip(halves, "core")
    others_got = flip(others, "core")
    tokens_grad = finish(
        here, 1, share_1, tokens, mod_blocks, grad_mid, groups, tokens_grad, after=(halves,)
    )
    up_weight_grad, down_weight_grad, qkv_weight_grad, out_weight_grad = spread(
        info,
        [halves, halves_got, others, others_got],
        [up_weight.shape, down_weight.shape, qkv_turned.shape, out_weight.shape],
        (tokens_grad,),
    )
    pays = pair(pays, pays_got, (up_weight_grad,))
    if lax.axis_size("rest") > 1:
        pays = lax.all_gather(pays, "rest", axis=0, tiled=True)
    ada_weight_grad, ada_b, out_b, down_b, up_b, qv_bias_grad = short(
        tail_kernel,
        [
            shape(ada_turned.shape, F32),
            shape((columns,), F32),
            shape((width,), F32),
            shape((width,), F32),
            shape((part,), F32),
            shape(qv_bias.shape, F32),
        ],
        [pays],
        "tail",
    )
    cond_float = conditioning.astype(F32)
    sigmoid = jax.nn.sigmoid(cond_float)
    conditioning_grad = cond_grad.reshape(micro, slots, width) * (
        sigmoid * (1.0 + cond_float * (1.0 - sigmoid))
    )
    return (
        layer_out,
        tokens_grad,
        conditioning_grad,
        ada_weight_grad.T,
        ada_b,
        qkv_weight_grad.transpose(0, 2, 1),
        qv_bias_grad,
        out_weight_grad,
        out_b,
        up_weight_grad,
        up_b,
        down_weight_grad,
        down_b,
    )


def solution(mesh):
    count, groups = mesh.devices.shape
    devices = mesh.devices.reshape(count // 8, 2, 2, 2, groups)
    fine = Mesh(devices, DP + ("tensor",))
    placed = (
        P(None, DP, None),
        P(None, DP, None),
        P(None, DP),
        P(None, DP, None),
        P(None, "tensor"),
        P("tensor"),
        P(None, None, "tensor"),
        P(None, "tensor"),
        P("tensor", None),
        P(),
        P(None, "tensor"),
        P("tensor"),
        P("tensor", None),
        P(),
    )
    return jax.shard_map(
        local,
        mesh=fine,
        in_specs=placed,
        out_specs=(
            P(None, DP + ("tensor",), None),
            P(None, DP + ("tensor",), None),
            P(None, DP, None),
            P(None, "tensor"),
            P("tensor"),
            P(None, None, "tensor"),
            P(None, "tensor"),
            P("tensor", None),
            P(),
            P(None, "tensor"),
            P("tensor"),
            P("tensor", None),
            P(),
        ),
        check_vma=False,
    )
```

```python
import functools
import math

import jax
import jax.numpy as jnp
from jax import lax
from jax.experimental import pallas as pl
from jax.experimental.pallas import tpu as pltpu
from jax.sharding import Mesh
from jax.sharding import PartitionSpec as P

HEAD_DIM = 72
EPSILON = 1e-06
LOG2E = math.log2(math.e)
GELU_C = 0.7978845608
GELU_A = 0.044715
VMEM = 60 * 1024 * 1024
BF = jnp.bfloat16
F32 = jnp.float32


def nn(a, b):
    return lax.dot_general(a, b, (((1,), (0,)), ((), ())), preferred_element_type=F32)


def nt(a, b):
    return lax.dot_general(a, b, (((1,), (1,)), ((), ())), preferred_element_type=F32)


def tn(a, b):
    return lax.dot_general(a, b, (((0,), (0,)), ((), ())), preferred_element_type=F32)


def params():
    return pltpu.CompilerParams(vmem_limit_bytes=VMEM)


def cost(micros):
    return pl.CostEstimate(
        flops=int(micros * 1.15e9), bytes_accessed=int(micros * 1e5), transcendentals=0
    )


ANY = pl.BlockSpec(memory_space=pl.ANY)


def shape(dims, dtype):
    return pltpu.HBM(tuple(dims), dtype)


def skipping(kernel, start, count):
    def body(*refs):
        kernel(*refs[:start], *refs[start + count :])

    return body


def simple(kernel, outs, operands, scalars=None, after=(), scratch=(), name="glue", micros=3):
    count = len(after)
    n_scalar = 0 if scalars is None else 1
    n_in = len(operands)

    body = skipping(kernel, n_scalar + n_in, count)

    def whole(array):
        zeros = (0,) * len(array.shape)
        return pl.BlockSpec(array.shape, lambda *_: zeros)

    return pl.pallas_call(
        body,
        grid_spec=pltpu.PrefetchScalarGridSpec(
            num_scalar_prefetch=n_scalar,
            grid=(1,),
            in_specs=[whole(a) for a in operands] + [ANY] * count,
            out_specs=[whole(o) for o in outs],
            scratch_shapes=list(scratch),
        ),
        out_shape=list(outs),
        compiler_params=params(),
        cost_estimate=cost(micros),
        name=name,
    )(*([] if scalars is None else [scalars]), *operands, *after)


def normalize(values):
    centred = values - jnp.mean(values, axis=-1, keepdims=True)
    inverse = lax.rsqrt(jnp.mean(centred * centred, axis=-1, keepdims=True) + EPSILON)
    return centred * inverse, inverse


def norm_backward(grad, normed, inverse):
    return inverse * (
        grad
        - jnp.mean(grad, axis=-1, keepdims=True)
        - normed * jnp.mean(grad * normed, axis=-1, keepdims=True)
    )


def project_kernel(tok_ref, mod_ref, w_ref, bias_ref, hid_ref, q_ref, k_ref, v_ref):
    heads = q_ref.shape[1]
    size = q_ref.shape[3]
    share = tok_ref.shape[1] // mod_ref.shape[0]
    for i in range(mod_ref.shape[0]):
        rows = slice(i * share, (i + 1) * share)
        normed, _ = normalize(tok_ref[0, rows].astype(F32))
        hid_ref[0, rows] = (normed * (1.0 + mod_ref[i, 1:2, :]) + mod_ref[i, 0:1, :]).astype(BF)
    proj = (nt(hid_ref[0], w_ref[...]) + bias_ref[...]).astype(BF)
    for which, out in enumerate((q_ref, k_ref, v_ref)):
        for h in range(heads):
            at = (which * heads + h) * size
            out[0, h] = proj[:, at : at + size]


def project(tokens, mod_blocks, qkv_weight, qv_bias, blocks):
    micro, rows, width = tokens.shape
    share = rows // blocks
    local = qkv_weight.shape[1]
    heads = local // HEAD_DIM
    weight = qkv_weight.reshape(3 * local, width)
    bias = jnp.concatenate([qv_bias[0], jnp.zeros_like(qv_bias[0]), qv_bias[1]])[None]
    head_shape = shape((micro, heads, rows, HEAD_DIM), BF)
    head_spec = pl.BlockSpec((1, heads, 2 * share, HEAD_DIM), lambda m, b: (m, 0, b, 0))
    return pl.pallas_call(
        project_kernel,
        grid=(micro, blocks // 2),
        in_specs=[
            pl.BlockSpec((1, 2 * share, width), lambda m, b: (m, b, 0)),
            pl.BlockSpec((2, 6, width), lambda m, b: (m * (blocks // 2) + b, 0, 0)),
            pl.BlockSpec(weight.shape, lambda m, b: (0, 0)),
            pl.BlockSpec(bias.shape, lambda m, b: (0, 0)),
        ],
        out_specs=[
            pl.BlockSpec((1, 2 * share, width), lambda m, b: (m, b, 0)),
            head_spec,
            head_spec,
            head_spec,
        ],
        out_shape=[shape(tokens.shape, BF), head_shape, head_shape, head_shape],
        compiler_params=params(),
        cost_estimate=cost(0.01),
        name="project",
    )(tokens, mod_blocks, weight, bias)


def attend_kernel(info_ref, q_ref, k_ref, v_ref, a0, a1, a2, a3, lse_ref):
    _, heads, rows, size = q_ref.shape
    share = rows // 4
    rank = info_ref[0]
    whole = info_ref[1 + pl.program_id(0)]
    factor = size ** (-0.5) * LOG2E
    lane = lax.broadcasted_iota(jnp.int32, (share, 128), 1)

    def run(full):
        for shift, att_ref in enumerate((a0, a1, a2, a3)):
            block = pl.ds(pl.multiple_of(lax.rem(rank + shift, 4) * share, share), share)
            span = slice(None) if full else block
            logs = jnp.zeros((share, 128), F32)
            outs = []
            for h in range(heads):
                scores = nt(q_ref[0, h, block, :], k_ref[0, h, span, :])
                top = jnp.max(scores, axis=-1, keepdims=True)
                weight = jnp.exp2((scores - top) * factor)
                total = jnp.sum(weight, axis=-1, keepdims=True)
                out = nn(weight.astype(BF), v_ref[0, h, span, :])
                outs.append((out * (1.0 / total)).astype(BF))
                logs = jnp.where(lane == h, top * factor + jnp.log2(total), logs)
            att_ref[0] = pack_rows(jnp.concatenate(outs, axis=1))
            lse_ref[0, :, block] = logs.T[0:heads, :]

    @pl.when(whole == 1)
    def _():
        run(True)

    @pl.when(whole == 0)
    def _():
        run(False)


def attend(info, query, key, value, after=()):
    micro, heads, rows, size = query.shape
    share = rows // 4
    full = pl.BlockSpec((1, heads, rows, size), lambda m, s: (m, 0, 0, 0))
    packed = (share // 4, 4 * heads * size)
    part = pl.BlockSpec((1, *packed), lambda m, s: (m, 0, 0))
    return pl.pallas_call(
        skipping(attend_kernel, 4, len(after)),
        grid_spec=pltpu.PrefetchScalarGridSpec(
            num_scalar_prefetch=1,
            grid=(micro,),
            in_specs=[full] * 3 + [ANY] * len(after),
            out_specs=[part] * 4 + [pl.BlockSpec((1, heads, rows), lambda m, s: (m, 0, 0))],
        ),
        out_shape=[shape((micro, *packed), BF)] * 4 + [shape((micro, heads, rows), F32)],
        compiler_params=params(),
        cost_estimate=cost(0.01),
        name="attend",
    )(info, query, key, value, *after)


def middle_kernel(info_ref, a0, a1, a2, a3, w_ref, bias_ref, tok_ref, mod_ref, attn_ref, mid_ref, hid_ref):
    rank = info_ref[0]
    total = bias_ref[0:1, :]
    for shift, part in enumerate((a0, a1, a2, a3)):
        total = total + nn(unpack_rows(part[0]), w_ref[lax.rem(rank + 4 - shift, 4)])
    attn_ref[0] = total
    mid = tok_ref[0].astype(F32) + mod_ref[0, 2:3, :] * total
    mid_ref[0] = mid
    normed, _ = normalize(mid)
    hid_ref[0] = (normed * (1.0 + mod_ref[0, 4:5, :]) + mod_ref[0, 3:4, :]).astype(BF)


def middle(info, parts, out_full, out_bias, tokens, mod_blocks, blocks, after=()):
    micro = parts[0].shape[0]
    share, width = tokens.shape[1] // blocks, tokens.shape[2]
    part = pl.BlockSpec((1, *parts[0].shape[1:]), lambda m, s: (m, 0, 0))
    row = pl.BlockSpec((1, share, width), lambda m, s: (m, 0, 0))
    return pl.pallas_call(
        skipping(middle_kernel, 9, len(after)),
        grid_spec=pltpu.PrefetchScalarGridSpec(
            num_scalar_prefetch=1,
            grid=(micro,),
            in_specs=[part] * 4
            + [
                pl.BlockSpec(out_full.shape, lambda m, s: (0, 0, 0)),
                pl.BlockSpec((1, width), lambda m, s: (0, 0)),
                pl.BlockSpec((1, share, width), lambda m, s: (m, s[0], 0)),
                pl.BlockSpec((1, 6, width), lambda m, s: (m * blocks + s[0], 0, 0)),
            ]
            + [ANY] * len(after),
            out_specs=[row, row, row],
        ),
        out_shape=[
            shape((micro, share, width), F32),
            shape((micro, share, width), F32),
            shape((micro, share, width), BF),
        ],
        compiler_params=params(),
        cost_estimate=cost(8),
        name="middle",
    )(info, *parts, out_full, out_bias, tokens, mod_blocks, *after)


def feed_kernel(first, kinds, *refs):
    xo, xt, go, gt = refs[:4]
    at = 4
    weights = []
    for kind in kinds:
        weights.append(refs[at : at + kind])
        at += kind
    bias_ref = refs[at]
    at += 1
    if not first:
        carry = refs[at : at + 4]
        at += 4
    mo, mt, ho, ht, wuk, wus, wdk, wds, bsum_ref = refs[at : at + 9]
    xs, gs, us, ds, acts, dps, wtmp = refs[at + 9 :]
    half = xo.shape[0]
    units = us.shape[0]
    piece = units // 4
    step = pl.program_id(0)
    chunk = 512

    @pl.when(step == 0)
    def _():
        xs[:half] = xo[...]
        xs[half:] = xt[...]
        gs[:half] = go[...]
        gs[half:] = gt[...]
        if first:
            for ref in (mo, mt, ho, ht):
                ref[...] = jnp.zeros_like(ref)
        else:
            for ref, old in zip((mo, mt, ho, ht), carry):
                ref[...] = old[...]

    index = 0
    for parts in weights:
        blocks = [parts]
        if len(parts[0].shape) == 3:
            blocks = [[ref.at[i] for ref in parts] for i in range(parts[0].shape[0])]
        for block in blocks:

            @pl.when(step == index)
            def _(block=block):
                if len(block) == 2:
                    us[...] = block[0][...]
                    ds[...] = block[1][...]
                    return
                for j in range(4):
                    up = block[j]
                    down = block[-1] if j == 3 else block[j]
                    us[j * piece : (j + 1) * piece] = up[:piece]
                    ds[j * piece : (j + 1) * piece] = down[down.shape[0] - piece :]

            index += 1

    bias = bias_ref[0]

    def rows_step(base, mlp_ref, gh_ref):
        def run(i, sums):
            rows = pl.ds(pl.multiple_of(base + i * chunk, chunk), chunk)
            out = pl.ds(pl.multiple_of(i * chunk, chunk), chunk)
            pre = nt(xs[rows, :], us[...]) + bias
            square = pre * pre
            tanh = jnp.tanh(GELU_C * pre * (1.0 + GELU_A * square))
            act = (0.5 * pre * (1.0 + tanh)).astype(BF)
            acts[rows, :] = act
            slope = 0.5 * (1.0 + tanh) + (0.5 * GELU_C) * pre * (1.0 - tanh * tanh) * (
                1.0 + 3.0 * GELU_A * square
            )
            dpre = nt(gs[rows, :], ds[...]) * slope
            low = dpre.astype(BF)
            dps[rows, :] = low
            mlp_ref[out, :] = mlp_ref[out, :] + nn(act, ds[...])
            gh_ref[out, :] = gh_ref[out, :] + nn(low, us[...])
            return sums + jnp.sum(dpre, axis=0, keepdims=True)

        return run

    sums = jnp.zeros((1, units), F32)
    sums = lax.fori_loop(0, half // chunk, rows_step(0, mo, ho), sums)
    sums = lax.fori_loop(0, half // chunk, rows_step(half, mt, ht), sums)
    bsum_ref[0] = sums
    for lhs, rhs, order in ((dps, xs, ((wuk, 0), (wuk, 1), (wus, 0), (wus, 1))),
                            (acts, gs, ((wdk, 0), (wds, 0), (wdk, 1), (wds, 1)))):
        for start in range(0, units, 256):
            stop = min(start + 256, units)
            wtmp[start:stop] = tn(lhs[:, start:stop], rhs[...]).astype(BF)
        for j, (ref, place) in enumerate(order):
            ref[0, place] = wtmp[j * piece : (j + 1) * piece]


def feed(own_x, other_x, own_g, other_g, weights, bias, carry):
    half, width = own_x.shape
    count, _, units = bias.shape
    piece = units // 4
    first = carry is None

    def whole(array):
        zeros = (0,) * len(array.shape)
        return pl.BlockSpec(array.shape, lambda k: zeros)

    operands = [own_x, other_x, own_g, other_g]
    for parts in weights:
        operands += list(parts)
    in_specs = [whole(a) for a in operands]
    in_specs.append(pl.BlockSpec((1, 1, units), lambda k: (k, 0, 0)))
    operands.append(bias)
    acc = pl.BlockSpec((half, width), lambda k: (0, 0))
    if not first:
        in_specs += [acc] * 4
        operands += list(carry)
    wspec = pl.BlockSpec((1, 2, piece, width), lambda k: (k, 0, 0, 0))
    return pl.pallas_call(
        functools.partial(feed_kernel, first, tuple(len(p) for p in weights)),
        grid=(count,),
        in_specs=in_specs,
        out_specs=[acc] * 4 + [wspec] * 4 + [pl.BlockSpec((1, 1, units), lambda k: (k, 0, 0))],
        out_shape=[shape((half, width), F32)] * 4
        + [shape((count, 2, piece, width), BF)] * 4
        + [shape((count, 1, units), F32)],
        scratch_shapes=[
            pltpu.VMEM((2 * half, width), BF),
            pltpu.VMEM((2 * half, width), BF),
            pltpu.VMEM((units, width), BF),
            pltpu.VMEM((units, width), BF),
            pltpu.VMEM((2 * half, units), BF),
            pltpu.VMEM((2 * half, units), BF),
            pltpu.VMEM((units, width), BF),
        ],
        compiler_params=params(),
        cost_estimate=cost(34),
        name="feed",
    )(*operands)


def between_kernel(
    info_ref, gho, ght, mlpo, mlpt, mid_ref, attn_ref, og_ref, mod_ref, dbias_ref, w_ref,
    a0, a1, a2, a3, layer_ref, gmid_ref, d0, d1, d2, d3, wkeep, wsend, sums_ref, wout_ref,
):
    rank = info_ref[0]
    micro = pl.program_id(0)
    valid = info_ref[1 + micro].astype(F32)
    mod = mod_ref[0]
    mid = mid_ref[0]
    attn = attn_ref[0]
    normed, inverse = normalize(mid)
    mlp_out = mlpo[...] + mlpt[...] + dbias_ref[0:1, :]
    layer_ref[0] = (valid * (mid + mod[5:6, :] * mlp_out)).astype(BF)
    grad_y = og_ref[0].astype(F32) * valid
    grad_hidden = gho[...] + ght[...]
    grad_mid = grad_y + norm_backward(grad_hidden * (1.0 + mod[4:5, :]), normed, inverse)
    gmid_ref[0] = grad_mid
    grad_attn = grad_mid * mod[2:3, :]
    sums_ref[0, 0:1, :] = jnp.sum(grad_mid * attn, axis=0, keepdims=True)
    sums_ref[0, 1:2, :] = jnp.sum(grad_hidden, axis=0, keepdims=True)
    sums_ref[0, 2:3, :] = jnp.sum(grad_hidden * normed, axis=0, keepdims=True)
    sums_ref[0, 3:4, :] = jnp.sum(grad_y * mlp_out, axis=0, keepdims=True)
    sums_ref[0, 4:5, :] = jnp.sum(grad_attn, axis=0, keepdims=True)
    sums_ref[0, 5:6, :] = jnp.sum(grad_y * mod[5:6, :], axis=0, keepdims=True)
    low = grad_attn.astype(BF)
    for shift, (out, part) in enumerate(((d0, a0), (d1, a1), (d2, a2), (d3, a3))):
        out[0] = pack_rows(nt(low, w_ref[lax.rem(rank + 4 - shift, 4)]).astype(BF))
        update = tn(unpack_rows(part[0]), low)
        half = update.shape[0] // 2

        @pl.when(micro == 0)
        def _(shift=shift, update=update):
            wout_ref[shift] = update

        @pl.when(micro > 0)
        def _(shift=shift, update=update):
            wout_ref[shift] = wout_ref[shift] + update

    @pl.when(micro == pl.num_programs(0) - 1)
    def _():
        core = info_ref[3]
        for shift in range(4):
            here = pl.ds(pl.multiple_of(core * half, half), half)
            there = pl.ds(pl.multiple_of((1 - core) * half, half), half)
            wkeep[shift] = wout_ref[shift, here, :].astype(BF)
            wsend[shift] = wout_ref[shift, there, :].astype(BF)


def between(info, feed_own, feed_other, mid, attn, out_grad, mod_blocks, down_bias, out_full, parts, blocks, after=()):
    micro, share, width = mid.shape
    local = parts[0].shape[2] // 4
    half = pl.BlockSpec((share, width), lambda m, s: (m, 0))
    row = pl.BlockSpec((1, share, width), lambda m, s: (m, 0, 0))
    part = pl.BlockSpec((1, *parts[0].shape[1:]), lambda m, s: (m, 0, 0))
    mlp_own, gh_own = feed_own
    mlp_other, gh_other = feed_other
    dshape = shape(parts[0].shape, BF)
    return pl.pallas_call(
        skipping(between_kernel, 15, len(after)),
        grid_spec=pltpu.PrefetchScalarGridSpec(
            num_scalar_prefetch=1,
            grid=(micro,),
            in_specs=[half] * 4
            + [
                row,
                row,
                pl.BlockSpec((1, share, width), lambda m, s: (m, s[0], 0)),
                pl.BlockSpec((1, 6, width), lambda m, s: (m * blocks + s[0], 0, 0)),
                pl.BlockSpec((1, width), lambda m, s: (0, 0)),
                pl.BlockSpec(out_full.shape, lambda m, s: (0, 0, 0)),
            ]
            + [part] * 4
            + [ANY] * len(after),
            out_specs=[row, row, part, part, part, part]
            + [
                pl.BlockSpec((blocks, local // 2, width), lambda m, s: (0, 0, 0)),
                pl.BlockSpec((blocks, local // 2, width), lambda m, s: (0, 0, 0)),
                pl.BlockSpec((1, 8, width), lambda m, s: (m, 0, 0)),
            ],
            scratch_shapes=[pltpu.VMEM((blocks, local, width), F32)],
        ),
        out_shape=[
            shape((micro, share, width), BF),
            shape((micro, share, width), F32),
            dshape,
            dshape,
            dshape,
            dshape,
            shape((blocks, local // 2, width), BF),
            shape((blocks, local // 2, width), BF),
            shape((micro, 8, width), F32),
        ],
        compiler_params=params(),
        cost_estimate=cost(18),
        name="between",
    )(info, gh_own, gh_other, mlp_own, mlp_other, mid, attn, out_grad, mod_blocks, down_bias, out_full, *parts, *after)


def attend_back_kernel(
    micro, last, count, info_ref, q_ref, k_ref, v_ref, lse_ref, g0, g1, g2, g3, w_ref, hid_ref, tok_ref, *refs
):
    if last:
        old_ref, refs = refs[0], refs[1:]
    refs = refs[count:]
    part_ref, refs = refs[0], refs[1:]
    if last:
        sums_ref, bias_ref, wkeep, wsend = refs[:4]
        refs = refs[4:]
    else:
        sums_ref, bias_ref, wout = refs[:3]
        refs = refs[3:]
    dos, dqs, dks, dvs, dq_ref, dk_ref, dv_ref, wtmp, w_here, hid_here, tok_here, sems, *old_here = refs
    copies = [
        pltpu.make_async_copy(source, here, sems.at[i])
        for i, (source, here) in enumerate(
            [(w_ref, w_here), (tok_ref.at[micro], tok_here), (hid_ref.at[micro], hid_here)]
            + ([(old_ref, old_here[0])] if last else [])
        )
    ]
    for copy in copies:
        copy.start()
    _, heads, rows, size = q_ref.shape
    share = rows // 4
    local = heads * size
    rank = info_ref[0]
    whole = info_ref[1]
    scale = size ** (-0.5)
    factor = scale * LOG2E
    for shift, grad in enumerate((g0, g1, g2, g3)):
        grad = unpack_rows(grad[0])
        for h in range(heads):
            dos[h, shift] = grad[:, h * size : (h + 1) * size]

    def block_of(shift):
        return pl.multiple_of(lax.rem(rank + shift, 4) * share, share)

    def tile(h, shift, keys, values, keys_t):
        query = q_ref[0, h, pl.ds(block_of(shift), share), :]
        grad = dos[h, shift]
        lse = lse_ref[0, pl.ds(h, 1), pl.ds(block_of(shift), share)]
        probs = jnp.exp2(nt(keys, query) * factor - lse)
        dprobs = nt(values, grad)
        inner = jnp.sum(probs * dprobs, axis=0, keepdims=True)
        dscores = (probs * (dprobs - inner)).astype(BF)
        dqs[h, pl.ds(block_of(shift), share), :] = (nn(keys_t, dscores) * scale).T.astype(BF)
        return nn(dscores, query), nn(probs.astype(BF), grad)

    @pl.when(whole == 1)
    def _():
        def head(h, carry):
            keys = k_ref[0, h]
            values = v_ref[0, h]
            keys_t = keys.astype(F32).T.astype(BF)
            dkey, dvalue = tile(h, 0, keys, values, keys_t)
            for shift in range(1, 4):
                more_key, more_value = tile(h, shift, keys, values, keys_t)
                dkey = dkey + more_key
                dvalue = dvalue + more_value
            dks[h] = (dkey * scale).astype(BF)
            dvs[h] = dvalue.astype(BF)
            return carry

        lax.fori_loop(0, heads, head, 0)

    @pl.when(whole == 0)
    def _():
        def head(h, carry):
            for shift in range(4):
                span = pl.ds(block_of(shift), share)
                keys = k_ref[0, h, span, :]
                values = v_ref[0, h, span, :]
                dkey, dvalue = tile(h, shift, keys, values, keys.astype(F32).T.astype(BF))
                dks[h, span, :] = (dkey * scale).astype(BF)
                dvs[h, span, :] = dvalue.astype(BF)
            return carry

        lax.fori_loop(0, heads, head, 0)

    for src, dst in ((dqs, dq_ref), (dks, dk_ref), (dvs, dv_ref)):
        for h in range(heads):
            dst[:, h * size : (h + 1) * size] = src[h]

    copies[0].wait()
    copies[1].wait()

    def out_rows(i, carry):
        span = pl.ds(pl.multiple_of(i * share, share), share)
        grad = nn(dq_ref[span, :], w_here[0]) + nn(dk_ref[span, :], w_here[1]) + nn(dv_ref[span, :], w_here[2])
        part_ref[span, :] = grad.astype(BF)
        normed, _ = normalize(tok_here[span, :].astype(F32))
        sums_ref[pl.ds(2 * i, 1), :] = jnp.sum(grad, axis=0, keepdims=True)
        sums_ref[pl.ds(2 * i + 1, 1), :] = jnp.sum(grad * normed, axis=0, keepdims=True)
        return carry

    lax.fori_loop(0, rows // share, out_rows, 0)
    bias_ref[...] = jnp.zeros_like(bias_ref)
    bias_ref[0:1, :] = jnp.sum(dq_ref[...].astype(F32), axis=0, keepdims=True)
    bias_ref[1:2, :] = jnp.sum(dv_ref[...].astype(F32), axis=0, keepdims=True)
    for copy in copies[2:]:
        copy.wait()
    for which, ref in enumerate((dq_ref, dk_ref, dv_ref)):
        span = slice(which * local, (which + 1) * local)
        update = tn(ref[...], hid_here[...])
        if last:
            wtmp[span] = (old_here[0][span] + update).astype(BF)
        else:
            wout[span] = update
    if last:
        core = info_ref[2]
        half = 3 * local // 2
        for ref, place in ((wkeep, core), (wsend, 1 - core)):
            ref[:half] = wtmp[pl.ds(pl.multiple_of(place * half, half), half), :]
            ref[half:] = jnp.zeros((ref.shape[0] - half, ref.shape[1]), BF)


def attend_back(micro, info, query, key, value, lse, grads, qkv_weight, hidden, tokens, old=None, after=()):
    _, heads, rows, size = query.shape
    share = rows // 4
    local = heads * size
    width = qkv_weight.shape[2]
    last = old is not None
    full = pl.BlockSpec((1, heads, rows, size), lambda i, s: (micro, 0, 0, 0))
    def flat(*dims):
        return pl.BlockSpec(dims, lambda i, s: (0,) * len(dims))

    outs = [((rows, width), BF), ((8, width), F32), ((8, local), F32)]
    if last:
        outs += [((-(-3 * local // 128) * 64, width), BF)] * 2
    else:
        outs += [((3 * local, width), F32)]
    return pl.pallas_call(
        functools.partial(attend_back_kernel, micro, last, len(after)),
        grid_spec=pltpu.PrefetchScalarGridSpec(
            num_scalar_prefetch=1,
            grid=(1,),
            in_specs=[full] * 3
            + [pl.BlockSpec((1, heads, rows), lambda i, s: (micro, 0, 0))]
            + [pl.BlockSpec((1, *grads[0].shape[1:]), lambda i, s: (micro, 0, 0))] * 4
            + [ANY] * (3 + int(last) + len(after)),
            out_specs=[flat(*dims) for dims, _ in outs],
            scratch_shapes=[
                pltpu.VMEM((heads, 4, share, size), BF),
                pltpu.VMEM((heads, rows, size), BF),
                pltpu.VMEM((heads, rows, size), BF),
                pltpu.VMEM((heads, rows, size), BF),
                pltpu.VMEM((rows, local), BF),
                pltpu.VMEM((rows, local), BF),
                pltpu.VMEM((rows, local), BF),
                pltpu.VMEM((3 * local, width), BF),
                pltpu.VMEM(qkv_weight.shape, BF),
                pltpu.VMEM((rows, width), BF),
                pltpu.VMEM((rows, width), BF),
                pltpu.SemaphoreType.DMA((4,)),
            ]
            + ([pltpu.VMEM((3 * local, width), F32)] if last else []),
        ),
        out_shape=[shape(dims, dtype) for dims, dtype in outs],
        compiler_params=params(),
        cost_estimate=cost(30),
        name="attend_back",
    )(info, query, key, value, lse, *grads, qkv_weight, hidden, tokens, *([old] if last else []), *after)


def finish_kernel(info_ref, grad_ref, tok_ref, mod_ref, gmid_ref, out_ref):
    normed, inverse = normalize(tok_ref[0].astype(F32))
    grad = grad_ref[...].astype(F32)
    out_ref[0] = gmid_ref[0] + norm_backward(grad * (1.0 + mod_ref[0, 1:2, :]), normed, inverse)


def finish(info, micro, grad, tokens, mod_blocks, gmid, blocks, old=None, after=()):
    _, share, width = gmid.shape
    more = ([] if old is None else [old]) + list(after)
    return pl.pallas_call(
        skipping(finish_kernel, 5, len(more)),
        grid_spec=pltpu.PrefetchScalarGridSpec(
            num_scalar_prefetch=1,
            grid=(1,),
            in_specs=[
                pl.BlockSpec((share, width), lambda i, s: (0, 0)),
                pl.BlockSpec((1, share, width), lambda i, s: (micro, s[0], 0)),
                pl.BlockSpec((1, 6, width), lambda i, s: (micro * blocks + s[0], 0, 0)),
                pl.BlockSpec((1, share, width), lambda i, s: (micro, 0, 0)),
            ]
            + [ANY] * len(more),
            out_specs=[pl.BlockSpec((1, share, width), lambda i, s: (micro, 0, 0))],
        ),
        out_shape=[shape(gmid.shape, F32)],
        input_output_aliases={} if old is None else {5: 0},
        compiler_params=params(),
        cost_estimate=cost(3),
        name="finish",
    )(info, grad, tokens, mod_blocks, gmid, *more)[0]


def in_order(row, quarter, piece):
    parts = [row[:, i * piece : (i + 1) * piece] for i in range(4)]
    out = []
    for j in range(4):
        source = jnp.bitwise_xor(quarter, j)
        value = parts[3]
        for i in range(3):
            value = jnp.where(source == i, parts[i], value)
        out.append(value)
    return jnp.concatenate(out, axis=1)


def ada_kernel(info, cond_ref, w_ref, bias_ref, units_ref, small_ref, act_ref):
    value = jnp.concatenate([cond_ref[m].astype(F32) for m in range(cond_ref.shape[0])], axis=0)
    act = (value / (1.0 + jnp.exp(-value))).astype(BF)
    act_ref[...] = act
    count, columns = act.shape[0], w_ref.shape[0]
    small_ref[:, :columns] = nt(act, w_ref[...]) + bias_ref[...][None]
    units = units_ref[...][None]
    half = units.shape[1] // 2
    mine = jnp.where(info[1] == 0, units[:, :half], units[:, half:])
    mine = in_order(mine, info[2], half // 4)
    each = half // count
    for i in range(count):
        small_ref[i : i + 1, columns:] = mine[:, i * each : (i + 1) * each]


def modulate_kernel(info, s0, s1, s2, s3, mod_ref, far_ref, near_ref, lanes, full):
    rank = info[0]
    count, columns = lanes.shape[1:]
    for shift, ref in enumerate((s0, s1, s2, s3)):
        lanes[lax.rem(rank + 4 - shift, 4)] = ref[:, :columns]
    full[...] = jnp.concatenate([lanes[i] for i in range(4)], axis=1)
    width = mod_ref.shape[2]
    for i in range(mod_ref.shape[0]):
        segment = info[3 + i]
        slot = (i // 4) * 4 + jnp.minimum(segment, 3)
        row = full[pl.ds(slot, 1), :] * (segment < 4).astype(F32)
        for j in range(6):
            mod_ref[i, j : j + 1, :] = row[:, j * width : (j + 1) * width]
    for ref, order in ((far_ref, (s2, s1)), (near_ref, (s3, s0))):
        for i, source in enumerate(order):
            ref[i] = jnp.concatenate([source[j : j + 1, columns:] for j in range(count)], axis=1)


def pile_kernel(info, l0, l1, sums, far, near, out):
    rank = info[0]
    out[...] = jnp.zeros_like(out)
    for m, late in enumerate((l0, l1)):
        for slot in range(4):
            row = 6 * (4 * m + slot)
            for i in range(2):
                total = jnp.zeros((1, out.shape[1]), F32)
                for block in range(4):
                    inside = (info[3 + m * 4 + block] == slot).astype(F32)
                    total = total + inside * late[2 * block + i : 2 * block + i + 1, :]
                out[row + i : row + i + 1, :] = total
            inside = (info[3 + m * 4 + rank] == slot).astype(F32)
            out[row + 2 : row + 6, :] = inside * sums[m, 0:4, :]
    out[48:50, :] = sums[0, 4:6, :] + sums[1, 4:6, :]
    half = far.shape[2]
    for k, (ref, i) in enumerate(((near, 1), (far, 1), (far, 0), (near, 0))):
        out[pl.ds(50 + lax.rem(rank + 4 - k, 4), 1), :half] = ref[i]


def sum_kernel(a, b, out):
    out[...] = a[...] + b[...]


def slots_kernel(info, mine, got, b0, b1, act_ref, pay_ref, low_ref, full):
    rank = info[0]
    width = mine.shape[1]
    total = mine[...] + got[...]
    for row in range(8):
        for i in range(6):
            full[row : row + 1, i * width : (i + 1) * width] = total[6 * row + i : 6 * row + i + 1, :]
    columns = pay_ref.shape[1]
    half = columns - width
    pay_ref[...] = jnp.zeros_like(pay_ref)
    for i in range(4):

        @pl.when(rank == i)
        def _(i=i):
            own = full[:, i * columns : (i + 1) * columns]
            pay_ref[0:8, :] = own
            low_ref[...] = own.astype(BF)
            pay_ref[8:9, width:] = in_order(total[50 + i : 51 + i, :half], info[2], half // 4)

    pay_ref[8:9, :width] = total[48:49]
    pay_ref[9:10, :width] = total[49:50]
    both = b0[0:2, :] + b1[0:2, :]
    pay_ref[9:10, width:] = jnp.concatenate([both[0:1], both[1:2]], axis=1)
    pay_ref[10:18, :width] = act_ref[...].astype(F32)


def tail_kernel(info, pay_ref, ada_ref, ada_b, out_b, down_b, up_b, qv_b):
    width = out_b.shape[0]
    columns = pay_ref.shape[2]
    half = columns - width
    count = pay_ref.shape[0]
    mods = jnp.concatenate([pay_ref[i, 0:8, :] for i in range(count)], axis=0)
    acts = jnp.concatenate([pay_ref[i, 10:18, :width] for i in range(count)], axis=0)
    ada_ref[...] = tn(mods.astype(BF), acts.astype(BF))
    ada_b[...] = jnp.sum(mods, axis=0)
    sums = [pay_ref[0, 8:10, :], pay_ref[1, 8:10, :]]
    for i in range(2, count):
        sums[i % 2] = sums[i % 2] + pay_ref[i, 8:10, :]
    total = sums[0] + sums[1]
    out_b[...] = total[0, :width]
    down_b[...] = total[1, :width]
    low = jnp.where(info[1] == 0, sums[0][0:1, width:], sums[1][0:1, width:])
    high = jnp.where(info[1] == 0, sums[1][0:1, width:], sums[0][0:1, width:])
    up_b[...] = jnp.concatenate([low, high], axis=1)[0]
    qv_b[0:1, :] = total[1:2, width : width + half // 2]
    qv_b[1:2, :] = total[1:2, width + half // 2 :]


def pack_kernel(info, up_ref, down_ref, up_out, down_out, mine_ref, turned):
    turned[...] = up_ref[...].T
    half = up_out.shape[0]
    piece = half // 4
    for j in range(4):
        at = info[1] * half + jnp.bitwise_xor(info[2], j) * piece
        rows = pl.ds(pl.multiple_of(at, piece), piece)
        up = turned[rows, :]
        down = down_ref[rows, :]
        up_out[j * piece : (j + 1) * piece] = up
        down_out[j * piece : (j + 1) * piece] = down
        if j == 0:
            mine_ref[:piece] = up
            mine_ref[piece:] = down


def tick_kernel(out):
    out[...] = jnp.zeros_like(out)


def copy_kernel(*refs):
    count = len(refs) // 2
    for source, out in zip(refs[:count], refs[count:]):
        out[...] = source[...]


def stack_kernel(first, second, out):
    out[0] = first[...]
    out[1] = second[...]


def pack_rows(array):
    rows = array.shape[0] // 4
    return jnp.concatenate([array[i * rows : (i + 1) * rows] for i in range(4)], axis=1)


def unpack_rows(array):
    columns = array.shape[1] // 4
    return jnp.concatenate([array[:, i * columns : (i + 1) * columns] for i in range(4)], axis=0)


def corner_kernel(x_ref, y_ref, up_out, down_out):
    piece = up_out.shape[1]
    up_out[...] = x_ref[:, :piece]
    down_out[...] = y_ref[:, piece:]


def plus(a, b):
    return a.astype(F32) + b.astype(F32)


def halve_kernel(uk, ur, dk, dr, u_keep, u_send, d_keep, d_send):
    for keep, got, mine, give in ((uk, ur, u_keep, u_send), (dk, dr, d_keep, d_send)):
        for i in range(keep.shape[0]):
            mine[i] = plus(keep[i, 0], got[i, 0]).astype(BF)
            give[i] = plus(keep[i, 1], got[i, 1]).astype(BF)


def quarter_kernel(uk, ur, dk, dr, first, second):
    piece = uk.shape[1]
    for i, out in enumerate((first, second)):
        out[:piece] = plus(uk[i], ur[i]).astype(BF)
        out[piece:] = plus(dk[i], dr[i]).astype(BF)


def mix_kernel(o_rows, info, uk, us, dk, ds, ok, og, u_keep, u_send, d_keep, d_send, room, sums):
    room[...] = jnp.zeros_like(room)
    for k in range(4):
        sums[...] = plus(ok[k], og[k])
        for i in range(4):
            room[k, jnp.bitwise_xor(info[2], i), :o_rows] = sums[i * o_rows : (i + 1) * o_rows].astype(BF)
    piece = uk.shape[2]
    wide = room.shape[2]
    for keep, send, mine, give, planes, near, far in (
        (uk, us, u_keep, u_send, (0, 1), (0, 1), (2, 3)),
        (dk, ds, d_keep, d_send, (2, 3), (0, 2), (1, 3)),
    ):
        for source, out, order in ((keep, mine, near), (send, give, far)):
            at = 0
            for place in range(2):
                for i in range(2):
                    out[at : at + piece] = source[i, place]
                    at += piece
                for k in planes:
                    out[at : at + wide] = room[k, order[place]]
                    at += wide


def halve_flat_kernel(uk, ur, dk, dr, u_keep, u_send, d_keep, d_send):
    for keep, got, mine, give in ((uk, ur, u_keep, u_send), (dk, dr, d_keep, d_send)):
        half = mine.shape[0]
        mine[...] = plus(keep[:half], got[:half]).astype(BF)
        give[...] = plus(keep[half:], got[half:]).astype(BF)


def last_kernel(uk, ur, dk, dr, third, o1, o2, own):
    wide = o1.shape[0]
    piece = (uk.shape[0] - 2 * wide) // 2
    up = plus(uk[...], ur[...]).astype(BF)
    down = plus(dk[...], dr[...]).astype(BF)
    for out, i in ((third, 0), (own, 1)):
        out[:piece] = up[i * piece : (i + 1) * piece]
        out[piece : 2 * piece] = down[i * piece : (i + 1) * piece]
    own[2 * piece :] = up[2 * piece : 2 * piece + wide]
    o1[...] = up[2 * piece + wide :]
    o2[...] = down[2 * piece : 2 * piece + wide]
    third[2 * piece :] = down[2 * piece + wide :]


def split_rows(total, bit, keep, send):
    half = total.shape[0] // 2
    keep[...] = total[pl.ds(pl.multiple_of(bit * half, half), half), :]
    send[...] = total[pl.ds(pl.multiple_of((1 - bit) * half, half), half), :]


def first_kernel(info, mine, got, keep, send, total):
    total[...] = plus(mine[...], got[...]).astype(BF)
    split_rows(total, jnp.bitwise_and(info[2], 1), keep, send)


def second_kernel(info, mine, got, keep, send, total):
    total[...] = plus(mine[...], got[...]).astype(BF)
    split_rows(total, info[2] >> 1, keep, send)


def merge_kernel(keep, got, own, first, second, third, o1, o2, out):
    at = keep.shape[0]
    out[:at] = plus(keep[...], got[...]).astype(BF)
    rows = first.shape[0]
    out[at : at + rows] = (plus(own[:rows], first[...]) + plus(second[...], third[:rows])).astype(BF)
    out[at + rows :] = (plus(own[rows:], o1[...]) + plus(o2[...], third[rows:])).astype(BF)


def order_kernel(o_rows, w_rows, info, b0, b1, b2, b3, halves, others, room):
    piece = halves.shape[1] // 4
    wide = room.shape[1]
    for j, ref in enumerate((b0, b1, b2, b3)):
        quarter = jnp.bitwise_xor(info[2], j)
        place = 2 * jnp.bitwise_and(quarter, 1) + (quarter >> 1)
        others[pl.ds(pl.multiple_of(place * w_rows, w_rows), w_rows), :] = ref[:w_rows]
        rows = pl.ds(pl.multiple_of(quarter * piece, piece), piece)
        halves[0, rows, :] = ref[w_rows : w_rows + piece]
        halves[1, rows, :] = ref[w_rows + piece : w_rows + 2 * piece]
        room[quarter] = ref[w_rows + 2 * piece :]
    outs = jnp.concatenate([room[i, :o_rows] for i in range(4)], axis=0)
    others[4 * w_rows :] = outs


def spread_kernel(info, own, other, own_o, other_o, up_out, down_out, qkv_out, out_out, turned, total):
    half = own.shape[1]
    here = pl.ds(pl.multiple_of(info[1] * half, half), half)
    there = pl.ds(pl.multiple_of((1 - info[1]) * half, half), half)
    turned[here, :] = own[0]
    turned[there, :] = other[0]
    down_out[here, :] = own[1].astype(F32)
    down_out[there, :] = other[1].astype(F32)
    rows = out_out.shape[0] // 2
    count = total.shape[0] // 2
    for ref, core in ((own_o, info[1]), (other_o, 1 - info[1])):
        out_out[pl.ds(pl.multiple_of(core * rows, rows), rows), :] = ref[ref.shape[0] - rows :].astype(F32)
        total[pl.ds(pl.multiple_of(core * count, count), count), :] = ref[:count]
    local = qkv_out.shape[1]
    for i in range(3):
        qkv_out[i] = total[i * local : (i + 1) * local].astype(F32)
    up_out[...] = turned[...].astype(F32).T


def spread(info, operands, outs, after):
    up, down, qkv, out = outs
    width = up[0]
    tile = 384 if width % 384 == 0 else width
    return pl.pallas_call(
        skipping(spread_kernel, 5, len(after)),
        grid_spec=pltpu.PrefetchScalarGridSpec(
            num_scalar_prefetch=1,
            grid=(width // tile,),
            in_specs=[pl.BlockSpec((*a.shape[:2], tile), lambda i, s: (0, 0, i)) for a in operands[:2]]
            + [pl.BlockSpec((a.shape[0], tile), lambda i, s: (0, i)) for a in operands[2:]]
            + [ANY] * len(after),
            out_specs=[
                pl.BlockSpec((tile, up[1]), lambda i, s: (i, 0)),
                pl.BlockSpec((down[0], tile), lambda i, s: (0, i)),
                pl.BlockSpec((*qkv[:2], tile), lambda i, s: (0, 0, i)),
                pl.BlockSpec((out[0], tile), lambda i, s: (0, i)),
            ],
            scratch_shapes=[pltpu.VMEM((up[1], tile), BF), pltpu.VMEM((3 * qkv[1], tile), BF)],
        ),
        out_shape=[shape(dims, F32) for dims in outs],
        compiler_params=params(),
        cost_estimate=cost(6),
        name="spread",
    )(info, *operands, *after)


def turn(array, shift):
    count = lax.axis_size("tensor")
    return lax.ppermute(array, "tensor", [(i, (i + shift) % count) for i in range(count)])


def flip(array, axis):
    return lax.ppermute(array, axis, [(0, 1), (1, 0)])


def diagonal(array):
    return lax.ppermute(array, ("y", "x"), [(0, 3), (1, 2), (2, 1), (3, 0)])


def over_rest(array):
    count = lax.axis_size("rest")
    bit = 1
    while bit < count:
        other = lax.ppermute(array, "rest", [(i, i ^ bit) for i in range(count)])
        array = plus(array, other).astype(BF)
        bit *= 2
    return array


DP = ("rest", "y", "x", "core")


def local(
    tokens, conditioning, lengths, out_grad, ada_weight, ada_bias, qkv_weight, qv_bias,
    out_weight, out_bias, up_weight, up_bias, down_weight, down_bias,
):
    groups = lax.axis_size("tensor")
    rank = lax.axis_index("tensor")
    core = lax.axis_index("core")
    quarter = 2 * lax.axis_index("y") + lax.axis_index("x")
    micro, rows, width = tokens.shape
    share = rows // groups
    slots = lengths.shape[1]
    part = up_weight.shape[1]
    half = part // 2
    piece = half // 4
    columns = ada_weight.shape[1]
    local_width = qkv_weight.shape[2]
    ada_turned = ada_weight.T
    qkv_turned = qkv_weight.transpose(0, 2, 1)
    here = jnp.stack([rank, core, quarter]).astype(jnp.int32)

    boundary = jnp.cumsum(lengths, axis=1)
    starts = jnp.arange(groups, dtype=jnp.int32) * share
    segment = jnp.sum((boundary[:, None, :] <= starts[None, :, None]).astype(jnp.int32), axis=2)
    whole = (segment[:, groups - 1] == 0).astype(jnp.int32)
    own_valid = (lax.dynamic_index_in_dim(segment, rank, 1, False) < slots).astype(jnp.int32)
    info = jnp.concatenate([here, segment.reshape(-1)])

    small, cond_act = simple(
        ada_kernel,
        [shape((micro * slots, columns + half // (micro * slots)), F32), shape((micro * slots, width), BF)],
        [conditioning, ada_turned, ada_bias, up_bias],
        info,
        name="ada", micros=0.01,
    )
    smalls = [small] + [turn(small, k) for k in (1, 2, 3)]

    up_near, down_near, mine = simple(
        pack_kernel,
        [shape((half, width), BF), shape((half, width), BF), shape((2 * piece, width), BF)],
        [up_weight, down_weight],
        info,
        after=(cond_act,),
        scratch=[pltpu.VMEM((part, width), BF)],
        name="pack", micros=0.01,
    )
    got = {k: turn(mine, k) for k in (2, 1)}
    out_rows = lax.dynamic_slice_in_dim(out_weight, quarter * (local_width // 4), local_width // 4, 0)
    out_full = lax.all_gather(out_rows, ("tensor", "y", "x"), axis=0, tiled=True)
    out_full = out_full.reshape(groups, local_width, width)

    mod_blocks, bias_a, bias_b = simple(
        modulate_kernel,
        [
            shape((micro * groups, 6, width), F32),
            shape((2, 1, half), F32),
            shape((2, 1, half), F32),
        ],
        smalls,
        info,
        after=(mine,),
        scratch=[
            pltpu.VMEM((4, micro * slots, columns), F32),
            pltpu.VMEM((micro * slots, 6 * width), F32),
        ],
        name="modulate", micros=0.01,
    )
    hidden_one, query, key, value = project(tokens, mod_blocks, qkv_turned, qv_bias, groups)

    own_gate = lax.dynamic_index_in_dim(
        mod_blocks.reshape(micro, groups, 6, width), rank, 1, False
    )[:, 5:6]
    own_grad = lax.dynamic_slice_in_dim(out_grad, rank * share, share, 1).astype(F32)
    grad_mlp = own_grad * (own_valid.astype(F32)[:, None, None] * own_gate)
    own_g = grad_mlp.astype(BF).reshape(micro * share, width)
    other_g = flip(own_g, "core")

    def release(arrays, after, micros=3):
        return simple(
            copy_kernel, [shape(a.shape, a.dtype) for a in arrays], arrays, after=after, name="release", micros=micros
        )

    *att, lse = attend(jnp.concatenate([rank[None], whole]), query, key, value)
    (two,) = simple(
        stack_kernel,
        [shape((2, 2 * piece, width), BF)],
        [got[2], got[1]],
        after=(lse,),
        name="two",
        micros=0.01,
    )
    two_parts = (two, flip(two, "x"), flip(two, "y"))
    sent = release([*att[1:], mine], (two, other_g), 0.01)
    parts = [att[0], turn(sent[0], 1), turn(sent[1], 2), turn(sent[2], 3)]
    got[3] = turn(sent[3], 3)

    corner = simple(
        corner_kernel,
        [shape((2, piece, width), BF)] * 2,
        two_parts[1:],
        after=(sent[0],),
        name="corner",
    )
    two_parts = (*two_parts, flip(corner[0], "y"), flip(corner[1], "x"))
    attn, mid, hidden_two = middle(
        here, parts, out_full, out_bias[None], tokens, mod_blocks, groups, after=(corner[0],)
    )
    own_x = hidden_two.reshape(micro * share, width)
    other_x = flip(own_x, "core")
    (third,) = release([got[3]], (mid,) + two_parts[3:], 100)
    third_parts = (third, flip(third, "x"), flip(third, "y"), diagonal(third))
    *carry, uk_a, us_a, dk_a, ds_a, bsum_a = feed(
        own_x, other_x, own_g, other_g, [two_parts], bias_a, None
    )
    ur_a = flip(us_a, "y")
    dr_a = flip(ds_a, "x")
    mlp_own, mlp_send, gh_own, gh_send, uk_b, us_b, dk_b, ds_b, bsum_b = feed(
        own_x, other_x, own_g, other_g, [third_parts, (up_near, down_near)], bias_b, carry
    )
    gh_got = flip(gh_send, "core")
    mlp_got = flip(mlp_send, "core")
    piece_shapes = [shape((2, piece, width), BF)] * 4
    uk_a, us_a, dk_a, ds_a = simple(
        halve_kernel, piece_shapes, [uk_a, ur_a, dk_a, dr_a], after=(gh_own,), name="halve", micros=100
    )
    ur_a = flip(us_a, "x")
    dr_a = flip(ds_a, "y")
    layer_out, grad_mid, d0, d1, d2, d3, o_keep, o_send, sums = between(
        jnp.concatenate([here[:1], own_valid, here[1:2]]),
        (mlp_own, gh_own),
        (mlp_got, gh_got),
        mid, attn, out_grad, mod_blocks, down_bias[None], out_full, parts, groups,
        after=(uk_a,),
    )
    grads = [d0] + [turn(d, -k) for k, d in ((1, d1), (2, d2), (3, d3))]
    o_got = flip(o_send, "core")
    o_rows = o_keep.shape[1] // 4
    o_room = -(-o_rows // 16) * 16

    (tick,) = simple(tick_kernel, [shape((8, 128), F32)], [], after=(d0, ur_a, dr_a), name="tick", micros=100)

    side = 4 * piece + 4 * o_room
    u_keep, u_send, d_keep, d_send = simple(
        functools.partial(mix_kernel, o_rows),
        [shape((side, width), BF)] * 4,
        [uk_b, us_b, dk_b, ds_b, o_keep, o_got],
        info,
        after=(tick,),
        scratch=[pltpu.VMEM((4, 4, o_room, width), BF), pltpu.VMEM((4 * o_rows, width), F32)],
        name="mix",
    )
    u_got = flip(u_send, "y")
    d_got = flip(d_send, "x")
    block_shape = shape((2 * piece, width), BF)
    t2, t1 = simple(
        quarter_kernel,
        [block_shape] * 2,
        [uk_a, ur_a, dk_a, dr_a],
        after=(u_send, *grads[1:]),
        name="quarter",
    )
    token = (t1,)
    t2 = turn(t2, -2)
    t1 = turn(t1, -1)

    back_info = [jnp.stack([rank, whole[m], core]) for m in range(micro)]
    part_0, lsum_0, bias_0, old = attend_back(
        0, back_info[0], query, key, value, lse, grads, qkv_turned, hidden_one, tokens, after=token
    )
    share_0 = lax.psum_scatter(part_0, "tensor", scatter_dimension=0, tiled=True)
    half_shape = shape((side // 2, width), BF)
    u_keep, u_send, d_keep, d_send = simple(
        halve_flat_kernel,
        [half_shape] * 4,
        [u_keep, u_got, d_keep, d_got],
        after=(lsum_0,),
        name="halve",
    )
    token = (u_keep,)
    u_got = flip(u_send, "x")
    d_got = flip(d_send, "y")
    part_1, lsum_1, bias_1, w_keep, w_send = attend_back(
        1, back_info[1], query, key, value, lse, grads, qkv_turned, hidden_one, tokens, old, after=token
    )
    w_got = flip(w_send, "core")
    def short(kernel, outs, operands, name, after=(), scratch=(), micros=3):
        return simple(
            kernel, outs, operands, info, after=after, scratch=scratch, name=name, micros=micros
        )

    def plain(kernel, outs, operands, name, after=(), micros=3):
        return simple(kernel, outs, operands, after=after, name=name, micros=micros)

    def rows_shape(count):
        return shape((count, width), BF)

    (tick,) = simple(
        tick_kernel, [shape((8, 128), F32)], [], after=(lsum_1, t1, t2), name="tick", micros=100
    )

    o_shape = rows_shape(o_room)
    block_shape = rows_shape(2 * piece + o_room)
    t3, o1, o2, t0 = plain(
        last_kernel,
        [block_shape, o_shape, o_shape, block_shape],
        [u_keep, u_got, d_keep, d_got],
        "last",
        (tick,),
        micros=60,
    )
    token = (t3,)
    t3 = turn(t3, -3)
    o1 = turn(o1, -1)
    o2 = turn(o2, -2)
    rows_all = w_keep.shape[0]
    keep, send = short(
        first_kernel,
        [rows_shape(rows_all // 2)] * 2,
        [w_keep, w_got],
        "first",
        token,
        [pltpu.VMEM((rows_all, width), BF)],
    )
    (pile,) = short(
        pile_kernel, [shape((56, width), F32)], [lsum_0, lsum_1, sums, bsum_a, bsum_b], "pile", (keep,)
    )
    pile_got = turn(pile, 2)
    keep, send = short(
        second_kernel,
        [rows_shape(rows_all // 4)] * 2,
        [keep, flip(send, "x")],
        "second",
        (*token, pile),
        [pltpu.VMEM((rows_all // 2, width), BF)],
    )
    tokens_grad = finish(here, 0, share_0, tokens, mod_blocks, grad_mid, groups, after=(keep,))
    send_got = flip(send, "y")
    (tick,) = plain(tick_kernel, [shape((8, 128), F32)], [], "tick", (keep, tokens_grad, o1, o2), micros=60)
    (merged,) = plain(
        merge_kernel,
        [rows_shape(rows_all // 4 + 2 * piece + o_room)],
        [keep, send_got, t0, t1, t2, t3, o1, o2],
        "merge",
        (tick,),
        micros=0.1,
    )
    (pile,) = plain(
        sum_kernel, [shape(pile.shape, F32)], [pile, pile_got], "sum", (merged,), micros=30
    )
    pile_far = turn(pile, 1)
    (part_1,) = release([part_1], (merged,))
    share_1 = lax.psum_scatter(part_1, "tensor", scatter_dimension=0, tiled=True)
    merged = over_rest(merged)
    all_four = [merged, flip(merged, "x"), flip(merged, "y"), diagonal(merged)]
    pay, mod_low = short(
        slots_kernel,
        [shape((24, columns), F32), shape((micro * slots, columns), BF)],
        [pile, pile_far, bias_0, bias_1, cond_act],
        "slots",
        (merged,),
        [pltpu.VMEM((micro * slots, 6 * width), F32)],
        micros=0.1,
    )
    pay_got = flip(pay, "core")
    cond_part = jnp.dot(mod_low, ada_turned, preferred_element_type=F32)

    cond_grad = cond_part + turn(cond_part, 2)
    cond_grad = cond_grad + turn(cond_grad, 1)

    def pair_kernel(mine, got, out):
        count = mine.shape[0]
        out[:count] = mine[...]
        out[count:] = got[...]

    def pair(mine, got, after=()):
        outs = [shape((2 * mine.shape[0], *mine.shape[1:]), F32)]
        return plain(pair_kernel, outs, [mine, got], "pair", after, micros=0.1)[0]

    pays = pair(pay[None], pay_got[None])
    pays = pair(pays, flip(pays, "x"))
    pays_got = flip(pays, "y")
    halves, others = short(
        functools.partial(order_kernel, o_rows, rows_all // 4),
        [shape((2, half, width), BF), rows_shape(rows_all + 4 * o_rows)],
        all_four,
        "order",
        (pays, cond_grad),
        [pltpu.VMEM((4, o_room, width), BF)],
        micros=0.1,
    )
    halves_got = flip(halves, "core")
    others_got = flip(others, "core")
    tokens_grad = finish(
        here, 1, share_1, tokens, mod_blocks, grad_mid, groups, tokens_grad, after=(halves,)
    )
    up_weight_grad, down_weight_grad, qkv_weight_grad, out_weight_grad = spread(
        info,
        [halves, halves_got, others, others_got],
        [up_weight.shape, down_weight.shape, qkv_turned.shape, out_weight.shape],
        (tokens_grad,),
    )
    pays = pair(pays, pays_got, (up_weight_grad,))
    if lax.axis_size("rest") > 1:
        pays = lax.all_gather(pays, "rest", axis=0, tiled=True)
    ada_weight_grad, ada_b, out_b, down_b, up_b, qv_bias_grad = short(
        tail_kernel,
        [
            shape(ada_turned.shape, F32),
            shape((columns,), F32),
            shape((width,), F32),
            shape((width,), F32),
            shape((part,), F32),
            shape(qv_bias.shape, F32),
        ],
        [pays],
        "tail",
    )
    cond_float = conditioning.astype(F32)
    sigmoid = jax.nn.sigmoid(cond_float)
    conditioning_grad = cond_grad.reshape(micro, slots, width) * (
        sigmoid * (1.0 + cond_float * (1.0 - sigmoid))
    )
    return (
        layer_out,
        tokens_grad,
        conditioning_grad,
        ada_weight_grad.T,
        ada_b,
        qkv_weight_grad.transpose(0, 2, 1),
        qv_bias_grad,
        out_weight_grad,
        out_b,
        up_weight_grad,
        up_b,
        down_weight_grad,
        down_b,
    )


def solution(mesh):
    count, groups = mesh.devices.shape
    devices = mesh.devices.reshape(count // 8, 2, 2, 2, groups)
    fine = Mesh(devices, DP + ("tensor",))
    placed = (
        P(None, DP, None),
        P(None, DP, None),
        P(None, DP),
        P(None, DP, None),
        P(None, "tensor"),
        P("tensor"),
        P(None, None, "tensor"),
        P(None, "tensor"),
        P("tensor", None),
        P(),
        P(None, "tensor"),
        P("tensor"),
        P("tensor", None),
        P(),
    )
    return jax.shard_map(
        local,
        mesh=fine,
        in_specs=placed,
        out_specs=(
            P(None, DP + ("tensor",), None),
            P(None, DP + ("tensor",), None),
            P(None, DP, None),
            P(None, "tensor"),
            P("tensor"),
            P(None, None, "tensor"),
            P(None, "tensor"),
            P("tensor", None),
            P(),
            P(None, "tensor"),
            P("tensor"),
            P("tensor", None),
            P(),
        ),
        check_vma=False,
    )
```
